32 devices in a mesh: parts: 2 (over x), store: 8 (over z, core), layer: 2 (over y).
Axes of the slice: x: 2, y: 2, z: 4, core: 2. Of those that a mesh axis runs over, the one named last changes fastest.
Arguments:
- train_grads: bfloat16 [16384, 2, 4096], P(('parts', 'store'), 'layer'), parts along dimension 0, may hold values from -0.09375 to 0.09375
- query_grads: bfloat16 [512, 2, 4096], P('store', 'layer'), may hold values from -6 to 6
- left_factor: float32 [2, 64, 64], P('layer'), may hold values from -0.75 to 0.75
- right_factor: float32 [2, 64, 64], P('layer'), may hold values from -0.75 to 0.75
- layer_weight: float32 [2], replicated, may hold values from 0.25 to 4
- layer_of: int32 [2], P('layer'), may hold values from 0 to 1, each once
- train_ids: int32 [16384], P(('parts', 'store')), parts along dimension 0, may hold values from 0 to 63
- query_ids: int32 [512], P('layer'), may hold values from 0 to 63
Outputs:
- scores: float32 [512, 16384], P('layer', ('parts', 'store')), parts along dimension 1
The draws below stay inside these ranges and needn't reach their ends.
There are 2 independent parts, one for each index of `parts`. The reference program is written for one: setup_inputs(seed, part) draws one part's arguments, and reference() takes and returns one part's arrays. A program takes and returns all parts, laid end to end along the dimension named above; an argument that names none is the same for every part. Nothing has to cross between parts.
Inputs may be any that keep to these rules, and one draw needn't show every extreme that they name: `layer_of`: each layer number appears once.
All inputs are finite; a program needn't handle non-finite values.
Results may differ from the reference program's by a relative error of at most 0.0029.
Values may be sent and summed in bfloat16 or wider, within the bound.
No kernel may reach another device: no remote copies, remote signals or barrier semaphores. Data moves between devices by JAX's collectives and lax.ppermute only.
A program may use at most 64 MiB of HBM per device.

```python
import math
import jax
import jax.numpy as jnp
from jax import lax

FACT = 64
P_SIZE = 4096
LAYERS = 2
TRAIN = 8192
QUERIES = 512
CLUSTERS = 64


def touch_ends(result, own_key, least, high):
    extent = result.shape
    index_at = [jax.random.randint(jax.random.fold_in(own_key, axis), (), 0, extent[axis]) for axis in range(len(extent))]
    result = result.at[tuple(index_at)].set(least)
    longest = extent.index(max(extent))
    index_at[longest] = (index_at[longest] + 1) % extent[longest]
    return result.at[tuple(index_at)].set(high)


def levels(own_key, shape, shards, low, high):
    def one(dim, shards_of):
        steps = jax.random.uniform(jax.random.fold_in(jax.random.fold_in(own_key, 6), dim), (shards_of,), jnp.float32, low / len(shards), high / len(shards))
        return jnp.repeat(jnp.exp(steps), shape[dim] // shards_of).reshape((-1,) + (1,) * (len(shape) - dim - 1))

    loudness = one(*shards[0])
    for cut in shards[1:]:
        loudness = loudness * one(*cut)
    return loudness


def normal_values(stream_key, shape, deviation, limit, split=(), kind=jnp.bfloat16):
    values = deviation * jax.random.normal(stream_key, shape, jnp.float32)
    if split:
        values = values * levels(stream_key, shape, split, -0.22, 0.18)
    return jnp.clip(values, -limit, limit).astype(kind)


def setup_inputs(seed: int = 0, part: int = 0) -> dict:
    seeds = jax.random.split(jax.random.key(seed), 9)
    part_keys = jax.random.split(jax.random.fold_in(seeds[8], part), 9)
    return {
        "train_grads": normal_values(part_keys[0], (TRAIN, LAYERS, P_SIZE), 0.015625, 0.09375, ((0, 8), (1, 2))),
        "query_grads": normal_values(seeds[1], (QUERIES, LAYERS, P_SIZE), 1.0, 6.0, ((0, 8), (1, 2))),
        "left_factor": normal_values(seeds[2], (LAYERS, FACT, FACT), FACT ** -0.5, 0.75, ((0, 2),), jnp.float32),
        "right_factor": normal_values(seeds[3], (LAYERS, FACT, FACT), FACT ** -0.5, 0.75, ((0, 2),), jnp.float32),
        "layer_weight": jnp.clip(jnp.exp(jax.random.uniform(seeds[4], (LAYERS,), jnp.float32, math.log(0.25), math.log(4.0))), 0.25, 4.0),
        "layer_of": jax.random.permutation(seeds[5], LAYERS).astype(jnp.int32),
        "train_ids": touch_ends(jax.random.randint(part_keys[6], (TRAIN,), 0, CLUSTERS), jax.random.fold_in(part_keys[6], 1), 0, CLUSTERS - 1).astype(jnp.int32),
        "query_ids": touch_ends(jax.random.randint(seeds[7], (QUERIES,), 0, CLUSTERS), jax.random.fold_in(seeds[7], 1), 0, CLUSTERS - 1).astype(jnp.int32),
    }


def reference(train_grads, query_grads, left_factor, right_factor, layer_weight, layer_of, train_ids, query_ids):
    mats = query_grads.astype(jnp.float32).reshape(QUERIES, LAYERS, FACT, FACT)
    half = jnp.einsum("lij,qljk->qlik", left_factor, mats, precision=lax.Precision.HIGHEST)
    full = jnp.einsum("qlik,lkm->qlim", half, right_factor, precision=lax.Precision.HIGHEST)
    precond = full.reshape(QUERIES, LAYERS, P_SIZE).astype(jnp.bfloat16)
    weights = layer_weight[layer_of]
    total = jnp.zeros((QUERIES, TRAIN), jnp.float32)
    for slot in range(LAYERS):
        partial_value = jnp.dot(precond[:, slot, :], train_grads[:, slot, :].T, preferred_element_type=jnp.float32)
        total = total + weights[slot] * partial_value
    same = query_ids[:, None] == train_ids[None, :]
    return jnp.where(same, jnp.float32(0.0), total)
```

```python
import functools

import jax
import jax.numpy as jnp
from jax import lax
from jax.experimental import pallas as pl
from jax.experimental.pallas import tpu as pltpu
from jax.sharding import PartitionSpec as P

AXES = ("parts", "store", "layer")
VMEM = pl.BlockSpec(memory_space=pltpu.VMEM)
SMEM = pl.BlockSpec(memory_space=pltpu.SMEM)
LIMIT = 48 * 1024 * 1024


def preconditioned(query_grads, left_factor, right_factor):
    q_rows, slots, width = query_grads.shape
    side = left_factor.shape[1]
    mats = query_grads.astype(jnp.float32).reshape(q_rows, slots, side, side)
    half = jnp.einsum("lij,qljk->qlik", left_factor, mats, precision=lax.Precision.HIGHEST)
    full = jnp.einsum("qlik,lkm->qlim", half, right_factor, precision=lax.Precision.HIGHEST)
    return full.reshape(q_rows, slots, width).astype(jnp.bfloat16)


def general(
    train_grads,
    query_grads,
    left_factor,
    right_factor,
    layer_weight,
    layer_of,
    train_ids,
    query_ids,
):
    precond = preconditioned(query_grads, left_factor, right_factor)
    weight = jnp.take(layer_weight, layer_of[0])
    queries = lax.all_gather(precond, "store", axis=0, tiled=True)
    terms = weight * jnp.dot(
        queries[:, 0, :], train_grads[:, 0, :].T, preferred_element_type=jnp.float32
    )
    summed = lax.psum_scatter(terms, "layer", scatter_dimension=0, tiled=True)
    same = query_ids[:, None] == train_ids[None, :]
    return jnp.where(same, jnp.float32(0.0), summed)


PARTS, CHIPS, CORES, LAYERS = 2, 4, 2, 2


def permute(value, target):
    pairs = []
    for p in range(PARTS):
        for z in range(CHIPS):
            for c in range(CORES):
                for l in range(LAYERS):
                    tp, tz, tc, tl = target(p, z, c, l)
                    source = ((p * CHIPS + z) * CORES + c) * LAYERS + l
                    pairs.append((source, ((tp * CHIPS + tz) * CORES + tc) * LAYERS + tl))
    return lax.ppermute(value, AXES, pairs)


to_part = functools.partial(permute, target=lambda p, z, c, l: (1 - p, z, c, l))
to_core = functools.partial(permute, target=lambda p, z, c, l: (p, z, 1 - c, l))
to_layer = functools.partial(permute, target=lambda p, z, c, l: (p, z, c, 1 - l))
to_near = functools.partial(permute, target=lambda p, z, c, l: (p, z ^ 1, c, l))
to_far = functools.partial(permute, target=lambda p, z, c, l: (p, z ^ 3, c, l))


def place():
    store = lax.axis_index("store")
    return lax.axis_index("parts"), store // CORES, store % CORES, lax.axis_index("layer")


def scores_of(pieces, train_ref, weight_ref, layer_ref, write):
    weight = weight_ref[layer_ref[0]]
    queries = jnp.concatenate([piece[...] for piece in pieces], axis=0)
    n, step = train_ref.shape[0], 256
    for at in range(0, n, step):
        part = lax.dot_general(
            queries,
            train_ref[at : at + step, :],
            (((1,), (1,)), ((), ())),
            preferred_element_type=jnp.float32,
        )
        write(slice(at, at + step), weight * part)


def keep_kernel(weight_ref, layer_ref, train_ref, *refs):
    *pieces, out = refs

    def write(columns, value):
        out[:, columns] = value

    scores_of(pieces, train_ref, weight_ref, layer_ref, write)


def swap_kernel(weight_ref, layer_ref, train_ref, early, *refs):
    *pieces, send, keep = refs
    _, z, _, layer = place()
    near_is_mine = z // 2 == layer

    def write(columns, value):
        before = early[:, columns]
        send[:, columns] = jnp.where(near_is_mine, value, before).astype(send.dtype)
        keep[:, columns] = jnp.where(near_is_mine, before, value)

    scores_of(pieces, train_ref, weight_ref, layer_ref, write)


def call_scores(kernel, weight, layer, train, inputs, outs):
    rows, n = 128, train.shape[0]
    return pl.pallas_call(
        kernel,
        out_shape=[jax.ShapeDtypeStruct((rows, n), t) for t in outs],
        in_specs=[SMEM, SMEM] + [VMEM] * (1 + len(inputs)),
        out_specs=[VMEM] * len(outs),
        compiler_params=pltpu.CompilerParams(vmem_limit_bytes=LIMIT),
        cost_estimate=pl.CostEstimate(
            flops=2 * rows * n * train.shape[1], bytes_accessed=train.size * 2, transcendentals=0
        ),
    )(weight, layer, train, *inputs)


def final_kernel(train_ids, query_ids, keep0, keep1, got0, got1, out):
    part, z, core, layer = place()
    near_is_mine = z // 2 == layer
    low = z % 2
    first = jnp.where(near_is_mine, low, 1 - low)
    quarter = out.shape[0] // 8
    ids = train_ids[...]
    for block, keep, got in ((first, keep0, got0), (1 - first, keep1, got1)):
        for k in range(4):
            c = core if k < 2 else 1 - core
            h = part if k % 2 == 0 else 1 - part
            at = pl.multiple_of(((block * 2 + c) * 2 + h) * quarter, quarter)
            here = pl.ds(k * quarter, quarter)
            total = keep[here, :] + got[here, :].astype(jnp.float32)
            same = query_ids[pl.ds(at, quarter), :] == ids
            out[pl.ds(at, quarter), :] = jnp.where(same, jnp.float32(0.0), total)


def small(
    train_grads,
    query_grads,
    left_factor,
    right_factor,
    layer_weight,
    layer_of,
    train_ids,
    query_ids,
):
    train = train_grads[:, 0, :]
    precond = preconditioned(query_grads, left_factor, right_factor)[:, 0, :]
    rows = precond.shape[0] // 2
    part = lax.axis_index("parts")
    mine = lax.dynamic_slice_in_dim(precond, part * rows, rows, 0)
    other = lax.dynamic_slice_in_dim(precond, (1 - part) * rows, rows, 0)

    near = to_near(mine)
    far = to_far(mine)
    cross = lambda a, b: to_core(jnp.concatenate([a, b], axis=0))
    score = functools.partial(call_scores, weight=layer_weight, layer=layer_of, train=train)
    f32, bf16 = jnp.float32, jnp.bfloat16

    (scores0,) = score(keep_kernel, inputs=[mine, other, cross(mine, other)], outs=[f32])
    near_x = to_part(near)
    (scores1,) = score(keep_kernel, inputs=[near, near_x, cross(near, near_x)], outs=[f32])
    last = to_near(far)
    far_x = to_part(far)
    send0, keep0 = score(
        swap_kernel, inputs=[scores0, far, far_x, cross(far, far_x)], outs=[bf16, f32]
    )
    got0 = to_layer(send0)
    last_x = to_part(last)
    send1, keep1 = score(
        swap_kernel, inputs=[scores1, last, last_x, cross(last, last_x)], outs=[bf16, f32]
    )
    got1 = to_layer(send1)
    return pl.pallas_call(
        final_kernel,
        out_shape=jax.ShapeDtypeStruct((query_ids.shape[0], train_ids.shape[0]), f32),
        in_specs=[VMEM] * 6,
        out_specs=VMEM,
        compiler_params=pltpu.CompilerParams(vmem_limit_bytes=LIMIT),
    )(train_ids[None, :], query_ids[:, None], keep0, keep1, got0, got1)


def solution(mesh):
    placed = (
        P(("parts", "store"), "layer", None),
        P("store", "layer", None),
        P("layer", None, None),
        P("layer", None, None),
        P(),
        P("layer"),
        P(("parts", "store")),
        P("layer"),
    )
    sizes = tuple(mesh.shape[axis] for axis in AXES)
    return jax.shard_map(
        small if sizes == (PARTS, CHIPS * CORES, LAYERS) else general,
        mesh=mesh,
        in_specs=placed,
        out_specs=P("layer", ("parts", "store")),
        check_vma=False,
    )
```

```python
import functools

import jax
import jax.numpy as jnp
from jax import lax
from jax.experimental import pallas as pl
from jax.experimental.pallas import tpu as pltpu
from jax.sharding import PartitionSpec as P

AXES = ("parts", "store", "layer")
VMEM = pl.BlockSpec(memory_space=pltpu.VMEM)
SMEM = pl.BlockSpec(memory_space=pltpu.SMEM)
bf16, f32 = jnp.bfloat16, jnp.float32
LIMIT = 20 * 1024 * 1024


def preconditioned(query_grads, left_factor, right_factor):
    q_rows, slots, width = query_grads.shape
    side = left_factor.shape[1]
    mats = query_grads.astype(jnp.float32).reshape(q_rows, slots, side, side)
    half = jnp.einsum("lij,qljk->qlik", left_factor, mats, precision=lax.Precision.HIGHEST)
    full = jnp.einsum("qlik,lkm->qlim", half, right_factor, precision=lax.Precision.HIGHEST)
    return full.reshape(q_rows, slots, width).astype(jnp.bfloat16)


def general(
    train_grads,
    query_grads,
    left_factor,
    right_factor,
    layer_weight,
    layer_of,
    train_ids,
    query_ids,
):
    precond = preconditioned(query_grads, left_factor, right_factor)
    weight = jnp.take(layer_weight, layer_of[0])
    queries = lax.all_gather(precond, "store", axis=0, tiled=True)
    terms = weight * jnp.dot(
        queries[:, 0, :], train_grads[:, 0, :].T, preferred_element_type=jnp.float32
    )
    summed = lax.psum_scatter(terms, "layer", scatter_dimension=0, tiled=True)
    same = query_ids[:, None] == train_ids[None, :]
    return jnp.where(same, jnp.float32(0.0), summed)


PARTS, CHIPS, CORES, LAYERS = 2, 4, 2, 2
CHUNK = 16
COST = 0


def permute(value, name, target):
    pairs = []
    for p in range(PARTS):
        for z in range(CHIPS):
            for c in range(CORES):
                for l in range(LAYERS):
                    tp, tz, tc, tl = target(p, z, c, l)
                    source = ((p * CHIPS + z) * CORES + c) * LAYERS + l
                    pairs.append((source, ((tp * CHIPS + tz) * CORES + tc) * LAYERS + tl))
    with jax.named_scope(name):
        return lax.ppermute(value, AXES, pairs)


to_part = functools.partial(permute, target=lambda p, z, c, l: (1 - p, z, c, l))
to_core = functools.partial(permute, target=lambda p, z, c, l: (p, z, 1 - c, l))
to_layer = functools.partial(permute, target=lambda p, z, c, l: (p, z, c, 1 - l))
to_near = functools.partial(permute, target=lambda p, z, c, l: (p, z ^ 1, c, l))
to_far = functools.partial(permute, target=lambda p, z, c, l: (p, z ^ 3, c, l))


def after(value, *others):
    return lax.optimization_barrier((value, *others))[0]


def place():
    store = lax.axis_index("store")
    return lax.axis_index("parts"), store // CORES, store % CORES, lax.axis_index("layer")


def split(x, terms):
    out = []
    for _ in range(terms):
        term = x.astype(bf16)
        out.append(term)
        x = x - term.astype(f32)
    return out


def dot(a, b):
    return lax.dot_general(a, b, (((1,), (0,)), ((), ())), preferred_element_type=f32)


def iota(shape, dim):
    return lax.broadcasted_iota(jnp.int32, shape, dim)


def factors(left, right):
    r, c = iota((256, 64), 0), iota((256, 64), 1)
    pick = jnp.where(c == 4 * (r % 16) + (r // 16) % 4, 1.0, 0.0).astype(bf16)
    r, c = iota((64, 256), 0), iota((64, 256), 1)
    pick_t = jnp.where(r == 4 * (c % 16) + (c // 16) % 4, 1.0, 0.0).astype(bf16)
    block = iota((256, 256), 0) // 64 == iota((256, 256), 1) // 64
    lefts = [
        jnp.where(block, dot(dot(pick, term).astype(bf16), pick_t), 0.0).astype(bf16)
        for term in split(left, 2)
    ]
    row = jnp.concatenate([right, right], axis=1)
    tiled = jnp.concatenate([jnp.concatenate([row] * 4, axis=1)] * 4, axis=0)
    block = iota((256, 512), 0) // 64 == iota((256, 512), 1) // 128
    return lefts, split(jnp.where(block, tiled, 0.0), 2)


def precond_chunk(q, lefts, rights, write):
    tiles = q.shape[1] // 256
    r, c = iota((256, 256), 0), iota((256, 256), 1)
    swap = jnp.where((r // 16 == c % 16) & (r % 16 == c // 16), 1.0, 0.0).astype(bf16)
    x = jnp.concatenate([q[:, t * 256 : (t + 1) * 256] for t in range(tiles)], axis=0)
    x = dot(swap, x).astype(bf16)
    z = dot(x, rights[0]) + dot(x, rights[1])
    sets = []
    for first in range(0, 16, 4):
        rows = [
            z[query * 16 : (query + 1) * 16, s * 128 : (s + 1) * 128]
            for query in range(first, first + 4)
            for s in range(4)
        ]
        sets.append(jnp.concatenate(rows, axis=0))
    high, low = split(jnp.concatenate(sets, axis=1), 2)
    z = dot(lefts[0], high) + (dot(lefts[0], low) + dot(lefts[1], high))
    side = iota((16, 128), 1) < 64
    rows = []
    for first in range(4):
        for k in range(4):
            o = z[k * 64 : (k + 1) * 64, first * 128 : (first + 1) * 128]
            pair = [jnp.where(side, o[0:16], o[16:32]), jnp.where(side, o[32:48], o[48:64])]
            rows.append(jnp.concatenate(pair, axis=1))
    y = dot(swap, jnp.concatenate(rows, axis=0).astype(bf16)).astype(bf16)
    for t in range(tiles):
        write(t, y[t * 16 : (t + 1) * 16])


def own_kernel(q_ref, left_ref, right_ref, mine, chunk0, chunk1, lefts_ref, rights_ref):
    lefts, rights = factors(left_ref[...], right_ref[...])
    for k in range(2):
        lefts_ref[k] = lefts[k]
        rights_ref[k] = rights[k]
    start = lax.axis_index("parts") * (2 * CHUNK)
    for k, chunk in enumerate((chunk0, chunk1)):

        def write(t, value):
            mine[k * CHUNK : (k + 1) * CHUNK, t * 256 : (t + 1) * 256] = value
            chunk[:, t * 256 : (t + 1) * 256] = value

        at = pl.multiple_of(start + k * CHUNK, CHUNK)
        precond_chunk(q_ref[pl.ds(at, CHUNK), :], lefts, rights, write)


def rest_kernel(q_ref, mine, lefts_ref, rights_ref, own):
    lefts, rights = [lefts_ref[0], lefts_ref[1]], [rights_ref[0], rights_ref[1]]
    own[: 2 * CHUNK, :] = mine[...]
    start = (1 - lax.axis_index("parts")) * (2 * CHUNK)
    for k in range(2):

        def write(t, value):
            own[(2 + k) * CHUNK : (3 + k) * CHUNK, t * 256 : (t + 1) * 256] = value

        at = pl.multiple_of(start + k * CHUNK, CHUNK)
        precond_chunk(q_ref[pl.ds(at, CHUNK), :], lefts, rights, write)


def score_kernel(weight_ref, layer_ref, train_ref, *refs, picks, stored, early, add):
    inputs, refs = refs[: len(picks)], refs[len(picks) :]
    n_before = sum(taken for _, _, taken in early)
    before, refs = refs[:n_before], refs[n_before:]
    adds, outs = (refs[:2], refs[2:]) if add else ((), refs)
    if add:
        outs[-1][...] = adds[0][...] + adds[1][...].astype(f32)
        outs = outs[:-1]
    weight = weight_ref[layer_ref[0]]
    queries = jnp.concatenate(
        [piece[at : at + CHUNK, :] for piece, rows in zip(inputs, picks) for at in rows], axis=0
    )
    _, z, _, layer = place()
    near_is_mine = z // 2 == layer
    n, step = train_ref.shape[0], 256
    for at in range(0, n, step):
        here = slice(at, at + step)
        value = lax.dot_general(
            train_ref[here, :], queries, (((1,), (1,)), ((), ())), preferred_element_type=f32
        )
        value = weight * value.T
        if stored:
            outs[0][:, here] = value[:stored]
        if early:
            send, keep = outs[-2:]
            old, given = [], list(before)
            for first, rows, taken in early:
                old.append(
                    given.pop(0)[first : first + rows, here] if taken else value[first : first + rows]
                )
            old, new = jnp.concatenate(old, axis=0), value[stored:]
            send[:, here] = jnp.where(near_is_mine, new, old).astype(send.dtype)
            keep[:, here] = jnp.where(near_is_mine, old, new)


def call_scores(weight, layer, train, inputs, stored=0, early=(), add=()):
    n = train.shape[0]
    total = CHUNK * sum(len(rows) for _, rows in inputs)
    outs = [jax.ShapeDtypeStruct((stored, n), f32)] if stored else []
    if early:
        outs += [jax.ShapeDtypeStruct((total - stored, n), t) for t in (bf16, f32)]
    if add:
        outs += [jax.ShapeDtypeStruct(add[0].shape, f32)]
    inputs_early = [a for a, _, _ in early if a is not None]
    return pl.pallas_call(
        functools.partial(
            score_kernel,
            picks=[rows for _, rows in inputs],
            stored=stored,
            early=[(first, rows, a is not None) for a, first, rows in early],
            add=bool(add),
        ),
        out_shape=outs,
        in_specs=[SMEM, SMEM] + [VMEM] * (1 + len(inputs) + len(inputs_early) + len(add)),
        out_specs=[VMEM] * len(outs),
        compiler_params=pltpu.CompilerParams(vmem_limit_bytes=LIMIT),
        cost_estimate=pl.CostEstimate(flops=COST, bytes_accessed=0, transcendentals=0),
    )(weight, layer, train, *[a for a, _ in inputs], *inputs_early, *add)


def final_kernel(train_ids, query_ids, sum1, keep2, got2, keep3, got3, out):
    part, z, core, layer = place()
    near_is_mine = z // 2 == layer
    low = z % 2
    first = jnp.where(near_is_mine, low, 1 - low)
    ids = train_ids[...]
    groups = (
        (0, 0, 0, (sum1,)),
        (0, 1, 0, (keep2, got2)),
        (1, 0, 64, (keep2, got2)),
        (1, 1, 0, (keep3, got3)),
    )
    for block, chunk, base, terms in groups:
        block = first if block == 0 else 1 - first
        for i in range(4):
            c = core if i < 2 else 1 - core
            h = part if i % 2 == 0 else 1 - part
            at = pl.multiple_of((((block * 2 + c) * 2 + h) * 2 + chunk) * CHUNK, CHUNK)
            here = slice(base + i * CHUNK, base + (i + 1) * CHUNK)
            total = terms[0][here, :]
            for term in terms[1:]:
                total = total + term[here, :].astype(f32)
            same = query_ids[pl.ds(at, CHUNK), :] == ids
            out[pl.ds(at, CHUNK), :] = jnp.where(same, jnp.float32(0.0), total)


def kernel_call(kernel, outs, inputs, flops=0):
    return pl.pallas_call(
        kernel,
        out_shape=outs,
        in_specs=[VMEM] * len(inputs),
        out_specs=[VMEM] * len(outs) if isinstance(outs, list) else VMEM,
        compiler_params=pltpu.CompilerParams(vmem_limit_bytes=LIMIT),
        cost_estimate=pl.CostEstimate(flops=flops, bytes_accessed=0, transcendentals=0),
    )(*inputs)


def small(
    train_grads,
    query_grads,
    left_factor,
    right_factor,
    layer_weight,
    layer_of,
    train_ids,
    query_ids,
):
    train, queries = train_grads[:, 0, :], query_grads[:, 0, :]
    width = queries.shape[1]
    shape = jax.ShapeDtypeStruct
    mine, mine_a, mine_b, lefts, rights = kernel_call(
        own_kernel,
        [shape((rows, width), bf16) for rows in (2 * CHUNK, CHUNK, CHUNK)]
        + [shape((2, 256, 256), bf16), shape((2, 256, 512), bf16)],
        [queries, left_factor[0], right_factor[0]],
    )
    far_a = to_far(mine_a, "far_a")
    far_b = to_far(mine_b, "far_b")
    near = to_near(mine, "near")
    (own,) = kernel_call(
        rest_kernel,
        [shape((4 * CHUNK, width), bf16)],
        [queries, mine, lefts, rights],
        flops=COST,
    )
    join = lambda *pieces: jnp.concatenate(pieces, axis=0)
    score = functools.partial(call_scores, layer_weight, layer_of, train)
    both = ((0, 32), (16, 48))
    pieces = lambda own_half, other_half, other_core: [
        (own_half, (0,)), (other_half, (0,)), (other_core, (0, 16))
    ]

    own_x = to_core(own, "own_x")
    far_a = after(far_a, own)
    far_pa = to_part(far_a, "far_pa")
    cross_a = to_near(far_a, "cross_a")
    own_x = after(own_x, far_a)
    (early0,) = score(
        [(own, both[0]), (own_x, both[0]), (own, both[1]), (own_x, both[1])], stored=128
    )
    near = after(near, early0)
    near_p = to_part(near, "near_p")
    cross_b = to_near(far_b, "cross_b")
    far_pb = to_part(far_b, "far_pb")
    far_xa = to_core(join(far_a, far_pa), "far_xa")
    near_x = to_core(join(near, near_p), "near_x")
    far_xa = after(far_xa, far_b)
    send1, keep1 = score(pieces(far_a, far_pa, far_xa), early=[(early0, 0, 64)])
    got1 = to_layer(send1, "got1")
    far_xb = to_core(join(far_b, far_pb), "far_xb")
    cross_pa = to_part(cross_a, "cross_pa")
    cross_xa = to_core(join(cross_a, cross_pa), "cross_xa")
    cross_xa = after(cross_xa, cross_b)
    cross_b = after(cross_b, send1)
    cross_pb = to_part(cross_b, "cross_pb")
    early1, send2, keep2 = score(
        [(near, (0,)), (near_p, (0,)), (near_x, both[0])]
        + [(near, (16,)), (near_p, (16,)), (near_x, both[1])]
        + pieces(far_b, far_pb, far_xb)
        + pieces(cross_a, cross_pa, cross_xa),
        stored=128,
        early=[(early0, 64, 64), (None, 0, 64)],
    )
    got2 = to_layer(send2, "got2")
    cross_xb = to_core(join(cross_b, after(cross_pb, send2)), "cross_xb")
    send3, keep3, sum1 = score(
        pieces(cross_b, cross_pb, cross_xb), early=[(early1, 64, 64)], add=(keep1, got1)
    )
    got3 = to_layer(send3, "got3")
    return kernel_call(
        final_kernel,
        shape((query_ids.shape[0], train_ids.shape[0]), f32),
        [train_ids[None, :], query_ids[:, None], sum1, keep2, got2, keep3, got3],
    )


def solution(mesh):
    placed = (
        P(("parts", "store"), "layer", None),
        P("store", "layer", None),
        P("layer", None, None),
        P("layer", None, None),
        P(),
        P("layer"),
        P(("parts", "store")),
        P("layer"),
    )
    sizes = tuple(mesh.shape[axis] for axis in AXES)
    return jax.shard_map(
        small if sizes == (PARTS, CHIPS * CORES, LAYERS) else general,
        mesh=mesh,
        in_specs=placed,
        out_specs=P("layer", ("parts", "store")),
        check_vma=False,
    )
```

```python
import functools

import jax
import jax.numpy as jnp
from jax import lax
from jax.experimental import pallas as pl
from jax.experimental.pallas import tpu as pltpu
from jax.sharding import PartitionSpec as P

AXES = ("parts", "store", "layer")
VMEM = pl.BlockSpec(memory_space=pltpu.VMEM)
SMEM = pl.BlockSpec(memory_space=pltpu.SMEM)
bf16, f32 = jnp.bfloat16, jnp.float32
LIMIT = 20 * 1024 * 1024


def preconditioned(query_grads, left_factor, right_factor):
    q_rows, slots, width = query_grads.shape
    side = left_factor.shape[1]
    mats = query_grads.astype(jnp.float32).reshape(q_rows, slots, side, side)
    half = jnp.einsum("lij,qljk->qlik", left_factor, mats, precision=lax.Precision.HIGHEST)
    full = jnp.einsum("qlik,lkm->qlim", half, right_factor, precision=lax.Precision.HIGHEST)
    return full.reshape(q_rows, slots, width).astype(jnp.bfloat16)


def general(
    train_grads,
    query_grads,
    left_factor,
    right_factor,
    layer_weight,
    layer_of,
    train_ids,
    query_ids,
):
    precond = preconditioned(query_grads, left_factor, right_factor)
    weight = jnp.take(layer_weight, layer_of[0])
    queries = lax.all_gather(precond, "store", axis=0, tiled=True)
    terms = weight * jnp.dot(
        queries[:, 0, :], train_grads[:, 0, :].T, preferred_element_type=jnp.float32
    )
    summed = lax.psum_scatter(terms, "layer", scatter_dimension=0, tiled=True)
    same = query_ids[:, None] == train_ids[None, :]
    return jnp.where(same, jnp.float32(0.0), summed)


PARTS, CHIPS, CORES, LAYERS = 2, 4, 2, 2
CHUNK = 16
HALF = 2 * CHUNK
STEP = 256
HBM = pl.BlockSpec(memory_space=pltpu.HBM)


def permute(value, name, target):
    pairs = []
    for p in range(PARTS):
        for z in range(CHIPS):
            for c in range(CORES):
                for l in range(LAYERS):
                    tp, tz, tc, tl = target(p, z, c, l)
                    source = ((p * CHIPS + z) * CORES + c) * LAYERS + l
                    pairs.append((source, ((tp * CHIPS + tz) * CORES + tc) * LAYERS + tl))
    with jax.named_scope(name):
        return lax.ppermute(value, AXES, pairs)


to_part = functools.partial(permute, target=lambda p, z, c, l: (1 - p, z, c, l))
to_core = functools.partial(permute, target=lambda p, z, c, l: (p, z, 1 - c, l))
to_layer = functools.partial(permute, target=lambda p, z, c, l: (p, z, c, 1 - l))
to_near = functools.partial(permute, target=lambda p, z, c, l: (p, z ^ 1, c, l))
to_far = functools.partial(permute, target=lambda p, z, c, l: (p, z ^ 3, c, l))


def after(value, *others):
    return lax.optimization_barrier((value, *others))[0]


def place():
    store = lax.axis_index("store")
    return lax.axis_index("parts"), store // CORES, store % CORES, lax.axis_index("layer")


def split(x, terms):
    out = []
    for _ in range(terms):
        term = x.astype(bf16)
        out.append(term)
        x = x - term.astype(f32)
    return out


def dot(a, b):
    return lax.dot_general(a, b, (((1,), (0,)), ((), ())), preferred_element_type=f32)


def iota(shape, dim):
    return lax.broadcasted_iota(jnp.int32, shape, dim)


def factors(left, right):
    r, c = iota((256, 64), 0), iota((256, 64), 1)
    pick = jnp.where(c == 4 * (r % 16) + (r // 16) % 4, 1.0, 0.0).astype(bf16)
    r, c = iota((64, 256), 0), iota((64, 256), 1)
    pick_t = jnp.where(r == 4 * (c % 16) + (c // 16) % 4, 1.0, 0.0).astype(bf16)
    block = iota((256, 256), 0) // 64 == iota((256, 256), 1) // 64
    lefts = [
        jnp.where(block, dot(dot(pick, term).astype(bf16), pick_t), 0.0).astype(bf16)
        for term in split(left, 2)
    ]
    row = jnp.concatenate([right, right], axis=1)
    tiled = jnp.concatenate([jnp.concatenate([row] * 4, axis=1)] * 4, axis=0)
    block = iota((256, 512), 0) // 64 == iota((256, 512), 1) // 128
    return lefts, split(jnp.where(block, tiled, 0.0), 2)


def precond_rows(q_ref, lefts, rights, out, base):
    for at in range(0, q_ref.shape[0], CHUNK):
        values = precond_chunk(q_ref[at : at + CHUNK, :], lefts, rights)
        for t, value in enumerate(values):
            out[base + at : base + at + CHUNK, t * 256 : (t + 1) * 256] = value


def precond_chunk(q, lefts, rights):
    tiles = q.shape[1] // 256
    r, c = iota((256, 256), 0), iota((256, 256), 1)
    swap = jnp.where((r // 16 == c % 16) & (r % 16 == c // 16), 1.0, 0.0).astype(bf16)
    x = jnp.concatenate([q[:, t * 256 : (t + 1) * 256] for t in range(tiles)], axis=0)
    x = dot(swap, x).astype(bf16)
    z = dot(x, rights[0]) + dot(x, rights[1])
    sets = []
    for first in range(0, 16, 4):
        rows = [
            z[query * 16 : (query + 1) * 16, s * 128 : (s + 1) * 128]
            for query in range(first, first + 4)
            for s in range(4)
        ]
        sets.append(jnp.concatenate(rows, axis=0))
    high, low = split(jnp.concatenate(sets, axis=1), 2)
    z = dot(lefts[0], high) + (dot(lefts[0], low) + dot(lefts[1], high))
    side = iota((16, 128), 1) < 64
    rows = []
    for first in range(4):
        for k in range(4):
            o = z[k * 64 : (k + 1) * 64, first * 128 : (first + 1) * 128]
            pair = [jnp.where(side, o[0:16], o[16:32]), jnp.where(side, o[32:48], o[48:64])]
            rows.append(jnp.concatenate(pair, axis=1))
    y = dot(swap, jnp.concatenate(rows, axis=0).astype(bf16)).astype(bf16)
    return [y[t * 16 : (t + 1) * 16] for t in range(tiles)]


def own_kernel(q_hbm, left_hbm, right_hbm, mine, lefts_ref, rights_ref, q_ref, left, right, sems):
    at = pl.multiple_of(lax.axis_index("parts") * HALF, HALF)
    copies = [
        pltpu.make_async_copy(source, target, sems.at[k])
        for k, (source, target) in enumerate(
            ((left_hbm, left), (right_hbm, right), (q_hbm.at[pl.ds(at, HALF), :], q_ref))
        )
    ]
    for copy in copies:
        copy.start()
    copies[0].wait()
    copies[1].wait()
    lefts, rights = factors(left[...], right[...])
    for k in range(2):
        lefts_ref[k] = lefts[k]
        rights_ref[k] = rights[k]
    copies[2].wait()
    precond_rows(q_ref, lefts, rights, mine, 0)


def rest_kernel(
    weight_ref, layer_ref, q_hbm, train_hbm, lefts_ref, rights_ref, rest, train, weight, q_ref, sems
):
    at = pl.multiple_of((1 - lax.axis_index("parts")) * HALF, HALF)
    q_copy = pltpu.make_async_copy(q_hbm.at[pl.ds(at, HALF), :], q_ref, sems.at[0])
    q_copy.start()
    copies = []
    for k in range(train.shape[0] // STEP):
        here = pl.ds(k * STEP, STEP)
        copies.append(pltpu.make_async_copy(train_hbm.at[here, :], train.at[here, :], sems.at[1 + k]))
        copies[-1].start()
    weight[...] = jnp.full(weight.shape, weight_ref[layer_ref[0]])
    lefts, rights = [lefts_ref[0], lefts_ref[1]], [rights_ref[0], rights_ref[1]]
    q_copy.wait()
    precond_rows(q_ref, lefts, rights, rest, 0)
    for copy in copies:
        copy.wait()


def score_kernel(weight_ref, train_ref, *refs, picks, stored, early):
    inputs, refs = refs[: len(picks)], refs[len(picks) :]
    n_before = sum(taken for _, _, taken in early)
    before, outs = refs[:n_before], refs[n_before:]
    weight = weight_ref[0:1, :]
    queries = jnp.concatenate(
        [piece[at : at + n, :] for piece, rows in zip(inputs, picks) for at, n in rows], axis=0
    )
    _, z, _, layer = place()
    near_is_mine = z // 2 == layer
    for at in range(0, train_ref.shape[0], STEP):
        here = slice(at, at + STEP)
        value = lax.dot_general(
            train_ref[here, :], queries, (((1,), (1,)), ((), ())), preferred_element_type=f32
        )
        value = weight * value.T
        if stored:
            outs[0][:, here] = value[:stored]
        if early:
            send, keep = outs[-2:]
            old, given = [], list(before)
            for first, rows, taken in early:
                old.append(
                    given.pop(0)[first : first + rows, here] if taken else value[first : first + rows]
                )
            old, new = jnp.concatenate(old, axis=0), value[stored:]
            send[:, here] = jnp.where(near_is_mine, new, old).astype(send.dtype)
            keep[:, here] = jnp.where(near_is_mine, old, new)


def kernel_call(kernel, outs, inputs, specs=None, scratch=()):
    return pl.pallas_call(
        kernel,
        out_shape=outs,
        in_specs=specs or [VMEM] * len(inputs),
        out_specs=[VMEM] * len(outs) if isinstance(outs, list) else VMEM,
        scratch_shapes=scratch,
        compiler_params=pltpu.CompilerParams(vmem_limit_bytes=LIMIT),
    )(*inputs)


def call_scores(weight, train, inputs, stored=0, early=()):
    n = train.shape[0]
    total = sum(count for _, rows in inputs for _, count in rows)
    outs = [jax.ShapeDtypeStruct((stored, n), f32)] if stored else []
    if early:
        outs += [jax.ShapeDtypeStruct((total - stored, n), t) for t in (bf16, f32)]
    return kernel_call(
        functools.partial(
            score_kernel,
            picks=[rows for _, rows in inputs],
            stored=stored,
            early=[(first, rows, a is not None) for a, first, rows in early],
        ),
        outs,
        [weight, train, *[a for a, _ in inputs], *[a for a, _, _ in early if a is not None]],
    )


def final_kernel(train_ids, query_ids, *refs, groups):
    out = refs[-1]
    part, z, core, layer = place()
    low = z % 2
    first = jnp.where(z // 2 == layer, low, 1 - low)
    ids = train_ids[...]
    for k, (block, start, rows) in enumerate(groups):
        keep, got = refs[2 * k], refs[2 * k + 1]
        block = first if block == 0 else 1 - first
        for i in range(4):
            c = core if i < 2 else 1 - core
            h = part if i % 2 == 0 else 1 - part
            at = pl.multiple_of(((block * 2 + c) * 2 + h) * HALF + start, CHUNK)
            here = slice(i * rows, (i + 1) * rows)
            total = keep[here, :] + got[here, :].astype(f32)
            same = query_ids[pl.ds(at, rows), :] == ids
            out[pl.ds(at, rows), :] = jnp.where(same, jnp.float32(0.0), total)


def small(
    train_grads,
    query_grads,
    left_factor,
    right_factor,
    layer_weight,
    layer_of,
    train_ids,
    query_ids,
):
    train, queries = train_grads[:, 0, :], query_grads[:, 0, :]
    width, side = queries.shape[1], left_factor.shape[1]
    shape = jax.ShapeDtypeStruct
    mine, lefts, rights = kernel_call(
        own_kernel,
        [shape((HALF, width), bf16), shape((2, 256, 256), bf16), shape((2, 256, 512), bf16)],
        [queries, left_factor[0], right_factor[0]],
        [HBM] * 3,
        [
            pltpu.VMEM((HALF, width), bf16),
            pltpu.VMEM((side, side), f32),
            pltpu.VMEM((side, side), f32),
            pltpu.SemaphoreType.DMA((3,)),
        ],
    )
    near = to_near(mine, "near")
    far = to_far(mine, "far")
    rest, train, weight = kernel_call(
        rest_kernel,
        [shape((HALF, width), bf16), shape(train.shape, bf16), shape((8, STEP), f32)],
        [layer_weight, layer_of, queries, train, lefts, rights],
        [SMEM, SMEM, HBM, HBM, VMEM, VMEM],
        [pltpu.VMEM((HALF, width), bf16), pltpu.SemaphoreType.DMA((1 + train.shape[0] // STEP,))],
    )
    score = functools.partial(call_scores, weight, train)
    whole = lambda *pieces: [(piece, ((0, HALF),)) for piece in pieces]

    mine_x = to_core(mine, "mine_x")
    rest_x = to_core(rest, "rest_x")
    near_x = to_core(near, "near_x")
    near_p = to_part(near, "near_p")
    far = after(far, near)
    cross = to_near(far, "cross")
    far_p = to_part(far, "far_p")
    far_x = to_core(far, "far_x")
    rest_x = after(rest_x, far)
    (early0,) = score(whole(mine, rest, mine_x, rest_x), stored=128)
    near_p = after(near_p, early0)
    near_px = to_core(near_p, "near_px")
    far_px = to_core(far_p, "far_px")
    cross_p = to_part(cross, "cross_p")
    cross_x = to_core(cross, "cross_x")
    early1, send0, keep0 = score(
        whole(near, near_p, near_x, near_px, far, far_p, far_x, far_px),
        stored=128,
        early=[(early0, 0, 128)],
    )
    got0 = to_layer(send0, "got0")
    cross_p = after(cross_p, send0)
    cross_px = to_core(cross_p, "cross_px")
    send1, keep1 = score(whole(cross, cross_p, cross_x, cross_px), early=[(early1, 0, 128)])
    got1 = to_layer(send1, "got1")
    return kernel_call(
        functools.partial(final_kernel, groups=((0, 0, HALF), (1, 0, HALF))),
        shape((query_ids.shape[0], train_ids.shape[0]), f32),
        [train_ids[None, :], query_ids[:, None], keep0, got0, keep1, got1],
    )


def solution(mesh):
    placed = (
        P(("parts", "store"), "layer", None),
        P("store", "layer", None),
        P("layer", None, None),
        P("layer", None, None),
        P(),
        P("layer"),
        P(("parts", "store")),
        P("layer"),
    )
    sizes = tuple(mesh.shape[axis] for axis in AXES)
    return jax.shard_map(
        small if sizes == (PARTS, CHIPS * CORES, LAYERS) else general,
        mesh=mesh,
        in_specs=placed,
        out_specs=P("layer", ("parts", "store")),
        check_vma=False,
    )
```

```python
import functools

import jax
import jax.numpy as jnp
from jax import lax
from jax.experimental import pallas as pl
from jax.experimental.pallas import tpu as pltpu
from jax.sharding import PartitionSpec as P

AXES = ("parts", "store", "layer")
VMEM = pl.BlockSpec(memory_space=pltpu.VMEM)
SMEM = pl.BlockSpec(memory_space=pltpu.SMEM)
bf16, f32 = jnp.bfloat16, jnp.float32
LIMIT = 20 * 1024 * 1024


def preconditioned(query_grads, left_factor, right_factor):
    q_rows, slots, width = query_grads.shape
    side = left_factor.shape[1]
    mats = query_grads.astype(jnp.float32).reshape(q_rows, slots, side, side)
    half = jnp.einsum("lij,qljk->qlik", left_factor, mats, precision=lax.Precision.HIGHEST)
    full = jnp.einsum("qlik,lkm->qlim", half, right_factor, precision=lax.Precision.HIGHEST)
    return full.reshape(q_rows, slots, width).astype(jnp.bfloat16)


def general(
    train_grads,
    query_grads,
    left_factor,
    right_factor,
    layer_weight,
    layer_of,
    train_ids,
    query_ids,
):
    precond = preconditioned(query_grads, left_factor, right_factor)
    weight = jnp.take(layer_weight, layer_of[0])
    queries = lax.all_gather(precond, "store", axis=0, tiled=True)
    terms = weight * jnp.dot(
        queries[:, 0, :], train_grads[:, 0, :].T, preferred_element_type=jnp.float32
    )
    summed = lax.psum_scatter(terms, "layer", scatter_dimension=0, tiled=True)
    same = query_ids[:, None] == train_ids[None, :]
    return jnp.where(same, jnp.float32(0.0), summed)


PARTS, CHIPS, CORES, LAYERS = 2, 4, 2, 2
CHUNK = 16
HALF = 2 * CHUNK
STEP = 256
HBM = pl.BlockSpec(memory_space=pltpu.HBM)


def permute(value, name, target):
    pairs = []
    for p in range(PARTS):
        for z in range(CHIPS):
            for c in range(CORES):
                for l in range(LAYERS):
                    tp, tz, tc, tl = target(p, z, c, l)
                    source = ((p * CHIPS + z) * CORES + c) * LAYERS + l
                    pairs.append((source, ((tp * CHIPS + tz) * CORES + tc) * LAYERS + tl))
    with jax.named_scope(name):
        return lax.ppermute(value, AXES, pairs)


to_part = functools.partial(permute, target=lambda p, z, c, l: (1 - p, z, c, l))
to_core = functools.partial(permute, target=lambda p, z, c, l: (p, z, 1 - c, l))
to_layer = functools.partial(permute, target=lambda p, z, c, l: (p, z, c, 1 - l))
to_near = functools.partial(permute, target=lambda p, z, c, l: (p, z ^ 1, c, l))
to_far = functools.partial(permute, target=lambda p, z, c, l: (p, z ^ 3, c, l))


def after(value, *others):
    return lax.optimization_barrier((value, *others))[0]


def place():
    store = lax.axis_index("store")
    return lax.axis_index("parts"), store // CORES, store % CORES, lax.axis_index("layer")


def split(x, terms):
    out = []
    for _ in range(terms):
        term = x.astype(bf16)
        out.append(term)
        x = x - term.astype(f32)
    return out


def dot(a, b):
    return lax.dot_general(a, b, (((1,), (0,)), ((), ())), preferred_element_type=f32)


def iota(shape, dim):
    return lax.broadcasted_iota(jnp.int32, shape, dim)


def factors(left, right):
    r, c = iota((256, 64), 0), iota((256, 64), 1)
    pick = jnp.where(c == 4 * (r % 16) + (r // 16) % 4, 1.0, 0.0).astype(bf16)
    r, c = iota((64, 256), 0), iota((64, 256), 1)
    pick_t = jnp.where(r == 4 * (c % 16) + (c // 16) % 4, 1.0, 0.0).astype(bf16)
    block = iota((256, 256), 0) // 64 == iota((256, 256), 1) // 64
    lefts = [
        jnp.where(block, dot(dot(pick, term).astype(bf16), pick_t), 0.0).astype(bf16)
        for term in split(left, 2)
    ]
    row = jnp.concatenate([right, right], axis=1)
    tiled = jnp.concatenate([jnp.concatenate([row] * 4, axis=1)] * 4, axis=0)
    block = iota((256, 512), 0) // 64 == iota((256, 512), 1) // 128
    return lefts, split(jnp.where(block, tiled, 0.0), 2)


def precond_rows(q_ref, lefts, rights, out):
    for at in range(0, q_ref.shape[0], CHUNK):
        values = precond_chunk(q_ref[at : at + CHUNK, :], lefts, rights)
        for t, value in enumerate(values):
            out[at : at + CHUNK, t * 256 : (t + 1) * 256] = value


def precond_chunk(q, lefts, rights):
    tiles = q.shape[1] // 256
    r, c = iota((256, 256), 0), iota((256, 256), 1)
    swap = jnp.where((r // 16 == c % 16) & (r % 16 == c // 16), 1.0, 0.0).astype(bf16)
    x = jnp.concatenate([q[:, t * 256 : (t + 1) * 256] for t in range(tiles)], axis=0)
    x = dot(swap, x).astype(bf16)
    z = dot(x, rights[0]) + dot(x, rights[1])
    sets = []
    for first in range(0, 16, 4):
        rows = [
            z[query * 16 : (query + 1) * 16, s * 128 : (s + 1) * 128]
            for query in range(first, first + 4)
            for s in range(4)
        ]
        sets.append(jnp.concatenate(rows, axis=0))
    high, low = split(jnp.concatenate(sets, axis=1), 2)
    z = dot(lefts[0], high) + (dot(lefts[0], low) + dot(lefts[1], high))
    side = iota((16, 128), 1) < 64
    rows = []
    for first in range(4):
        for k in range(4):
            o = z[k * 64 : (k + 1) * 64, first * 128 : (first + 1) * 128]
            pair = [jnp.where(side, o[0:16], o[16:32]), jnp.where(side, o[32:48], o[48:64])]
            rows.append(jnp.concatenate(pair, axis=1))
    y = dot(swap, jnp.concatenate(rows, axis=0).astype(bf16)).astype(bf16)
    return [y[t * 16 : (t + 1) * 16] for t in range(tiles)]


def own_kernel(q_hbm, left_hbm, right_hbm, mine, lefts_ref, rights_ref, q_ref, left, right, sems):
    at = pl.multiple_of(lax.axis_index("parts") * HALF, HALF)
    copies = [
        pltpu.make_async_copy(source, target, sems.at[k])
        for k, (source, target) in enumerate(
            ((left_hbm, left), (right_hbm, right), (q_hbm.at[pl.ds(at, HALF), :], q_ref))
        )
    ]
    for copy in copies:
        copy.start()
    copies[0].wait()
    copies[1].wait()
    lefts, rights = factors(left[...], right[...])
    for k in range(2):
        lefts_ref[k] = lefts[k]
        rights_ref[k] = rights[k]
    copies[2].wait()
    precond_rows(q_ref, lefts, rights, mine)


def rest_kernel(
    weight_ref, layer_ref, q_hbm, train_hbm, lefts_ref, rights_ref, rest, train, weight, q_ref, sems
):
    at = pl.multiple_of((1 - lax.axis_index("parts")) * HALF, HALF)
    q_copy = pltpu.make_async_copy(q_hbm.at[pl.ds(at, HALF), :], q_ref, sems.at[0])
    q_copy.start()
    copies = []
    for k in range(train.shape[0] // STEP):
        here = pl.ds(k * STEP, STEP)
        copies.append(pltpu.make_async_copy(train_hbm.at[here, :], train.at[here, :], sems.at[1 + k]))
        copies[-1].start()
    weight[...] = jnp.full(weight.shape, weight_ref[layer_ref[0]])
    lefts, rights = [lefts_ref[0], lefts_ref[1]], [rights_ref[0], rights_ref[1]]
    q_copy.wait()
    precond_rows(q_ref, lefts, rights, rest)
    for copy in copies:
        copy.wait()


def score_kernel(weight_ref, train_ref, *refs, picks, stored, early):
    inputs, refs = refs[: len(picks)], refs[len(picks) :]
    n_before = sum(taken for _, _, taken in early)
    before, outs = refs[:n_before], refs[n_before:]
    weight = weight_ref[0:1, :]
    queries = jnp.concatenate(
        [piece[at : at + n, :] for piece, rows in zip(inputs, picks) for at, n in rows], axis=0
    )
    _, z, _, layer = place()
    near_is_mine = z // 2 == layer
    for at in range(0, train_ref.shape[0], STEP):
        here = slice(at, at + STEP)
        value = lax.dot_general(
            train_ref[here, :], queries, (((1,), (1,)), ((), ())), preferred_element_type=f32
        )
        value = weight * value.T
        if stored:
            outs[0][:, here] = value[:stored]
        if early:
            send, keep = outs[-2:]
            old, given = [], list(before)
            for first, rows, taken in early:
                old.append(
                    given.pop(0)[first : first + rows, here] if taken else value[first : first + rows]
                )
            old, new = jnp.concatenate(old, axis=0), value[stored:]
            send[:, here] = jnp.where(near_is_mine, new, old).astype(send.dtype)
            keep[:, here] = jnp.where(near_is_mine, old, new)


def kernel_call(kernel, outs, inputs, specs=None, scratch=()):
    return pl.pallas_call(
        kernel,
        out_shape=outs,
        in_specs=specs or [VMEM] * len(inputs),
        out_specs=[VMEM] * len(outs) if isinstance(outs, list) else VMEM,
        scratch_shapes=scratch,
        compiler_params=pltpu.CompilerParams(vmem_limit_bytes=LIMIT),
    )(*inputs)


def call_scores(weight, train, inputs, stored=0, early=()):
    n = train.shape[0]
    total = sum(count for _, rows in inputs for _, count in rows)
    outs = [jax.ShapeDtypeStruct((stored, n), f32)] if stored else []
    if early:
        outs += [jax.ShapeDtypeStruct((total - stored, n), t) for t in (bf16, f32)]
    return kernel_call(
        functools.partial(
            score_kernel,
            picks=[rows for _, rows in inputs],
            stored=stored,
            early=[(first, rows, a is not None) for a, first, rows in early],
        ),
        outs,
        [weight, train, *[a for a, _ in inputs], *[a for a, _, _ in early if a is not None]],
    )


def final_kernel(train_ids, query_ids, *refs, groups):
    out = refs[-1]
    part, z, core, layer = place()
    low = z % 2
    first = jnp.where(z // 2 == layer, low, 1 - low)
    ids = train_ids[...]
    for k, (block, start, rows) in enumerate(groups):
        keep, got = refs[2 * k], refs[2 * k + 1]
        block = first if block == 0 else 1 - first
        for i in range(4):
            c = core if i < 2 else 1 - core
            h = part if i % 2 == 0 else 1 - part
            at = pl.multiple_of(((block * 2 + c) * 2 + h) * HALF + start, CHUNK)
            here = slice(i * rows, (i + 1) * rows)
            total = keep[here, :] + got[here, :].astype(f32)
            same = query_ids[pl.ds(at, rows), :] == ids
            out[pl.ds(at, rows), :] = jnp.where(same, jnp.float32(0.0), total)


def small(
    train_grads,
    query_grads,
    left_factor,
    right_factor,
    layer_weight,
    layer_of,
    train_ids,
    query_ids,
):
    in_hbm = lambda array: pltpu.with_memory_space_constraint(array, pltpu.HBM)
    train, queries = in_hbm(train_grads[:, 0, :]), in_hbm(query_grads[:, 0, :])
    width, side = queries.shape[1], left_factor.shape[1]
    shape = jax.ShapeDtypeStruct
    mine, lefts, rights = kernel_call(
        own_kernel,
        [shape((HALF, width), bf16), shape((2, 256, 256), bf16), shape((2, 256, 512), bf16)],
        [queries, in_hbm(left_factor[0]), in_hbm(right_factor[0])],
        [HBM] * 3,
        [
            pltpu.VMEM((HALF, width), bf16),
            pltpu.VMEM((side, side), f32),
            pltpu.VMEM((side, side), f32),
            pltpu.SemaphoreType.DMA((3,)),
        ],
    )
    near = to_near(mine, "near")
    far = to_far(mine, "far")
    rest, train, weight = kernel_call(
        rest_kernel,
        [shape((HALF, width), bf16), shape(train.shape, bf16), shape((8, STEP), f32)],
        [in_hbm(layer_weight), layer_of, queries, train, lefts, rights],
        [SMEM, SMEM, HBM, HBM, VMEM, VMEM],
        [pltpu.VMEM((HALF, width), bf16), pltpu.SemaphoreType.DMA((1 + train.shape[0] // STEP,))],
    )
    score = functools.partial(call_scores, weight, train)

    def rows_of(*pieces):
        return [(piece, ((0, piece.shape[0]),)) for piece in pieces]

    mine_x = to_core(mine, "mine_x")
    rest_x = to_core(rest, "rest_x")
    near_x = to_core(near, "near_x")
    near_p = to_part(near, "near_p")
    far = after(far, near)
    cross = to_near(far, "cross")
    far_p = to_part(far, "far_p")
    far_x = to_core(far, "far_x")
    rest_x = after(rest_x, far)
    (early0,) = score(rows_of(mine, rest, mine_x, rest_x), stored=128)
    near_p = after(near_p, early0)
    near_px = to_core(near_p, "near_px")
    far_px = to_core(far_p, "far_px")
    cross_p = to_part(cross, "cross_p")
    cross_x = to_core(cross, "cross_x")
    early1, send0, keep0 = score(
        rows_of(near, near_p, near_x, near_px, far, far_p, far_x, far_px),
        stored=128,
        early=[(early0, 0, 128)],
    )
    got0 = to_layer(send0, "got0")
    cross_p = after(cross_p, send0)
    cross_pxa = to_core(cross_p[:CHUNK], "cross_pxa")
    cross_pxb = to_core(cross_p[CHUNK:], "cross_pxb")
    send1, keep1 = score(
        rows_of(cross, cross_p, cross_x, cross_pxa, cross_pxb), early=[(early1, 0, 128)]
    )
    send1 = after(send1, got0)
    got1 = to_layer(send1, "got1")
    return kernel_call(
        functools.partial(final_kernel, groups=((0, 0, HALF), (1, 0, HALF))),
        shape((query_ids.shape[0], train_ids.shape[0]), f32),
        [train_ids[None, :], query_ids[:, None], keep0, got0, keep1, got1],
    )


def solution(mesh):
    placed = (
        P(("parts", "store"), "layer", None),
        P("store", "layer", None),
        P("layer", None, None),
        P("layer", None, None),
        P(),
        P("layer"),
        P(("parts", "store")),
        P("layer"),
    )
    sizes = tuple(mesh.shape[axis] for axis in AXES)
    return jax.shard_map(
        small if sizes == (PARTS, CHIPS * CORES, LAYERS) else general,
        mesh=mesh,
        in_specs=placed,
        out_specs=P("layer", ("parts", "store")),
        check_vma=False,
    )
```

```python
import functools

import jax
import jax.numpy as jnp
from jax import lax
from jax.experimental import pallas as pl
from jax.experimental.pallas import tpu as pltpu
from jax.sharding import PartitionSpec as P

AXES = ("parts", "store", "layer")
VMEM = pl.BlockSpec(memory_space=pltpu.VMEM)
SMEM = pl.BlockSpec(memory_space=pltpu.SMEM)
bf16, f32 = jnp.bfloat16, jnp.float32
LIMIT = 20 * 1024 * 1024


def preconditioned(query_grads, left_factor, right_factor):
    q_rows, slots, width = query_grads.shape
    side = left_factor.shape[1]
    mats = query_grads.astype(jnp.float32).reshape(q_rows, slots, side, side)
    half = jnp.einsum("lij,qljk->qlik", left_factor, mats, precision=lax.Precision.HIGHEST)
    full = jnp.einsum("qlik,lkm->qlim", half, right_factor, precision=lax.Precision.HIGHEST)
    return full.reshape(q_rows, slots, width).astype(jnp.bfloat16)


def general(
    train_grads,
    query_grads,
    left_factor,
    right_factor,
    layer_weight,
    layer_of,
    train_ids,
    query_ids,
):
    precond = preconditioned(query_grads, left_factor, right_factor)
    weight = jnp.take(layer_weight, layer_of[0])
    queries = lax.all_gather(precond, "store", axis=0, tiled=True)
    terms = weight * jnp.dot(
        queries[:, 0, :], train_grads[:, 0, :].T, preferred_element_type=jnp.float32
    )
    summed = lax.psum_scatter(terms, "layer", scatter_dimension=0, tiled=True)
    same = query_ids[:, None] == train_ids[None, :]
    return jnp.where(same, jnp.float32(0.0), summed)


PARTS, CHIPS, CORES, LAYERS = 2, 4, 2, 2
CHUNK = 16
HALF = 2 * CHUNK
STEP = 256
HBM = pl.BlockSpec(memory_space=pltpu.HBM)


def permute(value, name, target):
    pairs = []
    for p in range(PARTS):
        for z in range(CHIPS):
            for c in range(CORES):
                for l in range(LAYERS):
                    tp, tz, tc, tl = target(p, z, c, l)
                    source = ((p * CHIPS + z) * CORES + c) * LAYERS + l
                    pairs.append((source, ((tp * CHIPS + tz) * CORES + tc) * LAYERS + tl))
    with jax.named_scope(name):
        return lax.ppermute(value, AXES, pairs)


to_part = functools.partial(permute, target=lambda p, z, c, l: (1 - p, z, c, l))
to_core = functools.partial(permute, target=lambda p, z, c, l: (p, z, 1 - c, l))
to_layer = functools.partial(permute, target=lambda p, z, c, l: (p, z, c, 1 - l))
to_near = functools.partial(permute, target=lambda p, z, c, l: (p, z ^ 1, c, l))
to_far = functools.partial(permute, target=lambda p, z, c, l: (p, z ^ 3, c, l))


def after(value, *others):
    return lax.optimization_barrier((value, *others))[0]


def place():
    store = lax.axis_index("store")
    return lax.axis_index("parts"), store // CORES, store % CORES, lax.axis_index("layer")


def split(x, terms):
    out = []
    for _ in range(terms):
        term = x.astype(bf16)
        out.append(term)
        x = x - term.astype(f32)
    return out


def dot(a, b):
    return lax.dot_general(a, b, (((1,), (0,)), ((), ())), preferred_element_type=f32)


def iota(shape, dim):
    return lax.broadcasted_iota(jnp.int32, shape, dim)


def factors(left, right):
    r, c = iota((256, 64), 0), iota((256, 64), 1)
    pick = jnp.where(c == 4 * (r % 16) + (r // 16) % 4, 1.0, 0.0).astype(bf16)
    r, c = iota((64, 256), 0), iota((64, 256), 1)
    pick_t = jnp.where(r == 4 * (c % 16) + (c // 16) % 4, 1.0, 0.0).astype(bf16)
    block = iota((256, 256), 0) // 64 == iota((256, 256), 1) // 64
    lefts = [
        jnp.where(block, dot(dot(pick, term).astype(bf16), pick_t), 0.0).astype(bf16)
        for term in split(left, 2)
    ]
    row = jnp.concatenate([right, right], axis=1)
    tiled = jnp.concatenate([jnp.concatenate([row] * 4, axis=1)] * 4, axis=0)
    block = iota((256, 512), 0) // 64 == iota((256, 512), 1) // 128
    return lefts, split(jnp.where(block, tiled, 0.0), 2)


def precond_rows(q_ref, lefts, rights, out):
    for at in range(0, q_ref.shape[0], CHUNK):
        values = precond_chunk(q_ref[at : at + CHUNK, :], lefts, rights)
        for t, value in enumerate(values):
            out[at : at + CHUNK, t * 256 : (t + 1) * 256] = value


def precond_chunk(q, lefts, rights):
    tiles = q.shape[1] // 256
    r, c = iota((256, 256), 0), iota((256, 256), 1)
    swap = jnp.where((r // 16 == c % 16) & (r % 16 == c // 16), 1.0, 0.0).astype(bf16)
    x = jnp.concatenate([q[:, t * 256 : (t + 1) * 256] for t in range(tiles)], axis=0)
    x = dot(swap, x).astype(bf16)
    z = dot(x, rights[0]) + dot(x, rights[1])
    sets = []
    for first in range(0, 16, 4):
        rows = [
            z[query * 16 : (query + 1) * 16, s * 128 : (s + 1) * 128]
            for query in range(first, first + 4)
            for s in range(4)
        ]
        sets.append(jnp.concatenate(rows, axis=0))
    high, low = split(jnp.concatenate(sets, axis=1), 2)
    z = dot(lefts[0], high) + (dot(lefts[0], low) + dot(lefts[1], high))
    side = iota((16, 128), 1) < 64
    rows = []
    for first in range(4):
        for k in range(4):
            o = z[k * 64 : (k + 1) * 64, first * 128 : (first + 1) * 128]
            pair = [jnp.where(side, o[0:16], o[16:32]), jnp.where(side, o[32:48], o[48:64])]
            rows.append(jnp.concatenate(pair, axis=1))
    y = dot(swap, jnp.concatenate(rows, axis=0).astype(bf16)).astype(bf16)
    return [y[t * 16 : (t + 1) * 16] for t in range(tiles)]


def own_kernel(q_hbm, left_hbm, right_hbm, mine, lefts_ref, rights_ref, q_ref, left, right, sems):
    at = pl.multiple_of(lax.axis_index("parts") * HALF, HALF)
    copies = [
        pltpu.make_async_copy(source, target, sems.at[k])
        for k, (source, target) in enumerate(
            ((left_hbm, left), (right_hbm, right), (q_hbm.at[pl.ds(at, HALF), :], q_ref))
        )
    ]
    for copy in copies:
        copy.start()
    copies[0].wait()
    copies[1].wait()
    lefts, rights = factors(left[...], right[...])
    for k in range(2):
        lefts_ref[k] = lefts[k]
        rights_ref[k] = rights[k]
    copies[2].wait()
    precond_rows(q_ref, lefts, rights, mine)


def rest_kernel(
    weight_ref, layer_ref, q_hbm, train_hbm, lefts_ref, rights_ref, rest, train, weight, q_ref, sems
):
    at = pl.multiple_of((1 - lax.axis_index("parts")) * HALF, HALF)
    q_copy = pltpu.make_async_copy(q_hbm.at[pl.ds(at, HALF), :], q_ref, sems.at[0])
    q_copy.start()
    copies = []
    for k in range(train.shape[0] // STEP):
        here = pl.ds(k * STEP, STEP)
        copies.append(pltpu.make_async_copy(train_hbm.at[here, :], train.at[here, :], sems.at[1 + k]))
        copies[-1].start()
    weight[...] = jnp.full(weight.shape, weight_ref[layer_ref[0]])
    lefts, rights = [lefts_ref[0], lefts_ref[1]], [rights_ref[0], rights_ref[1]]
    q_copy.wait()
    precond_rows(q_ref, lefts, rights, rest)
    for copy in copies:
        copy.wait()


def score_kernel(weight_ref, train_ref, *refs, picks, stored, early):
    inputs, refs = refs[: len(picks)], refs[len(picks) :]
    n_before = sum(taken for _, _, taken in early)
    before, outs = refs[:n_before], refs[n_before:]
    weight = weight_ref[0:1, :]
    queries = jnp.concatenate(
        [piece[at : at + n, :] for piece, rows in zip(inputs, picks) for at, n in rows], axis=0
    )
    _, z, _, layer = place()
    near_is_mine = z // 2 == layer
    for at in range(0, train_ref.shape[0], STEP):
        here = slice(at, at + STEP)
        value = lax.dot_general(
            train_ref[here, :], queries, (((1,), (1,)), ((), ())), preferred_element_type=f32
        )
        value = weight * value.T
        if stored:
            outs[0][:, here] = value[:stored]
        if early:
            send, keep = outs[-2:]
            old, given = [], list(before)
            for first, rows, taken in early:
                old.append(
                    given.pop(0)[first : first + rows, here] if taken else value[first : first + rows]
                )
            old, new = jnp.concatenate(old, axis=0), value[stored:]
            send[:, here] = jnp.where(near_is_mine, new, old).astype(send.dtype)
            keep[:, here] = jnp.where(near_is_mine, old, new)


def kernel_call(kernel, outs, inputs, specs=None, scratch=()):
    return pl.pallas_call(
        kernel,
        out_shape=outs,
        in_specs=specs or [VMEM] * len(inputs),
        out_specs=[VMEM] * len(outs) if isinstance(outs, list) else VMEM,
        scratch_shapes=scratch,
        compiler_params=pltpu.CompilerParams(vmem_limit_bytes=LIMIT),
    )(*inputs)


def call_scores(weight, train, inputs, stored=0, early=()):
    n = train.shape[0]
    total = sum(count for _, rows in inputs for _, count in rows)
    outs = [jax.ShapeDtypeStruct((stored, n), f32)] if stored else []
    if early:
        outs += [jax.ShapeDtypeStruct((total - stored, n), t) for t in (bf16, f32)]
    return kernel_call(
        functools.partial(
            score_kernel,
            picks=[rows for _, rows in inputs],
            stored=stored,
            early=[(first, rows, a is not None) for a, first, rows in early],
        ),
        outs,
        [weight, train, *[a for a, _ in inputs], *[a for a, _, _ in early if a is not None]],
    )


def final_kernel(train_ids, query_ids, *refs):
    out = refs[-1]
    part, z, core, layer = place()
    low = z % 2
    first = jnp.where(z // 2 == layer, low, 1 - low)
    ids = train_ids[...]
    for k in range(4):
        keep, got = refs[2 * k], refs[2 * k + 1]
        block = first if k < 2 else 1 - first
        half = part if k % 2 == 0 else 1 - part
        for i, c in enumerate((core, 1 - core)):
            at = pl.multiple_of(((block * 2 + c) * 2 + half) * HALF, HALF)
            here = slice(i * HALF, (i + 1) * HALF)
            total = keep[here, :] + got[here, :].astype(f32)
            same = query_ids[pl.ds(at, HALF), :] == ids
            out[pl.ds(at, HALF), :] = jnp.where(same, jnp.float32(0.0), total)


def small(
    train_grads,
    query_grads,
    left_factor,
    right_factor,
    layer_weight,
    layer_of,
    train_ids,
    query_ids,
):
    in_hbm = lambda array: pltpu.with_memory_space_constraint(array, pltpu.HBM)
    train, queries = in_hbm(train_grads[:, 0, :]), in_hbm(query_grads[:, 0, :])
    width, side = queries.shape[1], left_factor.shape[1]
    shape = jax.ShapeDtypeStruct
    mine, lefts, rights = kernel_call(
        own_kernel,
        [shape((HALF, width), bf16), shape((2, 256, 256), bf16), shape((2, 256, 512), bf16)],
        [queries, in_hbm(left_factor[0]), in_hbm(right_factor[0])],
        [HBM] * 3,
        [
            pltpu.VMEM((HALF, width), bf16),
            pltpu.VMEM((side, side), f32),
            pltpu.VMEM((side, side), f32),
            pltpu.SemaphoreType.DMA((3,)),
        ],
    )
    near = to_near(mine, "near")
    far = to_far(mine, "far")
    rest, train, weight = kernel_call(
        rest_kernel,
        [shape((HALF, width), bf16), shape(train.shape, bf16), shape((8, STEP), f32)],
        [in_hbm(layer_weight), layer_of, queries, train, lefts, rights],
        [SMEM, SMEM, HBM, HBM, VMEM, VMEM],
        [pltpu.VMEM((HALF, width), bf16), pltpu.SemaphoreType.DMA((1 + train.shape[0] // STEP,))],
    )
    score = functools.partial(call_scores, weight, train)

    def rows_of(*pieces):
        return [(piece, ((0, piece.shape[0]),)) for piece in pieces]

    mine_x = to_core(mine, "mine_x")
    rest_x = to_core(rest, "rest_x")
    near = after(near, rest)
    near_x = to_core(near, "near_x")
    near_p = to_part(near, "near_p")
    far = after(far, near)
    cross = to_near(far, "cross")
    far_p = to_part(far, "far_p")
    far_xa = to_core(far[:CHUNK], "far_xa")
    far_xb = to_core(far[CHUNK:], "far_xb")
    early0, send0, keep0 = score(
        rows_of(mine, mine_x, rest, rest_x, far, far_xa, far_xb), stored=128, early=[(None, 0, 64)]
    )
    got0 = to_layer(send0, "got0")

    near_p = after(near_p, send0)
    near_px = to_core(near_p, "near_px")
    far_pxa = to_core(far_p[:CHUNK], "far_pxa")
    far_pxb = to_core(far_p[CHUNK:], "far_pxb")
    cross_pa = to_part(cross[:CHUNK], "cross_pa")
    cross_pb = to_near(far_p[CHUNK:], "cross_pb")
    cross_xa = to_core(cross[:CHUNK], "cross_xa")
    cross_xb = to_core(cross[CHUNK:], "cross_xb")
    early1, send1, keep1 = score(
        rows_of(near, near_x, near_p, near_px, far_p, far_pxa, far_pxb),
        stored=128,
        early=[(early0, 64, 64)],
    )
    got1 = to_layer(send1, "got1")

    send2, keep2 = score(rows_of(cross, cross_xa, cross_xb), early=[(early1, 0, 64)])
    got2 = to_layer(send2, "got2")

    cross_pa, cross_pb = after(cross_pa, send2, got0), after(cross_pb, send2, got0)
    cross_pxa = to_core(cross_pa, "cross_pxa")
    cross_pxb = to_core(cross_pb, "cross_pxb")
    send3, keep3 = score(
        rows_of(cross_pa, cross_pb, cross_pxa, cross_pxb), early=[(early1, 64, 64)]
    )
    send3 = after(send3, got1)
    got3 = to_layer(send3, "got3")
    return kernel_call(
        final_kernel,
        shape((query_ids.shape[0], train_ids.shape[0]), f32),
        [train_ids[None, :], query_ids[:, None], keep0, got0, keep1, got1, keep2, got2, keep3, got3],
    )


def solution(mesh):
    placed = (
        P(("parts", "store"), "layer", None),
        P("store", "layer", None),
        P("layer", None, None),
        P("layer", None, None),
        P(),
        P("layer"),
        P(("parts", "store")),
        P("layer"),
    )
    sizes = tuple(mesh.shape[axis] for axis in AXES)
    return jax.shard_map(
        small if sizes == (PARTS, CHIPS * CORES, LAYERS) else general,
        mesh=mesh,
        in_specs=placed,
        out_specs=P("layer", ("parts", "store")),
        check_vma=False,
    )
```

```python
import functools

import jax
import jax.numpy as jnp
from jax import lax
from jax.experimental import pallas as pl
from jax.experimental.pallas import tpu as pltpu
from jax.sharding import PartitionSpec as P

AXES = ("parts", "store", "layer")
VMEM = pl.BlockSpec(memory_space=pltpu.VMEM)
SMEM = pl.BlockSpec(memory_space=pltpu.SMEM)
bf16, f32 = jnp.bfloat16, jnp.float32
LIMIT = 20 * 1024 * 1024


def preconditioned(query_grads, left_factor, right_factor):
    q_rows, slots, width = query_grads.shape
    side = left_factor.shape[1]
    mats = query_grads.astype(jnp.float32).reshape(q_rows, slots, side, side)
    half = jnp.einsum("lij,qljk->qlik", left_factor, mats, precision=lax.Precision.HIGHEST)
    full = jnp.einsum("qlik,lkm->qlim", half, right_factor, precision=lax.Precision.HIGHEST)
    return full.reshape(q_rows, slots, width).astype(jnp.bfloat16)


def general(
    train_grads,
    query_grads,
    left_factor,
    right_factor,
    layer_weight,
    layer_of,
    train_ids,
    query_ids,
):
    precond = preconditioned(query_grads, left_factor, right_factor)
    weight = jnp.take(layer_weight, layer_of[0])
    queries = lax.all_gather(precond, "store", axis=0, tiled=True)
    terms = weight * jnp.dot(
        queries[:, 0, :], train_grads[:, 0, :].T, preferred_element_type=jnp.float32
    )
    summed = lax.psum_scatter(terms, "layer", scatter_dimension=0, tiled=True)
    same = query_ids[:, None] == train_ids[None, :]
    return jnp.where(same, jnp.float32(0.0), summed)


PARTS, CHIPS, CORES, LAYERS = 2, 4, 2, 2
CHUNK = 16
HALF = 2 * CHUNK
STEP = 256
HBM = pl.BlockSpec(memory_space=pltpu.HBM)


def permute(value, name, target):
    pairs = []
    for p in range(PARTS):
        for z in range(CHIPS):
            for c in range(CORES):
                for l in range(LAYERS):
                    tp, tz, tc, tl = target(p, z, c, l)
                    source = ((p * CHIPS + z) * CORES + c) * LAYERS + l
                    pairs.append((source, ((tp * CHIPS + tz) * CORES + tc) * LAYERS + tl))
    with jax.named_scope(name):
        return lax.ppermute(value, AXES, pairs)


to_part = functools.partial(permute, target=lambda p, z, c, l: (1 - p, z, c, l))
to_core = functools.partial(permute, target=lambda p, z, c, l: (p, z, 1 - c, l))
to_layer = functools.partial(permute, target=lambda p, z, c, l: (p, z, c, 1 - l))
to_near = functools.partial(permute, target=lambda p, z, c, l: (p, z ^ 1, c, l))
to_far = functools.partial(permute, target=lambda p, z, c, l: (p, z ^ 3, c, l))


def after(value, *others):
    return lax.optimization_barrier((value, *others))[0]


def place():
    store = lax.axis_index("store")
    return lax.axis_index("parts"), store // CORES, store % CORES, lax.axis_index("layer")


def split(x, terms):
    out = []
    for _ in range(terms):
        term = x.astype(bf16)
        out.append(term)
        x = x - term.astype(f32)
    return out


def dot(a, b):
    return lax.dot_general(a, b, (((1,), (0,)), ((), ())), preferred_element_type=f32)


def iota(shape, dim):
    return lax.broadcasted_iota(jnp.int32, shape, dim)


def factors(left, right):
    r, c = iota((256, 64), 0), iota((256, 64), 1)
    pick = jnp.where(c == 4 * (r % 16) + (r // 16) % 4, 1.0, 0.0).astype(bf16)
    r, c = iota((64, 256), 0), iota((64, 256), 1)
    pick_t = jnp.where(r == 4 * (c % 16) + (c // 16) % 4, 1.0, 0.0).astype(bf16)
    block = iota((256, 256), 0) // 64 == iota((256, 256), 1) // 64
    lefts = [
        jnp.where(block, dot(dot(pick, term).astype(bf16), pick_t), 0.0).astype(bf16)
        for term in split(left, 2)
    ]
    row = jnp.concatenate([right, right], axis=1)
    tiled = jnp.concatenate([jnp.concatenate([row] * 4, axis=1)] * 4, axis=0)
    block = iota((256, 512), 0) // 64 == iota((256, 512), 1) // 128
    return lefts, split(jnp.where(block, tiled, 0.0), 2)


def precond_rows(q_ref, lefts, rights, out):
    for at in range(0, q_ref.shape[0], CHUNK):
        values = precond_chunk(q_ref[at : at + CHUNK, :], lefts, rights)
        for t, value in enumerate(values):
            out[at : at + CHUNK, t * 256 : (t + 1) * 256] = value


def precond_chunk(q, lefts, rights):
    tiles = q.shape[1] // 256
    r, c = iota((256, 256), 0), iota((256, 256), 1)
    swap = jnp.where((r // 16 == c % 16) & (r % 16 == c // 16), 1.0, 0.0).astype(bf16)
    x = jnp.concatenate([q[:, t * 256 : (t + 1) * 256] for t in range(tiles)], axis=0)
    x = dot(swap, x).astype(bf16)
    z = dot(x, rights[0]) + dot(x, rights[1])
    sets = []
    for first in range(0, 16, 4):
        rows = [
            z[query * 16 : (query + 1) * 16, s * 128 : (s + 1) * 128]
            for query in range(first, first + 4)
            for s in range(4)
        ]
        sets.append(jnp.concatenate(rows, axis=0))
    high, low = split(jnp.concatenate(sets, axis=1), 2)
    z = dot(lefts[0], high) + (dot(lefts[0], low) + dot(lefts[1], high))
    side = iota((16, 128), 1) < 64
    rows = []
    for first in range(4):
        for k in range(4):
            o = z[k * 64 : (k + 1) * 64, first * 128 : (first + 1) * 128]
            pair = [jnp.where(side, o[0:16], o[16:32]), jnp.where(side, o[32:48], o[48:64])]
            rows.append(jnp.concatenate(pair, axis=1))
    y = dot(swap, jnp.concatenate(rows, axis=0).astype(bf16)).astype(bf16)
    return [y[t * 16 : (t + 1) * 16] for t in range(tiles)]


def own_kernel(q_hbm, left_hbm, right_hbm, mine, lefts_ref, rights_ref, q_ref, left, right, sems):
    at = pl.multiple_of(lax.axis_index("parts") * HALF, HALF)
    copies = [
        pltpu.make_async_copy(source, target, sems.at[k])
        for k, (source, target) in enumerate(
            ((left_hbm, left), (right_hbm, right), (q_hbm.at[pl.ds(at, HALF), :], q_ref))
        )
    ]
    for copy in copies:
        copy.start()
    copies[0].wait()
    copies[1].wait()
    lefts, rights = factors(left[...], right[...])
    for k in range(2):
        lefts_ref[k] = lefts[k]
        rights_ref[k] = rights[k]
    copies[2].wait()
    precond_rows(q_ref, lefts, rights, mine)


def rest_kernel(
    weight_ref, layer_ref, q_hbm, train_hbm, lefts_ref, rights_ref, rest, train, weight, q_ref, sems
):
    at = pl.multiple_of((1 - lax.axis_index("parts")) * HALF, HALF)
    q_copy = pltpu.make_async_copy(q_hbm.at[pl.ds(at, HALF), :], q_ref, sems.at[0])
    q_copy.start()
    copies = []
    for k in range(train.shape[0] // STEP):
        here = pl.ds(k * STEP, STEP)
        copies.append(pltpu.make_async_copy(train_hbm.at[here, :], train.at[here, :], sems.at[1 + k]))
        copies[-1].start()
    weight[...] = jnp.full(weight.shape, weight_ref[layer_ref[0]])
    lefts, rights = [lefts_ref[0], lefts_ref[1]], [rights_ref[0], rights_ref[1]]
    q_copy.wait()
    precond_rows(q_ref, lefts, rights, rest)
    for copy in copies:
        copy.wait()


def score_kernel(weight_ref, train_ref, *refs, picks, stored, early, columns):
    inputs, refs = refs[: len(picks)], refs[len(picks) :]
    n_before = sum(taken for _, _, taken in early)
    before, outs = refs[:n_before], refs[n_before:]
    weight = weight_ref[0:1, :]
    queries = jnp.concatenate(
        [piece[at : at + n, :] for piece, rows in zip(inputs, picks) for at, n in rows], axis=0
    )
    _, z, _, layer = place()
    near_is_mine = z // 2 == layer
    for at in range(*columns, STEP):
        there, here = slice(at, at + STEP), slice(at - columns[0], at - columns[0] + STEP)
        value = lax.dot_general(
            train_ref[there, :], queries, (((1,), (1,)), ((), ())), preferred_element_type=f32
        )
        value = weight * value.T
        if stored:
            outs[0][:, here] = value[:stored]
        if early:
            send, keep = outs[-2:]
            old, given = [], list(before)
            for first, rows, taken in early:
                old.append(
                    given.pop(0)[first : first + rows, there] if taken else value[first : first + rows]
                )
            old, new = jnp.concatenate(old, axis=0), value[stored:]
            send[:, here] = jnp.where(near_is_mine, new, old).astype(send.dtype)
            keep[:, here] = jnp.where(near_is_mine, old, new)


def kernel_call(kernel, outs, inputs, specs=None, scratch=()):
    return pl.pallas_call(
        kernel,
        out_shape=outs,
        in_specs=specs or [VMEM] * len(inputs),
        out_specs=[VMEM] * len(outs) if isinstance(outs, list) else VMEM,
        scratch_shapes=scratch,
        compiler_params=pltpu.CompilerParams(vmem_limit_bytes=LIMIT),
    )(*inputs)


def call_scores(weight, train, inputs, stored=0, early=(), columns=None):
    columns = columns or (0, train.shape[0])
    n = columns[1] - columns[0]
    total = sum(count for _, rows in inputs for _, count in rows)
    outs = [jax.ShapeDtypeStruct((stored, n), f32)] if stored else []
    if early:
        outs += [jax.ShapeDtypeStruct((total - stored, n), t) for t in (bf16, f32)]
    return kernel_call(
        functools.partial(
            score_kernel,
            picks=[rows for _, rows in inputs],
            stored=stored,
            early=[(first, rows, a is not None) for a, first, rows in early],
            columns=columns,
        ),
        outs,
        [weight, train, *[a for a, _ in inputs], *[a for a, _, _ in early if a is not None]],
    )


def final_kernel(train_ids, query_ids, *refs, groups, n_given):
    given, refs = refs[:n_given], refs[n_given:]
    *_, out, done, sems = refs
    part, z, core, layer = place()
    low = z % 2
    first = jnp.where(z // 2 == layer, low, 1 - low)
    copies = []
    for k, (which, terms) in enumerate(groups):
        block = first if which < 2 else 1 - first
        half = part if which % 2 == 0 else 1 - part
        for i, c in enumerate((core, 1 - core)):
            at = pl.multiple_of(((block * 2 + c) * 2 + half) * HALF, HALF)
            to = slice((2 * k + i) * HALF, (2 * k + i + 1) * HALF)
            ids = query_ids[pl.ds(at, HALF), :]
            for keep, got, row, column in terms:
                keep, got = given[keep], given[got]
                columns = slice(column, column + keep.shape[1])
                total = keep[row + i * HALF : row + (i + 1) * HALF, :]
                total = total + got[row + i * HALF : row + (i + 1) * HALF, :].astype(f32)
                same = ids == train_ids[:, columns]
                done[to, columns] = jnp.where(same, jnp.float32(0.0), total)
            copies.append(
                pltpu.make_async_copy(done.at[to, :], out.at[pl.ds(at, HALF), :], sems.at[2 * k + i])
            )
            copies[-1].start()
    for copy in copies:
        copy.wait()


def call_final(train_ids, query_ids, given, groups, before=None):
    rows, n = query_ids.shape[0], train_ids.shape[1]
    inputs = [train_ids, query_ids, *given] + ([] if before is None else [before])
    return pl.pallas_call(
        functools.partial(final_kernel, groups=groups, n_given=len(given)),
        out_shape=jax.ShapeDtypeStruct((rows, n), f32),
        in_specs=[VMEM] * (2 + len(given)) + ([] if before is None else [HBM]),
        out_specs=HBM,
        scratch_shapes=[
            pltpu.VMEM((2 * len(groups) * HALF, n), f32),
            pltpu.SemaphoreType.DMA((2 * len(groups),)),
        ],
        input_output_aliases={} if before is None else {len(inputs) - 1: 0},
        compiler_params=pltpu.CompilerParams(vmem_limit_bytes=LIMIT),
    )(*inputs)


def small(
    train_grads,
    query_grads,
    left_factor,
    right_factor,
    layer_weight,
    layer_of,
    train_ids,
    query_ids,
):
    in_hbm = lambda array: pltpu.with_memory_space_constraint(array, pltpu.HBM)
    train, queries = in_hbm(train_grads[:, 0, :]), in_hbm(query_grads[:, 0, :])
    width, side = queries.shape[1], left_factor.shape[1]
    shape = jax.ShapeDtypeStruct
    mine, lefts, rights = kernel_call(
        own_kernel,
        [shape((HALF, width), bf16), shape((2, 256, 256), bf16), shape((2, 256, 512), bf16)],
        [queries, in_hbm(left_factor[0]), in_hbm(right_factor[0])],
        [HBM] * 3,
        [
            pltpu.VMEM((HALF, width), bf16),
            pltpu.VMEM((side, side), f32),
            pltpu.VMEM((side, side), f32),
            pltpu.SemaphoreType.DMA((3,)),
        ],
    )
    near = to_near(mine, "near")
    far = to_far(mine, "far")
    rest, train, weight = kernel_call(
        rest_kernel,
        [shape((HALF, width), bf16), shape(train.shape, bf16), shape((8, STEP), f32)],
        [in_hbm(layer_weight), layer_of, queries, train, lefts, rights],
        [SMEM, SMEM, HBM, HBM, VMEM, VMEM],
        [pltpu.VMEM((HALF, width), bf16), pltpu.SemaphoreType.DMA((1 + train.shape[0] // STEP,))],
    )
    score = functools.partial(call_scores, weight, train)

    def rows_of(*pieces):
        return [(piece, ((0, piece.shape[0]),)) for piece in pieces]

    parts_of = lambda piece: (piece[:CHUNK], piece[CHUNK:])
    mine_x = to_core(mine, "mine_x")
    rest_a, rest_b = parts_of(rest)
    rest_xa = to_core(rest_a, "rest_xa")
    rest_xb = to_core(rest_b, "rest_xb")
    near = after(near, rest)
    near_a, near_b = parts_of(near)
    near_xa = to_core(near_a, "near_xa")
    near_xb = to_core(near_b, "near_xb")
    near_p = to_part(near, "near_p")
    (early0,) = score(
        rows_of(mine, mine_x, rest, rest_xa, rest_xb, near, near_xa, near_xb), stored=192
    )

    far = after(far, near, early0)
    cross = to_near(far, "cross")
    far_a, far_b = parts_of(far)
    far_pa = to_part(far_a, "far_pa")
    far_pb = to_part(far_b, "far_pb")
    far_xa = to_core(after(far_a, near_p), "far_xa")
    far_xb = to_core(after(far_b, near_p), "far_xb")
    send0, keep0 = score(rows_of(far, far_xa, far_xb), early=[(early0, 0, 64)])
    got0 = to_layer(send0, "got0")

    far_pa, far_pb, near_p = after(far_pa, send0), after(far_pb, send0), after(near_p, send0)
    near_px = to_core(near_p, "near_px")
    far_pxa = to_core(far_pa, "far_pxa")
    far_pxb = to_core(far_pb, "far_pxb")
    cross_pb = to_near(far_pb, "cross_pb")
    cross_a, cross_b = parts_of(cross)
    cross_a = after(cross_a, send0)
    cross_pa = to_part(cross_a, "cross_pa")
    cross_xa = to_core(after(cross_a, far_pa, far_pb), "cross_xa")
    cross_xb = to_core(after(cross_b, far_pa, far_pb), "cross_xb")
    early1, send1, keep1 = score(
        rows_of(near_p, near_px, far_pa, far_pb, far_pxa, far_pxb, cross, cross_xa, cross_xb),
        stored=64,
        early=[(early0, 64, 64), (early0, 128, 64)],
    )
    got1 = to_layer(send1, "got1")

    cross_pa, cross_pb = after(cross_pa, send1, got0), after(cross_pb, send1, got0)
    cross_pxa = to_core(cross_pa, "cross_pxa")
    cross_pxb = to_core(cross_pb, "cross_pxb")
    last = rows_of(cross_pa, cross_pb, cross_pxa, cross_pxb)
    n = train.shape[0]
    send2, keep2 = score(last, early=[(early1, 0, 64)], columns=(0, n // 2))
    got2 = to_layer(send2, "got2")
    send3, keep3 = score(last, early=[(early1, 0, 64)], columns=(n // 2, n))
    got3 = to_layer(send3, "got3")

    train_ids, query_ids = train_ids[None, :], query_ids[:, None]
    most = call_final(
        train_ids,
        query_ids,
        [keep0, got0, keep1, got1],
        ((0, [(0, 1, 0, 0)]), (1, [(2, 3, 0, 0)]), (2, [(2, 3, 64, 0)])),
    )
    return call_final(
        train_ids,
        query_ids,
        [keep2, got2, keep3, got3],
        ((3, [(0, 1, 0, 0), (2, 3, 0, n // 2)]),),
        most,
    )


def solution(mesh):
    placed = (
        P(("parts", "store"), "layer", None),
        P("store", "layer", None),
        P("layer", None, None),
        P("layer", None, None),
        P(),
        P("layer"),
        P(("parts", "store")),
        P("layer"),
    )
    sizes = tuple(mesh.shape[axis] for axis in AXES)
    return jax.shard_map(
        small if sizes == (PARTS, CHIPS * CORES, LAYERS) else general,
        mesh=mesh,
        in_specs=placed,
        out_specs=P("layer", ("parts", "store")),
        check_vma=False,
    )
```

```python
import functools

import jax
import jax.numpy as jnp
from jax import lax
from jax.experimental import pallas as pl
from jax.experimental.pallas import tpu as pltpu
from jax.sharding import PartitionSpec as P

AXES = ("parts", "store", "layer")
VMEM = pl.BlockSpec(memory_space=pltpu.VMEM)
SMEM = pl.BlockSpec(memory_space=pltpu.SMEM)
bf16, f32 = jnp.bfloat16, jnp.float32
LIMIT = 20 * 1024 * 1024


def preconditioned(query_grads, left_factor, right_factor):
    q_rows, slots, width = query_grads.shape
    side = left_factor.shape[1]
    mats = query_grads.astype(jnp.float32).reshape(q_rows, slots, side, side)
    half = jnp.einsum("lij,qljk->qlik", left_factor, mats, precision=lax.Precision.HIGHEST)
    full = jnp.einsum("qlik,lkm->qlim", half, right_factor, precision=lax.Precision.HIGHEST)
    return full.reshape(q_rows, slots, width).astype(jnp.bfloat16)


def general(
    train_grads,
    query_grads,
    left_factor,
    right_factor,
    layer_weight,
    layer_of,
    train_ids,
    query_ids,
):
    precond = preconditioned(query_grads, left_factor, right_factor)
    weight = jnp.take(layer_weight, layer_of[0])
    queries = lax.all_gather(precond, "store", axis=0, tiled=True)
    terms = weight * jnp.dot(
        queries[:, 0, :], train_grads[:, 0, :].T, preferred_element_type=jnp.float32
    )
    summed = lax.psum_scatter(terms, "layer", scatter_dimension=0, tiled=True)
    same = query_ids[:, None] == train_ids[None, :]
    return jnp.where(same, jnp.float32(0.0), summed)


PARTS, CHIPS, CORES, LAYERS = 2, 4, 2, 2
CHUNK = 16
HALF = 2 * CHUNK
STEP = 256
HBM = pl.BlockSpec(memory_space=pltpu.HBM)


def permute(value, name, target):
    pairs = []
    for p in range(PARTS):
        for z in range(CHIPS):
            for c in range(CORES):
                for l in range(LAYERS):
                    tp, tz, tc, tl = target(p, z, c, l)
                    source = ((p * CHIPS + z) * CORES + c) * LAYERS + l
                    pairs.append((source, ((tp * CHIPS + tz) * CORES + tc) * LAYERS + tl))
    with jax.named_scope(name):
        return lax.ppermute(value, AXES, pairs)


to_part = functools.partial(permute, target=lambda p, z, c, l: (1 - p, z, c, l))
to_core = functools.partial(permute, target=lambda p, z, c, l: (p, z, 1 - c, l))
to_layer = functools.partial(permute, target=lambda p, z, c, l: (p, z, c, 1 - l))
to_near = functools.partial(permute, target=lambda p, z, c, l: (p, z ^ 1, c, l))
to_far = functools.partial(permute, target=lambda p, z, c, l: (p, z ^ 3, c, l))


def after(value, *others):
    return lax.optimization_barrier((value, *others))[0]


def place():
    store = lax.axis_index("store")
    return lax.axis_index("parts"), store // CORES, store % CORES, lax.axis_index("layer")


def split(x, terms):
    out = []
    for _ in range(terms):
        term = x.astype(bf16)
        out.append(term)
        x = x - term.astype(f32)
    return out


def dot(a, b):
    return lax.dot_general(a, b, (((1,), (0,)), ((), ())), preferred_element_type=f32)


def iota(shape, dim):
    return lax.broadcasted_iota(jnp.int32, shape, dim)


def factors(left, right):
    r, c = iota((256, 64), 0), iota((256, 64), 1)
    pick = jnp.where(c == 4 * (r % 16) + (r // 16) % 4, 1.0, 0.0).astype(bf16)
    r, c = iota((64, 256), 0), iota((64, 256), 1)
    pick_t = jnp.where(r == 4 * (c % 16) + (c // 16) % 4, 1.0, 0.0).astype(bf16)
    block = iota((256, 256), 0) // 64 == iota((256, 256), 1) // 64
    lefts = [
        jnp.where(block, dot(dot(pick, term).astype(bf16), pick_t), 0.0).astype(bf16)
        for term in split(left, 2)
    ]
    row = jnp.concatenate([right, right], axis=1)
    tiled = jnp.concatenate([jnp.concatenate([row] * 4, axis=1)] * 4, axis=0)
    block = iota((256, 512), 0) // 64 == iota((256, 512), 1) // 128
    return lefts, split(jnp.where(block, tiled, 0.0), 2)


def precond_rows(q_ref, lefts, rights, out):
    for at in range(0, q_ref.shape[0], CHUNK):
        values = precond_chunk(q_ref[at : at + CHUNK, :], lefts, rights)
        for t, value in enumerate(values):
            out[at : at + CHUNK, t * 256 : (t + 1) * 256] = value


def precond_chunk(q, lefts, rights):
    tiles = q.shape[1] // 256
    r, c = iota((256, 256), 0), iota((256, 256), 1)
    swap = jnp.where((r // 16 == c % 16) & (r % 16 == c // 16), 1.0, 0.0).astype(bf16)
    x = jnp.concatenate([q[:, t * 256 : (t + 1) * 256] for t in range(tiles)], axis=0)
    x = dot(swap, x).astype(bf16)
    z = dot(x, rights[0]) + dot(x, rights[1])
    sets = []
    for first in range(0, 16, 4):
        rows = [
            z[query * 16 : (query + 1) * 16, s * 128 : (s + 1) * 128]
            for query in range(first, first + 4)
            for s in range(4)
        ]
        sets.append(jnp.concatenate(rows, axis=0))
    high, low = split(jnp.concatenate(sets, axis=1), 2)
    z = dot(lefts[0], high) + (dot(lefts[0], low) + dot(lefts[1], high))
    side = iota((16, 128), 1) < 64
    rows = []
    for first in range(4):
        for k in range(4):
            o = z[k * 64 : (k + 1) * 64, first * 128 : (first + 1) * 128]
            pair = [jnp.where(side, o[0:16], o[16:32]), jnp.where(side, o[32:48], o[48:64])]
            rows.append(jnp.concatenate(pair, axis=1))
    y = dot(swap, jnp.concatenate(rows, axis=0).astype(bf16)).astype(bf16)
    return [y[t * 16 : (t + 1) * 16] for t in range(tiles)]


def own_kernel(q_hbm, left_hbm, right_hbm, mine, lefts_ref, rights_ref, q_ref, left, right, sems):
    at = pl.multiple_of(lax.axis_index("parts") * HALF, HALF)
    copies = [
        pltpu.make_async_copy(source, target, sems.at[k])
        for k, (source, target) in enumerate(
            ((left_hbm, left), (right_hbm, right), (q_hbm.at[pl.ds(at, HALF), :], q_ref))
        )
    ]
    for copy in copies:
        copy.start()
    copies[0].wait()
    copies[1].wait()
    lefts, rights = factors(left[...], right[...])
    for k in range(2):
        lefts_ref[k] = lefts[k]
        rights_ref[k] = rights[k]
    copies[2].wait()
    precond_rows(q_ref, lefts, rights, mine)


def rest_kernel(weight_ref, layer_ref, q_hbm, lefts_ref, rights_ref, rest, weight, q_ref, sem):
    at = pl.multiple_of((1 - lax.axis_index("parts")) * HALF, HALF)
    q_copy = pltpu.make_async_copy(q_hbm.at[pl.ds(at, HALF), :], q_ref, sem)
    q_copy.start()
    weight[...] = jnp.full(weight.shape, weight_ref[layer_ref[0]])
    lefts, rights = [lefts_ref[0], lefts_ref[1]], [rights_ref[0], rights_ref[1]]
    q_copy.wait()
    precond_rows(q_ref, lefts, rights, rest)


def score_kernel(weight_ref, train_ref, *refs, picks, stored, early, columns, fetch):
    if fetch:
        *refs, train, sems = refs
        copies = []
        for k, at in enumerate(range(*columns, STEP)):
            here = pl.ds(at, STEP)
            copies.append(pltpu.make_async_copy(train_ref.at[here, :], train.at[here, :], sems.at[k]))
            copies[-1].start()
        train_ref = train
    inputs, refs = refs[: len(picks)], refs[len(picks) :]
    n_before = sum(taken for _, _, taken in early)
    before, outs = refs[:n_before], refs[n_before:]
    weight = weight_ref[0:1, :]
    queries = jnp.concatenate(
        [piece[at : at + n, :] for piece, rows in zip(inputs, picks) for at, n in rows], axis=0
    )
    _, z, _, layer = place()
    near_is_mine = z // 2 == layer
    for at in range(*columns, STEP):
        there, here = slice(at, at + STEP), slice(at - columns[0], at - columns[0] + STEP)
        if fetch:
            copies[at // STEP].wait()
        value = lax.dot_general(
            train_ref[there, :], queries, (((1,), (1,)), ((), ())), preferred_element_type=f32
        )
        value = weight * value.T
        if stored:
            outs[0][:, here] = value[:stored]
        if early:
            send, keep = outs[-2:]
            old, given = [], list(before)
            for first, rows, taken in early:
                old.append(
                    given.pop(0)[first : first + rows, there] if taken else value[first : first + rows]
                )
            old, new = jnp.concatenate(old, axis=0), value[stored:]
            send[:, here] = jnp.where(near_is_mine, new, old).astype(send.dtype)
            keep[:, here] = jnp.where(near_is_mine, old, new)


def kernel_call(kernel, outs, inputs, specs=None, scratch=()):
    return pl.pallas_call(
        kernel,
        out_shape=outs,
        in_specs=specs or [VMEM] * len(inputs),
        out_specs=[VMEM] * len(outs) if isinstance(outs, list) else VMEM,
        scratch_shapes=scratch,
        compiler_params=pltpu.CompilerParams(vmem_limit_bytes=LIMIT),
    )(*inputs)


def call_scores(weight, train, inputs, stored=0, early=(), columns=None, fetch=False):
    columns = columns or (0, train.shape[0])
    n = columns[1] - columns[0]
    total = sum(count for _, rows in inputs for _, count in rows)
    others = [a for a, _ in inputs] + [a for a, _, _ in early if a is not None]
    outs = [jax.ShapeDtypeStruct((stored, n), f32)] if stored else []
    if early:
        outs += [jax.ShapeDtypeStruct((total - stored, n), t) for t in (bf16, f32)]
    return kernel_call(
        functools.partial(
            score_kernel,
            picks=[rows for _, rows in inputs],
            stored=stored,
            early=[(first, rows, a is not None) for a, first, rows in early],
            columns=columns,
            fetch=fetch,
        ),
        outs + ([jax.ShapeDtypeStruct(train.shape, train.dtype)] if fetch else []),
        [weight, train, *others],
        [VMEM, HBM if fetch else VMEM] + [VMEM] * len(others),
        [pltpu.SemaphoreType.DMA((n // STEP,))] if fetch else [],
    )


def final_kernel(train_ids, query_ids, *refs, groups, n_given):
    given, refs = refs[:n_given], refs[n_given:]
    *_, out, done, sems = refs
    part, z, core, layer = place()
    low = z % 2
    first = jnp.where(z // 2 == layer, low, 1 - low)
    copies = []
    for k, (which, terms) in enumerate(groups):
        block = first if which < 2 else 1 - first
        half = part if which % 2 == 0 else 1 - part
        for i, c in enumerate((core, 1 - core)):
            at = pl.multiple_of(((block * 2 + c) * 2 + half) * HALF, HALF)
            to = slice((2 * k + i) * HALF, (2 * k + i + 1) * HALF)
            ids = query_ids[pl.ds(at, HALF), :]
            for keep, got, row, column in terms:
                keep, got = given[keep], given[got]
                columns = slice(column, column + keep.shape[1])
                total = keep[row + i * HALF : row + (i + 1) * HALF, :]
                total = total + got[row + i * HALF : row + (i + 1) * HALF, :].astype(f32)
                same = ids == train_ids[:, columns]
                done[to, columns] = jnp.where(same, jnp.float32(0.0), total)
            copies.append(
                pltpu.make_async_copy(done.at[to, :], out.at[pl.ds(at, HALF), :], sems.at[2 * k + i])
            )
            copies[-1].start()
    for copy in copies:
        copy.wait()


def call_final(train_ids, query_ids, given, groups, before=None):
    rows, n = query_ids.shape[0], train_ids.shape[1]
    inputs = [train_ids, query_ids, *given] + ([] if before is None else [before])
    return pl.pallas_call(
        functools.partial(final_kernel, groups=groups, n_given=len(given)),
        out_shape=jax.ShapeDtypeStruct((rows, n), f32),
        in_specs=[VMEM] * (2 + len(given)) + ([] if before is None else [HBM]),
        out_specs=HBM,
        scratch_shapes=[
            pltpu.VMEM((2 * len(groups) * HALF, n), f32),
            pltpu.SemaphoreType.DMA((2 * len(groups),)),
        ],
        input_output_aliases={} if before is None else {len(inputs) - 1: 0},
        compiler_params=pltpu.CompilerParams(vmem_limit_bytes=LIMIT),
    )(*inputs)


def small(
    train_grads,
    query_grads,
    left_factor,
    right_factor,
    layer_weight,
    layer_of,
    train_ids,
    query_ids,
):
    in_hbm = lambda array: pltpu.with_memory_space_constraint(array, pltpu.HBM)
    train, queries = in_hbm(train_grads[:, 0, :]), in_hbm(query_grads[:, 0, :])
    width, side = queries.shape[1], left_factor.shape[1]
    shape = jax.ShapeDtypeStruct
    mine, lefts, rights = kernel_call(
        own_kernel,
        [shape((HALF, width), bf16), shape((2, 256, 256), bf16), shape((2, 256, 512), bf16)],
        [queries, in_hbm(left_factor[0]), in_hbm(right_factor[0])],
        [HBM] * 3,
        [
            pltpu.VMEM((HALF, width), bf16),
            pltpu.VMEM((side, side), f32),
            pltpu.VMEM((side, side), f32),
            pltpu.SemaphoreType.DMA((3,)),
        ],
    )
    near = to_near(mine, "near")
    far = to_far(mine, "far")
    rest, weight = kernel_call(
        rest_kernel,
        [shape((HALF, width), bf16), shape((8, STEP), f32)],
        [in_hbm(layer_weight), layer_of, queries, lefts, rights],
        [SMEM, SMEM, HBM, VMEM, VMEM],
        [pltpu.VMEM((HALF, width), bf16), pltpu.SemaphoreType.DMA],
    )

    def rows_of(*pieces):
        return [(piece, ((0, piece.shape[0]),)) for piece in pieces]

    mine_x = to_core(mine, "mine_x")
    rest_x = to_core(rest, "rest_x")
    near_x = to_core(near, "near_x")
    near_p = to_part(near, "near_p")
    far = after(far, near)
    cross = to_near(far, "cross")
    far_p = to_part(far, "far_p")
    far_x = to_core(far, "far_x")
    rest_x = after(rest_x, far)
    early0, train = call_scores(
        weight, train, rows_of(mine, mine_x, rest, rest_x), stored=128, fetch=True
    )
    score = functools.partial(call_scores, weight, train)
    near_p = after(near_p, early0)
    near_px = to_core(near_p, "near_px")
    far_px = to_core(far_p, "far_px")
    cross_pa = to_part(cross[:CHUNK], "cross_pa")
    cross_pb = to_near(far_p[CHUNK:], "cross_pb")
    cross_x = to_core(cross, "cross_x")
    early1, send0, keep0 = score(
        rows_of(near, near_x, near_p, near_px, far, far_x, far_p, far_px),
        stored=128,
        early=[(early0, 0, 128)],
    )
    got0 = to_layer(send0, "got0")
    cross_pa, cross_pb = after(cross_pa, send0), after(cross_pb, send0)
    cross_pxa = to_core(cross_pa, "cross_pxa")
    cross_pxb = to_core(cross_pb, "cross_pxb")
    last = rows_of(cross, cross_x, cross_pa, cross_pb, cross_pxa, cross_pxb)
    n = train.shape[0]
    send1, keep1 = score(last, early=[(early1, 0, 128)], columns=(0, n // 2))
    got1 = to_layer(send1, "got1")
    early1 = after(early1, send1)
    send2, keep2 = score(last, early=[(early1, 0, 128)], columns=(n // 2, n))
    send2 = after(send2, got0)
    got2 = to_layer(send2, "got2")

    train_ids, query_ids = train_ids[None, :], query_ids[:, None]
    most = call_final(
        train_ids, query_ids, [keep0, got0], ((0, [(0, 1, 0, 0)]), (1, [(0, 1, 64, 0)]))
    )
    return call_final(
        train_ids,
        query_ids,
        [keep1, got1, keep2, got2],
        ((2, [(0, 1, 0, 0), (2, 3, 0, n // 2)]), (3, [(0, 1, 64, 0), (2, 3, 64, n // 2)])),
        most,
    )


def solution(mesh):
    placed = (
        P(("parts", "store"), "layer", None),
        P("store", "layer", None),
        P("layer", None, None),
        P("layer", None, None),
        P(),
        P("layer"),
        P(("parts", "store")),
        P("layer"),
    )
    sizes = tuple(mesh.shape[axis] for axis in AXES)
    return jax.shard_map(
        small if sizes == (PARTS, CHIPS * CORES, LAYERS) else general,
        mesh=mesh,
        in_specs=placed,
        out_specs=P("layer", ("parts", "store")),
        check_vma=False,
    )
```

```python
import functools

import jax
import jax.numpy as jnp
from jax import lax
from jax.experimental import pallas as pl
from jax.experimental.pallas import tpu as pltpu
from jax.sharding import PartitionSpec as P

AXES = ("parts", "store", "layer")
VMEM = pl.BlockSpec(memory_space=pltpu.VMEM)
SMEM = pl.BlockSpec(memory_space=pltpu.SMEM)
bf16, f32 = jnp.bfloat16, jnp.float32
LIMIT = 20 * 1024 * 1024


def preconditioned(query_grads, left_factor, right_factor):
    q_rows, slots, width = query_grads.shape
    side = left_factor.shape[1]
    mats = query_grads.astype(jnp.float32).reshape(q_rows, slots, side, side)
    half = jnp.einsum("lij,qljk->qlik", left_factor, mats, precision=lax.Precision.HIGHEST)
    full = jnp.einsum("qlik,lkm->qlim", half, right_factor, precision=lax.Precision.HIGHEST)
    return full.reshape(q_rows, slots, width).astype(jnp.bfloat16)


def general(
    train_grads,
    query_grads,
    left_factor,
    right_factor,
    layer_weight,
    layer_of,
    train_ids,
    query_ids,
):
    precond = preconditioned(query_grads, left_factor, right_factor)
    weight = jnp.take(layer_weight, layer_of[0])
    queries = lax.all_gather(precond, "store", axis=0, tiled=True)
    terms = weight * jnp.dot(
        queries[:, 0, :], train_grads[:, 0, :].T, preferred_element_type=jnp.float32
    )
    summed = lax.psum_scatter(terms, "layer", scatter_dimension=0, tiled=True)
    same = query_ids[:, None] == train_ids[None, :]
    return jnp.where(same, jnp.float32(0.0), summed)


PARTS, CHIPS, CORES, LAYERS = 2, 4, 2, 2
CHUNK = 16
HALF = 2 * CHUNK
STEP = 256
HBM = pl.BlockSpec(memory_space=pltpu.HBM)


def permute(value, name, target):
    pairs = []
    for p in range(PARTS):
        for z in range(CHIPS):
            for c in range(CORES):
                for l in range(LAYERS):
                    tp, tz, tc, tl = target(p, z, c, l)
                    source = ((p * CHIPS + z) * CORES + c) * LAYERS + l
                    pairs.append((source, ((tp * CHIPS + tz) * CORES + tc) * LAYERS + tl))
    with jax.named_scope(name):
        return lax.ppermute(value, AXES, pairs)


to_part = functools.partial(permute, target=lambda p, z, c, l: (1 - p, z, c, l))
to_core = functools.partial(permute, target=lambda p, z, c, l: (p, z, 1 - c, l))
to_layer = functools.partial(permute, target=lambda p, z, c, l: (p, z, c, 1 - l))
to_near = functools.partial(permute, target=lambda p, z, c, l: (p, z ^ 1, c, l))
to_far = functools.partial(permute, target=lambda p, z, c, l: (p, z ^ 3, c, l))


def after(value, *others):
    return lax.optimization_barrier((value, *others))[0]


def place():
    store = lax.axis_index("store")
    return lax.axis_index("parts"), store // CORES, store % CORES, lax.axis_index("layer")


def split(x, terms):
    out = []
    for _ in range(terms):
        term = x.astype(bf16)
        out.append(term)
        x = x - term.astype(f32)
    return out


def dot(a, b):
    return lax.dot_general(a, b, (((1,), (0,)), ((), ())), preferred_element_type=f32)


def iota(shape, dim):
    return lax.broadcasted_iota(jnp.int32, shape, dim)


def factors(left, right):
    r, c = iota((256, 64), 0), iota((256, 64), 1)
    pick = jnp.where(c == 4 * (r % 16) + (r // 16) % 4, 1.0, 0.0).astype(bf16)
    r, c = iota((64, 256), 0), iota((64, 256), 1)
    pick_t = jnp.where(r == 4 * (c % 16) + (c // 16) % 4, 1.0, 0.0).astype(bf16)
    block = iota((256, 256), 0) // 64 == iota((256, 256), 1) // 64
    lefts = [
        jnp.where(block, dot(dot(pick, term).astype(bf16), pick_t), 0.0).astype(bf16)
        for term in split(left, 2)
    ]
    row = jnp.concatenate([right, right], axis=1)
    tiled = jnp.concatenate([jnp.concatenate([row] * 4, axis=1)] * 4, axis=0)
    block = iota((256, 512), 0) // 64 == iota((256, 512), 1) // 128
    return lefts, split(jnp.where(block, tiled, 0.0), 2)


def precond_rows(q_ref, lefts, rights, out):
    for at in range(0, q_ref.shape[0], CHUNK):
        values = precond_chunk(q_ref[at : at + CHUNK, :], lefts, rights)
        for t, value in enumerate(values):
            out[at : at + CHUNK, t * 256 : (t + 1) * 256] = value


def precond_chunk(q, lefts, rights):
    tiles = q.shape[1] // 256
    r, c = iota((256, 256), 0), iota((256, 256), 1)
    swap = jnp.where((r // 16 == c % 16) & (r % 16 == c // 16), 1.0, 0.0).astype(bf16)
    x = jnp.concatenate([q[:, t * 256 : (t + 1) * 256] for t in range(tiles)], axis=0)
    x = dot(swap, x).astype(bf16)
    z = dot(x, rights[0]) + dot(x, rights[1])
    sets = []
    for first in range(0, 16, 4):
        rows = [
            z[query * 16 : (query + 1) * 16, s * 128 : (s + 1) * 128]
            for query in range(first, first + 4)
            for s in range(4)
        ]
        sets.append(jnp.concatenate(rows, axis=0))
    high, low = split(jnp.concatenate(sets, axis=1), 2)
    z = dot(lefts[0], high) + (dot(lefts[0], low) + dot(lefts[1], high))
    side = iota((16, 128), 1) < 64
    rows = []
    for first in range(4):
        for k in range(4):
            o = z[k * 64 : (k + 1) * 64, first * 128 : (first + 1) * 128]
            pair = [jnp.where(side, o[0:16], o[16:32]), jnp.where(side, o[32:48], o[48:64])]
            rows.append(jnp.concatenate(pair, axis=1))
    y = dot(swap, jnp.concatenate(rows, axis=0).astype(bf16)).astype(bf16)
    return [y[t * 16 : (t + 1) * 16] for t in range(tiles)]


def own_kernel(q_hbm, left_hbm, right_hbm, mine, lefts_ref, rights_ref, q_ref, left, right, sems):
    at = pl.multiple_of(lax.axis_index("parts") * HALF, HALF)
    copies = [
        pltpu.make_async_copy(source, target, sems.at[k])
        for k, (source, target) in enumerate(
            ((left_hbm, left), (right_hbm, right), (q_hbm.at[pl.ds(at, HALF), :], q_ref))
        )
    ]
    for copy in copies:
        copy.start()
    copies[0].wait()
    copies[1].wait()
    lefts, rights = factors(left[...], right[...])
    for k in range(2):
        lefts_ref[k] = lefts[k]
        rights_ref[k] = rights[k]
    copies[2].wait()
    precond_rows(q_ref, lefts, rights, mine)


def rest_kernel(weight_ref, layer_ref, q_hbm, lefts_ref, rights_ref, rest, weight, q_ref, sem):
    at = pl.multiple_of((1 - lax.axis_index("parts")) * HALF, HALF)
    q_copy = pltpu.make_async_copy(q_hbm.at[pl.ds(at, HALF), :], q_ref, sem)
    q_copy.start()
    weight[...] = jnp.full(weight.shape, weight_ref[layer_ref[0]])
    lefts, rights = [lefts_ref[0], lefts_ref[1]], [rights_ref[0], rights_ref[1]]
    q_copy.wait()
    precond_rows(q_ref, lefts, rights, rest)


def train_kernel(train_hbm, _, train, sems):
    copies = []
    for k in range(train.shape[0] // STEP):
        here = pl.ds(k * STEP, STEP)
        copies.append(pltpu.make_async_copy(train_hbm.at[here, :], train.at[here, :], sems.at[k]))
        copies[-1].start()
    for copy in copies:
        copy.wait()


def score_kernel(weight_ref, train_ref, *refs, picks, stored, early, columns):
    inputs, refs = refs[: len(picks)], refs[len(picks) :]
    n_before = sum(taken for _, _, taken in early)
    before, outs = refs[:n_before], refs[n_before:]
    weight = weight_ref[0:1, :]
    queries = jnp.concatenate(
        [piece[at : at + n, :] for piece, rows in zip(inputs, picks) for at, n in rows], axis=0
    )
    _, z, _, layer = place()
    near_is_mine = z // 2 == layer
    for at in range(*columns, STEP):
        there, here = slice(at, at + STEP), slice(at - columns[0], at - columns[0] + STEP)
        value = lax.dot_general(
            train_ref[there, :], queries, (((1,), (1,)), ((), ())), preferred_element_type=f32
        )
        value = weight * value.T
        if stored:
            outs[0][:, here] = value[:stored]
        if early:
            send, keep = outs[-2:]
            old, given = [], list(before)
            for first, rows, taken in early:
                old.append(
                    given.pop(0)[first : first + rows, there] if taken else value[first : first + rows]
                )
            old, new = jnp.concatenate(old, axis=0), value[stored:]
            send[:, here] = jnp.where(near_is_mine, new, old).astype(send.dtype)
            keep[:, here] = jnp.where(near_is_mine, old, new)


def kernel_call(kernel, outs, inputs, specs=None, scratch=()):
    return pl.pallas_call(
        kernel,
        out_shape=outs,
        in_specs=specs or [VMEM] * len(inputs),
        out_specs=[VMEM] * len(outs) if isinstance(outs, list) else VMEM,
        scratch_shapes=scratch,
        compiler_params=pltpu.CompilerParams(vmem_limit_bytes=LIMIT),
    )(*inputs)


def call_scores(weight, train, inputs, stored=0, early=(), columns=None):
    columns = columns or (0, train.shape[0])
    n = columns[1] - columns[0]
    total = sum(count for _, rows in inputs for _, count in rows)
    others = [a for a, _ in inputs] + [a for a, _, _ in early if a is not None]
    outs = [jax.ShapeDtypeStruct((stored, n), f32)] if stored else []
    if early:
        outs += [jax.ShapeDtypeStruct((total - stored, n), t) for t in (bf16, f32)]
    return kernel_call(
        functools.partial(
            score_kernel,
            picks=[rows for _, rows in inputs],
            stored=stored,
            early=[(first, rows, a is not None) for a, first, rows in early],
            columns=columns,
        ),
        outs,
        [weight, train, *others],
    )


def final_kernel(train_ids, query_ids, *refs, groups, n_given):
    given, refs = refs[:n_given], refs[n_given:]
    *_, out, done, sems = refs
    part, z, core, layer = place()
    low = z % 2
    first = jnp.where(z // 2 == layer, low, 1 - low)
    copies = []
    for k, (which, terms) in enumerate(groups):
        block = first if which < 2 else 1 - first
        half = part if which % 2 == 0 else 1 - part
        for i, c in enumerate((core, 1 - core)):
            at = pl.multiple_of(((block * 2 + c) * 2 + half) * HALF, HALF)
            to = slice((2 * k + i) * HALF, (2 * k + i + 1) * HALF)
            ids = query_ids[pl.ds(at, HALF), :]
            for keep, got, row, column in terms:
                keep, got = given[keep], given[got]
                columns = slice(column, column + keep.shape[1])
                total = keep[row + i * HALF : row + (i + 1) * HALF, :]
                total = total + got[row + i * HALF : row + (i + 1) * HALF, :].astype(f32)
                same = ids == train_ids[:, columns]
                done[to, columns] = jnp.where(same, jnp.float32(0.0), total)
            copies.append(
                pltpu.make_async_copy(done.at[to, :], out.at[pl.ds(at, HALF), :], sems.at[2 * k + i])
            )
            copies[-1].start()
    for copy in copies:
        copy.wait()


def call_final(train_ids, query_ids, given, groups, before=None):
    rows, n = query_ids.shape[0], train_ids.shape[1]
    inputs = [train_ids, query_ids, *given] + ([] if before is None else [before])
    return pl.pallas_call(
        functools.partial(final_kernel, groups=groups, n_given=len(given)),
        out_shape=jax.ShapeDtypeStruct((rows, n), f32),
        in_specs=[VMEM] * (2 + len(given)) + ([] if before is None else [HBM]),
        out_specs=HBM,
        scratch_shapes=[
            pltpu.VMEM((2 * len(groups) * HALF, n), f32),
            pltpu.SemaphoreType.DMA((2 * len(groups),)),
        ],
        input_output_aliases={} if before is None else {len(inputs) - 1: 0},
        compiler_params=pltpu.CompilerParams(vmem_limit_bytes=LIMIT),
    )(*inputs)


def small(
    train_grads,
    query_grads,
    left_factor,
    right_factor,
    layer_weight,
    layer_of,
    train_ids,
    query_ids,
):
    in_hbm = lambda array: pltpu.with_memory_space_constraint(array, pltpu.HBM)
    train, queries = in_hbm(train_grads[:, 0, :]), in_hbm(query_grads[:, 0, :])
    width, side = queries.shape[1], left_factor.shape[1]
    shape = jax.ShapeDtypeStruct
    mine, lefts, rights = kernel_call(
        own_kernel,
        [shape((HALF, width), bf16), shape((2, 256, 256), bf16), shape((2, 256, 512), bf16)],
        [queries, in_hbm(left_factor[0]), in_hbm(right_factor[0])],
        [HBM] * 3,
        [
            pltpu.VMEM((HALF, width), bf16),
            pltpu.VMEM((side, side), f32),
            pltpu.VMEM((side, side), f32),
            pltpu.SemaphoreType.DMA((3,)),
        ],
    )
    near = to_near(mine, "near")
    rest, weight = kernel_call(
        rest_kernel,
        [shape((HALF, width), bf16), shape((8, STEP), f32)],
        [in_hbm(layer_weight), layer_of, queries, lefts, rights],
        [SMEM, SMEM, HBM, VMEM, VMEM],
        [pltpu.VMEM((HALF, width), bf16), pltpu.SemaphoreType.DMA],
    )
    far = to_far(after(mine, rest), "far")
    (train,) = kernel_call(
        train_kernel,
        [shape(train.shape, bf16)],
        [train, weight],
        [HBM, VMEM],
        [pltpu.SemaphoreType.DMA((train.shape[0] // STEP,))],
    )
    score = functools.partial(call_scores, weight, train)

    def rows_of(*pieces):
        return [(piece, ((0, piece.shape[0]),)) for piece in pieces]

    mine_x = to_core(mine, "mine_x")
    rest_x = to_core(rest, "rest_x")
    near = after(near, train)
    near_x = to_core(near, "near_x")
    near_p = to_part(near, "near_p")
    far = after(far, near)
    cross = to_near(far, "cross")
    far_p = to_part(far, "far_p")
    far_xa = to_core(after(far[:CHUNK], near_p), "far_xa")
    far_xb = to_core(after(far[CHUNK:], near_p), "far_xb")
    early0, send0, keep0 = score(
        rows_of(mine, mine_x, rest, rest_x, far, far_xa, far_xb), stored=128, early=[(None, 0, 64)]
    )
    got0 = to_layer(send0, "got0")
    near_p, far_p, cross = after(near_p, send0), after(far_p, send0), after(cross, send0)
    near_px = to_core(near_p, "near_px")
    far_px = to_core(far_p, "far_px")
    cross_pa = to_part(cross[:CHUNK], "cross_pa")
    cross_pb = to_near(far_p[CHUNK:], "cross_pb")
    cross_x = to_core(cross, "cross_x")
    early1, send1, keep1 = score(
        rows_of(near, near_x, near_p, near_px, far_p, far_px, cross, cross_x),
        stored=128,
        early=[(early0, 64, 64), (None, 0, 64)],
    )
    got1 = to_layer(send1, "got1")
    cross_pa, cross_pb = after(cross_pa, send1, got0), after(cross_pb, send1, got0)
    cross_pxa = to_core(cross_pa, "cross_pxa")
    cross_pxb = to_core(cross_pb, "cross_pxb")
    last = rows_of(cross_pa, cross_pb, cross_pxa, cross_pxb)
    n = train.shape[0]
    send2, keep2 = score(last, early=[(early1, 64, 64)], columns=(0, n // 2))
    got2 = to_layer(send2, "got2")
    early1 = after(early1, send2)
    send3, keep3 = score(last, early=[(early1, 64, 64)], columns=(n // 2, n))
    got3 = to_layer(send3, "got3")

    train_ids, query_ids = train_ids[None, :], query_ids[:, None]
    most = call_final(
        train_ids,
        query_ids,
        [keep0, got0, keep1, got1],
        ((0, [(0, 1, 0, 0)]), (1, [(2, 3, 0, 0)]), (2, [(2, 3, 64, 0)])),
    )
    return call_final(
        train_ids,
        query_ids,
        [keep2, got2, keep3, got3],
        ((3, [(0, 1, 0, 0), (2, 3, 0, n // 2)]),),
        most,
    )


def solution(mesh):
    placed = (
        P(("parts", "store"), "layer", None),
        P("store", "layer", None),
        P("layer", None, None),
        P("layer", None, None),
        P(),
        P("layer"),
        P(("parts", "store")),
        P("layer"),
    )
    sizes = tuple(mesh.shape[axis] for axis in AXES)
    return jax.shard_map(
        small if sizes == (PARTS, CHIPS * CORES, LAYERS) else general,
        mesh=mesh,
        in_specs=placed,
        out_specs=P("layer", ("parts", "store")),
        check_vma=False,
    )
```

```python
import functools

import jax
import jax.numpy as jnp
from jax import lax
from jax.experimental import pallas as pl
from jax.experimental.pallas import tpu as pltpu
from jax.sharding import PartitionSpec as P

AXES = ("parts", "store", "layer")
VMEM = pl.BlockSpec(memory_space=pltpu.VMEM)
SMEM = pl.BlockSpec(memory_space=pltpu.SMEM)
bf16, f32 = jnp.bfloat16, jnp.float32
LIMIT = 20 * 1024 * 1024


def preconditioned(query_grads, left_factor, right_factor):
    q_rows, slots, width = query_grads.shape
    side = left_factor.shape[1]
    mats = query_grads.astype(jnp.float32).reshape(q_rows, slots, side, side)
    half = jnp.einsum("lij,qljk->qlik", left_factor, mats, precision=lax.Precision.HIGHEST)
    full = jnp.einsum("qlik,lkm->qlim", half, right_factor, precision=lax.Precision.HIGHEST)
    return full.reshape(q_rows, slots, width).astype(jnp.bfloat16)


def general(
    train_grads,
    query_grads,
    left_factor,
    right_factor,
    layer_weight,
    layer_of,
    train_ids,
    query_ids,
):
    precond = preconditioned(query_grads, left_factor, right_factor)
    weight = jnp.take(layer_weight, layer_of[0])
    queries = lax.all_gather(precond, "store", axis=0, tiled=True)
    terms = weight * jnp.dot(
        queries[:, 0, :], train_grads[:, 0, :].T, preferred_element_type=jnp.float32
    )
    summed = lax.psum_scatter(terms, "layer", scatter_dimension=0, tiled=True)
    same = query_ids[:, None] == train_ids[None, :]
    return jnp.where(same, jnp.float32(0.0), summed)


PARTS, CHIPS, CORES, LAYERS = 2, 4, 2, 2
CHUNK = 16
HALF = 2 * CHUNK
STEP = 256
HBM = pl.BlockSpec(memory_space=pltpu.HBM)


def permute(value, name, target):
    pairs = []
    for p in range(PARTS):
        for z in range(CHIPS):
            for c in range(CORES):
                for l in range(LAYERS):
                    tp, tz, tc, tl = target(p, z, c, l)
                    source = ((p * CHIPS + z) * CORES + c) * LAYERS + l
                    pairs.append((source, ((tp * CHIPS + tz) * CORES + tc) * LAYERS + tl))
    with jax.named_scope(name):
        return lax.ppermute(value, AXES, pairs)


to_part = functools.partial(permute, target=lambda p, z, c, l: (1 - p, z, c, l))
to_core = functools.partial(permute, target=lambda p, z, c, l: (p, z, 1 - c, l))
to_layer = functools.partial(permute, target=lambda p, z, c, l: (p, z, c, 1 - l))
to_previous = functools.partial(permute, target=lambda p, z, c, l: (p, (z - 1) % CHIPS, c, l))
to_next = functools.partial(permute, target=lambda p, z, c, l: (p, (z + 1) % CHIPS, c, l))


def after(value, *others):
    return lax.optimization_barrier((value, *others))[0]


def place():
    store = lax.axis_index("store")
    return lax.axis_index("parts"), store // CORES, store % CORES, lax.axis_index("layer")


def split(x, terms):
    out = []
    for _ in range(terms):
        term = x.astype(bf16)
        out.append(term)
        x = x - term.astype(f32)
    return out


def dot(a, b):
    return lax.dot_general(a, b, (((1,), (0,)), ((), ())), preferred_element_type=f32)


def iota(shape, dim):
    return lax.broadcasted_iota(jnp.int32, shape, dim)


def factors(left, right):
    r, c = iota((256, 64), 0), iota((256, 64), 1)
    pick = jnp.where(c == 4 * (r % 16) + (r // 16) % 4, 1.0, 0.0).astype(bf16)
    r, c = iota((64, 256), 0), iota((64, 256), 1)
    pick_t = jnp.where(r == 4 * (c % 16) + (c // 16) % 4, 1.0, 0.0).astype(bf16)
    block = iota((256, 256), 0) // 64 == iota((256, 256), 1) // 64
    lefts = [
        jnp.where(block, dot(dot(pick, term).astype(bf16), pick_t), 0.0).astype(bf16)
        for term in split(left, 2)
    ]
    row = jnp.concatenate([right, right], axis=1)
    tiled = jnp.concatenate([jnp.concatenate([row] * 4, axis=1)] * 4, axis=0)
    block = iota((256, 512), 0) // 64 == iota((256, 512), 1) // 128
    return lefts, split(jnp.where(block, tiled, 0.0), 2)


def precond_rows(q_ref, lefts, rights, out):
    for at in range(0, q_ref.shape[0], CHUNK):
        values = precond_chunk(q_ref[at : at + CHUNK, :], lefts, rights)
        for t, value in enumerate(values):
            out[at : at + CHUNK, t * 256 : (t + 1) * 256] = value


def precond_chunk(q, lefts, rights):
    tiles = q.shape[1] // 256
    r, c = iota((256, 256), 0), iota((256, 256), 1)
    swap = jnp.where((r // 16 == c % 16) & (r % 16 == c // 16), 1.0, 0.0).astype(bf16)
    x = jnp.concatenate([q[:, t * 256 : (t + 1) * 256] for t in range(tiles)], axis=0)
    x = dot(swap, x).astype(bf16)
    z = dot(x, rights[0]) + dot(x, rights[1])
    sets = []
    for first in range(0, 16, 4):
        rows = [
            z[query * 16 : (query + 1) * 16, s * 128 : (s + 1) * 128]
            for query in range(first, first + 4)
            for s in range(4)
        ]
        sets.append(jnp.concatenate(rows, axis=0))
    high, low = split(jnp.concatenate(sets, axis=1), 2)
    z = dot(lefts[0], high) + (dot(lefts[0], low) + dot(lefts[1], high))
    side = iota((16, 128), 1) < 64
    rows = []
    for first in range(4):
        for k in range(4):
            o = z[k * 64 : (k + 1) * 64, first * 128 : (first + 1) * 128]
            pair = [jnp.where(side, o[0:16], o[16:32]), jnp.where(side, o[32:48], o[48:64])]
            rows.append(jnp.concatenate(pair, axis=1))
    y = dot(swap, jnp.concatenate(rows, axis=0).astype(bf16)).astype(bf16)
    return [y[t * 16 : (t + 1) * 16] for t in range(tiles)]


def own_kernel(q_hbm, left_hbm, right_hbm, mine, lefts_ref, rights_ref, q_ref, left, right, sems):
    at = pl.multiple_of(lax.axis_index("parts") * HALF, HALF)
    copies = [
        pltpu.make_async_copy(source, target, sems.at[k])
        for k, (source, target) in enumerate(
            ((left_hbm, left), (right_hbm, right), (q_hbm.at[pl.ds(at, HALF), :], q_ref))
        )
    ]
    for copy in copies:
        copy.start()
    copies[0].wait()
    copies[1].wait()
    lefts, rights = factors(left[...], right[...])
    for k in range(2):
        lefts_ref[k] = lefts[k]
        rights_ref[k] = rights[k]
    copies[2].wait()
    precond_rows(q_ref, lefts, rights, mine)


def rest_kernel(weight_ref, layer_ref, q_hbm, lefts_ref, rights_ref, rest, weight, q_ref, sem):
    at = pl.multiple_of((1 - lax.axis_index("parts")) * HALF, HALF)
    q_copy = pltpu.make_async_copy(q_hbm.at[pl.ds(at, HALF), :], q_ref, sem)
    q_copy.start()
    weight[...] = jnp.full(weight.shape, weight_ref[layer_ref[0]])
    lefts, rights = [lefts_ref[0], lefts_ref[1]], [rights_ref[0], rights_ref[1]]
    q_copy.wait()
    precond_rows(q_ref, lefts, rights, rest)


def train_kernel(train_hbm, _, train, sems):
    copies = []
    for k in range(train.shape[0] // STEP):
        here = pl.ds(k * STEP, STEP)
        copies.append(pltpu.make_async_copy(train_hbm.at[here, :], train.at[here, :], sems.at[k]))
        copies[-1].start()
    for copy in copies:
        copy.wait()


def scored(weight_ref, train_ref, pieces, columns, write):
    weight = weight_ref[0:1, :]
    queries = jnp.concatenate([piece[...] for piece in pieces], axis=0)
    for at in range(*columns, STEP):
        value = lax.dot_general(
            train_ref[at : at + STEP, :],
            queries,
            (((1,), (1,)), ((), ())),
            preferred_element_type=f32,
        )
        write(slice(at - columns[0], at - columns[0] + STEP), weight * value.T)


def swap(theirs, ours, send, keep, here):
    _, z, _, layer = place()
    mine = z // 2 == layer
    send[:, here] = jnp.where(mine, theirs, ours).astype(send.dtype)
    keep[:, here] = jnp.where(mine, ours, theirs)


def beside_across(a, b):
    even = place()[1] % 2 == 0
    return jnp.where(even, a, b), jnp.where(even, b, a)


def first_kernel(weight_ref, train_ref, *refs, columns):
    *pieces, own_p, beside, send, keep = refs

    def write(here, value):
        own_p[:, here] = value[64:128]
        beside[:, here], across = beside_across(value[128:192], value[192:])
        swap(across, value[:64], send, keep, here)

    scored(weight_ref, train_ref, pieces, columns, write)


def second_kernel(weight_ref, train_ref, own_p, *refs, columns):
    *pieces, beside_p, send, keep = refs

    def write(here, value):
        beside_p[:, here], across = beside_across(value[:64], value[64:])
        swap(across, own_p[:, here], send, keep, here)

    scored(weight_ref, train_ref, pieces, columns, write)


def third_kernel(weight_ref, train_ref, beside, beside_p, *refs, columns):
    *pieces, send, keep = refs

    def write(here, value):
        there = slice(here.start + columns[0], here.stop + columns[0])
        ours = jnp.concatenate([beside[:, there], beside_p[:, there]], axis=0)
        swap(value, ours, send, keep, here)

    scored(weight_ref, train_ref, pieces, columns, write)


def call_scores(kernel, weight, train, inputs, outs, columns=None):
    columns = columns or (0, train.shape[0])
    return kernel_call(
        functools.partial(kernel, columns=columns),
        [jax.ShapeDtypeStruct((rows, columns[1] - columns[0]), t) for rows, t in outs],
        [weight, train, *inputs],
    )


def kernel_call(kernel, outs, inputs, specs=None, scratch=()):
    return pl.pallas_call(
        kernel,
        out_shape=outs,
        in_specs=specs or [VMEM] * len(inputs),
        out_specs=[VMEM] * len(outs),
        scratch_shapes=scratch,
        compiler_params=pltpu.CompilerParams(vmem_limit_bytes=LIMIT),
    )(*inputs)


def final_kernel(train_ids, query_ids, *refs, groups, n_given):
    given, refs = refs[:n_given], refs[n_given:]
    *_, out, done, sems = refs
    part, z, core, layer = place()
    low = z % 2
    first = jnp.where(z // 2 == layer, low, 1 - low)
    copies = []
    for k, (which, terms) in enumerate(groups):
        block = first if which < 2 else 1 - first
        half = part if which % 2 == 0 else 1 - part
        for i, c in enumerate((core, 1 - core)):
            at = pl.multiple_of(((block * 2 + c) * 2 + half) * HALF, HALF)
            to = slice((2 * k + i) * HALF, (2 * k + i + 1) * HALF)
            ids = query_ids[pl.ds(at, HALF), :]
            for keep, got, row, column in terms:
                keep, got = given[keep], given[got]
                columns = slice(column, column + keep.shape[1])
                total = keep[row + i * HALF : row + (i + 1) * HALF, :]
                total = total + got[row + i * HALF : row + (i + 1) * HALF, :].astype(f32)
                same = ids == train_ids[:, columns]
                done[to, columns] = jnp.where(same, jnp.float32(0.0), total)
            copies.append(
                pltpu.make_async_copy(done.at[to, :], out.at[pl.ds(at, HALF), :], sems.at[2 * k + i])
            )
            copies[-1].start()
    for copy in copies:
        copy.wait()


def call_final(train_ids, query_ids, given, groups, before=None):
    rows, n = query_ids.shape[0], train_ids.shape[1]
    inputs = [train_ids, query_ids, *given] + ([] if before is None else [before])
    return pl.pallas_call(
        functools.partial(final_kernel, groups=groups, n_given=len(given)),
        out_shape=jax.ShapeDtypeStruct((rows, n), f32),
        in_specs=[VMEM] * (2 + len(given)) + ([] if before is None else [HBM]),
        out_specs=HBM,
        scratch_shapes=[
            pltpu.VMEM((2 * len(groups) * HALF, n), f32),
            pltpu.SemaphoreType.DMA((2 * len(groups),)),
        ],
        input_output_aliases={} if before is None else {len(inputs) - 1: 0},
        compiler_params=pltpu.CompilerParams(vmem_limit_bytes=LIMIT),
    )(*inputs)


def small(
    train_grads,
    query_grads,
    left_factor,
    right_factor,
    layer_weight,
    layer_of,
    train_ids,
    query_ids,
):
    in_hbm = lambda array: pltpu.with_memory_space_constraint(array, pltpu.HBM)
    train, queries = in_hbm(train_grads[:, 0, :]), in_hbm(query_grads[:, 0, :])
    width, side = queries.shape[1], left_factor.shape[1]
    shape = jax.ShapeDtypeStruct
    mine, lefts, rights = kernel_call(
        own_kernel,
        [shape((HALF, width), bf16), shape((2, 256, 256), bf16), shape((2, 256, 512), bf16)],
        [queries, in_hbm(left_factor[0]), in_hbm(right_factor[0])],
        [HBM] * 3,
        [
            pltpu.VMEM((HALF, width), bf16),
            pltpu.VMEM((side, side), f32),
            pltpu.VMEM((side, side), f32),
            pltpu.SemaphoreType.DMA((3,)),
        ],
    )
    a = to_previous(mine, "a")
    rest, weight = kernel_call(
        rest_kernel,
        [shape((HALF, width), bf16), shape((8, STEP), f32)],
        [in_hbm(layer_weight), layer_of, queries, lefts, rights],
        [SMEM, SMEM, HBM, VMEM, VMEM],
        [pltpu.VMEM((HALF, width), bf16), pltpu.SemaphoreType.DMA],
    )
    b = to_next(after(mine, rest), "b")
    mine_x = to_core(mine, "mine_x")
    rest_x = to_core(rest, "rest_x")
    (train,) = kernel_call(
        train_kernel,
        [shape(train.shape, bf16)],
        [train, after(weight, a, mine_x, rest_x)],
        [HBM, VMEM],
        [pltpu.SemaphoreType.DMA((train.shape[0] // STEP,))],
    )
    score = lambda kernel, *rest: call_scores(kernel, weight, train, *rest)

    a_x = to_core(a, "a_x")
    a_p = to_part(a, "a_p")
    b = after(b, a, train, a_x)
    b_p = to_part(b, "b_p")
    c0 = to_next(b[:CHUNK], "c0")
    c1 = to_previous(a[CHUNK:], "c1")
    b_x = to_core(after(b, a_p), "b_x")
    own_p, beside, send0, keep0 = score(
        first_kernel,
        [mine, mine_x, rest, rest_x, a, a_x, b, b_x],
        [(64, f32), (64, f32), (64, bf16), (64, f32)],
    )
    got0 = to_layer(send0, "got0")

    a_p, b_p, c0, c1 = [after(piece, send0) for piece in (a_p, b_p, c0, c1)]
    c_p0 = to_part(c0, "c_p0")
    c_p1 = to_previous(a_p[CHUNK:], "c_p1")
    a_px0, a_px1 = to_core(a_p[:CHUNK], "a_px0"), to_core(a_p[CHUNK:], "a_px1")
    b_px0, b_px1 = to_core(b_p[:CHUNK], "b_px0"), to_core(b_p[CHUNK:], "b_px1")
    c_x0, c_x1 = to_core(c0, "c_x0"), to_core(c1, "c_x1")
    beside_p, send1, keep1 = score(
        second_kernel, [own_p, a_p, a_px0, a_px1, b_p, b_px0, b_px1], [(64, f32), (64, bf16), (64, f32)]
    )
    got1 = to_layer(send1, "got1")

    c_p0, c_p1 = after(c_p0, send1, got0), after(c_p1, send1, got0)
    c_px0, c_px1 = to_core(c_p0, "c_px0"), to_core(c_p1, "c_px1")
    last = [c0, c1, c_x0, c_x1, c_p0, c_p1, c_px0, c_px1]
    n, outs = train.shape[0], [(128, bf16), (128, f32)]
    send2, keep2 = score(third_kernel, [beside, beside_p, *last], outs, (0, n // 2))
    got2 = to_layer(send2, "got2")
    beside = after(beside, send2)
    send3, keep3 = score(third_kernel, [beside, beside_p, *last], outs, (n // 2, n))
    got3 = to_layer(send3, "got3")

    train_ids, query_ids = train_ids[None, :], query_ids[:, None]
    most = call_final(
        train_ids, query_ids, [keep0, got0, keep1, got1], ((0, [(0, 1, 0, 0)]), (1, [(2, 3, 0, 0)]))
    )
    return call_final(
        train_ids,
        query_ids,
        [keep2, got2, keep3, got3],
        ((2, [(0, 1, 0, 0), (2, 3, 0, n // 2)]), (3, [(0, 1, 64, 0), (2, 3, 64, n // 2)])),
        most,
    )


def solution(mesh):
    placed = (
        P(("parts", "store"), "layer", None),
        P("store", "layer", None),
        P("layer", None, None),
        P("layer", None, None),
        P(),
        P("layer"),
        P(("parts", "store")),
        P("layer"),
    )
    sizes = tuple(mesh.shape[axis] for axis in AXES)
    return jax.shard_map(
        small if sizes == (PARTS, CHIPS * CORES, LAYERS) else general,
        mesh=mesh,
        in_specs=placed,
        out_specs=P("layer", ("parts", "store")),
        check_vma=False,
    )
```

```python
import functools

import jax
import jax.numpy as jnp
from jax import lax
from jax.experimental import pallas as pl
from jax.experimental.pallas import tpu as pltpu
from jax.sharding import PartitionSpec as P

AXES = ("parts", "store", "layer")
VMEM = pl.BlockSpec(memory_space=pltpu.VMEM)
SMEM = pl.BlockSpec(memory_space=pltpu.SMEM)
bf16, f32 = jnp.bfloat16, jnp.float32
LIMIT = 20 * 1024 * 1024


def preconditioned(query_grads, left_factor, right_factor):
    q_rows, slots, width = query_grads.shape
    side = left_factor.shape[1]
    mats = query_grads.astype(jnp.float32).reshape(q_rows, slots, side, side)
    half = jnp.einsum("lij,qljk->qlik", left_factor, mats, precision=lax.Precision.HIGHEST)
    full = jnp.einsum("qlik,lkm->qlim", half, right_factor, precision=lax.Precision.HIGHEST)
    return full.reshape(q_rows, slots, width).astype(jnp.bfloat16)


def general(
    train_grads,
    query_grads,
    left_factor,
    right_factor,
    layer_weight,
    layer_of,
    train_ids,
    query_ids,
):
    precond = preconditioned(query_grads, left_factor, right_factor)
    weight = jnp.take(layer_weight, layer_of[0])
    queries = lax.all_gather(precond, "store", axis=0, tiled=True)
    terms = weight * jnp.dot(
        queries[:, 0, :], train_grads[:, 0, :].T, preferred_element_type=jnp.float32
    )
    summed = lax.psum_scatter(terms, "layer", scatter_dimension=0, tiled=True)
    same = query_ids[:, None] == train_ids[None, :]
    return jnp.where(same, jnp.float32(0.0), summed)


PARTS, CHIPS, CORES, LAYERS = 2, 4, 2, 2
CHUNK = 16
HALF = 2 * CHUNK
STEP = 256
HBM = pl.BlockSpec(memory_space=pltpu.HBM)


def permute(value, name, target):
    pairs = []
    for p in range(PARTS):
        for z in range(CHIPS):
            for c in range(CORES):
                for l in range(LAYERS):
                    tp, tz, tc, tl = target(p, z, c, l)
                    source = ((p * CHIPS + z) * CORES + c) * LAYERS + l
                    pairs.append((source, ((tp * CHIPS + tz) * CORES + tc) * LAYERS + tl))
    with jax.named_scope(name):
        return lax.ppermute(value, AXES, pairs)


to_part = functools.partial(permute, target=lambda p, z, c, l: (1 - p, z, c, l))
to_core = functools.partial(permute, target=lambda p, z, c, l: (p, z, 1 - c, l))
to_layer = functools.partial(permute, target=lambda p, z, c, l: (p, z, c, 1 - l))
to_near = functools.partial(permute, target=lambda p, z, c, l: (p, z ^ 1, c, l))
to_far = functools.partial(permute, target=lambda p, z, c, l: (p, z ^ 3, c, l))


def after(value, *others):
    return lax.optimization_barrier((value, *others))[0]


def place():
    store = lax.axis_index("store")
    return lax.axis_index("parts"), store // CORES, store % CORES, lax.axis_index("layer")


def split(x, terms):
    out = []
    for _ in range(terms):
        term = x.astype(bf16)
        out.append(term)
        x = x - term.astype(f32)
    return out


def dot(a, b):
    return lax.dot_general(a, b, (((1,), (0,)), ((), ())), preferred_element_type=f32)


def iota(shape, dim):
    return lax.broadcasted_iota(jnp.int32, shape, dim)


def factors(left, right):
    r, c = iota((256, 64), 0), iota((256, 64), 1)
    pick = jnp.where(c == 4 * (r % 16) + (r // 16) % 4, 1.0, 0.0).astype(bf16)
    r, c = iota((64, 256), 0), iota((64, 256), 1)
    pick_t = jnp.where(r == 4 * (c % 16) + (c // 16) % 4, 1.0, 0.0).astype(bf16)
    block = iota((256, 256), 0) // 64 == iota((256, 256), 1) // 64
    lefts = [
        jnp.where(block, dot(dot(pick, term).astype(bf16), pick_t), 0.0).astype(bf16)
        for term in split(left, 2)
    ]
    row = jnp.concatenate([right, right], axis=1)
    tiled = jnp.concatenate([jnp.concatenate([row] * 4, axis=1)] * 4, axis=0)
    block = iota((256, 512), 0) // 64 == iota((256, 512), 1) // 128
    return lefts, split(jnp.where(block, tiled, 0.0), 2)


def precond_rows(q_ref, lefts, rights, out):
    for at in range(0, q_ref.shape[0], CHUNK):
        values = precond_chunk(q_ref[at : at + CHUNK, :], lefts, rights)
        for t, value in enumerate(values):
            out[at : at + CHUNK, t * 256 : (t + 1) * 256] = value


def precond_chunk(q, lefts, rights):
    tiles = q.shape[1] // 256
    r, c = iota((256, 256), 0), iota((256, 256), 1)
    swap = jnp.where((r // 16 == c % 16) & (r % 16 == c // 16), 1.0, 0.0).astype(bf16)
    x = jnp.concatenate([q[:, t * 256 : (t + 1) * 256] for t in range(tiles)], axis=0)
    x = dot(swap, x).astype(bf16)
    z = dot(x, rights[0]) + dot(x, rights[1])
    sets = []
    for first in range(0, 16, 4):
        rows = [
            z[query * 16 : (query + 1) * 16, s * 128 : (s + 1) * 128]
            for query in range(first, first + 4)
            for s in range(4)
        ]
        sets.append(jnp.concatenate(rows, axis=0))
    high, low = split(jnp.concatenate(sets, axis=1), 2)
    z = dot(lefts[0], high) + (dot(lefts[0], low) + dot(lefts[1], high))
    side = iota((16, 128), 1) < 64
    rows = []
    for first in range(4):
        for k in range(4):
            o = z[k * 64 : (k + 1) * 64, first * 128 : (first + 1) * 128]
            pair = [jnp.where(side, o[0:16], o[16:32]), jnp.where(side, o[32:48], o[48:64])]
            rows.append(jnp.concatenate(pair, axis=1))
    y = dot(swap, jnp.concatenate(rows, axis=0).astype(bf16)).astype(bf16)
    return [y[t * 16 : (t + 1) * 16] for t in range(tiles)]


def own_kernel(q_hbm, left_hbm, right_hbm, mine, lefts_ref, rights_ref, q_ref, left, right, sems):
    at = pl.multiple_of(lax.axis_index("parts") * HALF, HALF)
    copies = [
        pltpu.make_async_copy(source, target, sems.at[k])
        for k, (source, target) in enumerate(
            ((left_hbm, left), (right_hbm, right), (q_hbm.at[pl.ds(at, HALF), :], q_ref))
        )
    ]
    for copy in copies:
        copy.start()
    copies[0].wait()
    copies[1].wait()
    lefts, rights = factors(left[...], right[...])
    for k in range(2):
        lefts_ref[k] = lefts[k]
        rights_ref[k] = rights[k]
    copies[2].wait()
    precond_rows(q_ref, lefts, rights, mine)


def rest_kernel(
    weight_ref, layer_ref, q_hbm, train_hbm, lefts_ref, rights_ref, rest, train, weight, q_ref, sems
):
    at = pl.multiple_of((1 - lax.axis_index("parts")) * HALF, HALF)
    q_copy = pltpu.make_async_copy(q_hbm.at[pl.ds(at, HALF), :], q_ref, sems.at[0])
    q_copy.start()
    copies = []
    for k in range(train.shape[0] // STEP):
        here = pl.ds(k * STEP, STEP)
        copies.append(pltpu.make_async_copy(train_hbm.at[here, :], train.at[here, :], sems.at[1 + k]))
        copies[-1].start()
    weight[...] = jnp.full(weight.shape, weight_ref[layer_ref[0]])
    lefts, rights = [lefts_ref[0], lefts_ref[1]], [rights_ref[0], rights_ref[1]]
    q_copy.wait()
    precond_rows(q_ref, lefts, rights, rest)
    for copy in copies:
        copy.wait()


def score_kernel(weight_ref, train_ref, *refs, picks, stored, early, columns):
    inputs, refs = refs[: len(picks)], refs[len(picks) :]
    n_before = sum(taken for _, _, taken in early)
    before, outs = refs[:n_before], refs[n_before:]
    weight = weight_ref[0:1, :]
    queries = jnp.concatenate(
        [piece[at : at + n, :] for piece, rows in zip(inputs, picks) for at, n in rows], axis=0
    )
    _, z, _, layer = place()
    near_is_mine = z // 2 == layer
    for at in range(*columns, STEP):
        there, here = slice(at, at + STEP), slice(at - columns[0], at - columns[0] + STEP)
        value = lax.dot_general(
            train_ref[there, :], queries, (((1,), (1,)), ((), ())), preferred_element_type=f32
        )
        value = weight * value.T
        if stored:
            outs[0][:, here] = value[:stored]
        if early:
            send, keep = outs[-2:]
            old, given = [], list(before)
            for first, rows, taken in early:
                old.append(
                    given.pop(0)[first : first + rows, there] if taken else value[first : first + rows]
                )
            old, new = jnp.concatenate(old, axis=0), value[stored:]
            send[:, here] = jnp.where(near_is_mine, new, old).astype(send.dtype)
            keep[:, here] = jnp.where(near_is_mine, old, new)


def kernel_call(kernel, outs, inputs, specs=None, scratch=()):
    return pl.pallas_call(
        kernel,
        out_shape=outs,
        in_specs=specs or [VMEM] * len(inputs),
        out_specs=[VMEM] * len(outs) if isinstance(outs, list) else VMEM,
        scratch_shapes=scratch,
        compiler_params=pltpu.CompilerParams(vmem_limit_bytes=LIMIT),
    )(*inputs)


def call_scores(weight, train, inputs, stored=0, early=(), columns=None):
    columns = columns or (0, train.shape[0])
    n = columns[1] - columns[0]
    total = sum(count for _, rows in inputs for _, count in rows)
    others = [a for a, _ in inputs] + [a for a, _, _ in early if a is not None]
    outs = [jax.ShapeDtypeStruct((stored, n), f32)] if stored else []
    if early:
        outs += [jax.ShapeDtypeStruct((total - stored, n), t) for t in (bf16, f32)]
    return kernel_call(
        functools.partial(
            score_kernel,
            picks=[rows for _, rows in inputs],
            stored=stored,
            early=[(first, rows, a is not None) for a, first, rows in early],
            columns=columns,
        ),
        outs,
        [weight, train, *others],
    )


def final_kernel(train_ids, query_ids, *refs, groups, n_given):
    given, refs = refs[:n_given], refs[n_given:]
    *_, out, done, sems = refs
    part, z, core, layer = place()
    low = z % 2
    first = jnp.where(z // 2 == layer, low, 1 - low)
    copies = []
    for k, (which, terms) in enumerate(groups):
        block = first if which < 2 else 1 - first
        half = part if which % 2 == 0 else 1 - part
        for i, c in enumerate((core, 1 - core)):
            at = pl.multiple_of(((block * 2 + c) * 2 + half) * HALF, HALF)
            to = slice((2 * k + i) * HALF, (2 * k + i + 1) * HALF)
            ids = query_ids[pl.ds(at, HALF), :]
            for keep, got, row, column in terms:
                keep, got = given[keep], given[got]
                columns = slice(column, column + keep.shape[1])
                total = keep[row + i * HALF : row + (i + 1) * HALF, :]
                total = total + got[row + i * HALF : row + (i + 1) * HALF, :].astype(f32)
                same = ids == train_ids[:, columns]
                done[to, columns] = jnp.where(same, jnp.float32(0.0), total)
            copies.append(
                pltpu.make_async_copy(done.at[to, :], out.at[pl.ds(at, HALF), :], sems.at[2 * k + i])
            )
            copies[-1].start()
    for copy in copies:
        copy.wait()


def call_final(train_ids, query_ids, given, groups, before=None):
    rows, n = query_ids.shape[0], train_ids.shape[1]
    inputs = [train_ids, query_ids, *given] + ([] if before is None else [before])
    return pl.pallas_call(
        functools.partial(final_kernel, groups=groups, n_given=len(given)),
        out_shape=jax.ShapeDtypeStruct((rows, n), f32),
        in_specs=[VMEM] * (2 + len(given)) + ([] if before is None else [HBM]),
        out_specs=HBM,
        scratch_shapes=[
            pltpu.VMEM((2 * len(groups) * HALF, n), f32),
            pltpu.SemaphoreType.DMA((2 * len(groups),)),
        ],
        input_output_aliases={} if before is None else {len(inputs) - 1: 0},
        compiler_params=pltpu.CompilerParams(vmem_limit_bytes=LIMIT),
    )(*inputs)


def small(
    train_grads,
    query_grads,
    left_factor,
    right_factor,
    layer_weight,
    layer_of,
    train_ids,
    query_ids,
):
    in_hbm = lambda array: pltpu.with_memory_space_constraint(array, pltpu.HBM)
    train, queries = in_hbm(train_grads[:, 0, :]), in_hbm(query_grads[:, 0, :])
    width, side = queries.shape[1], left_factor.shape[1]
    shape = jax.ShapeDtypeStruct
    mine, lefts, rights = kernel_call(
        own_kernel,
        [shape((HALF, width), bf16), shape((2, 256, 256), bf16), shape((2, 256, 512), bf16)],
        [queries, in_hbm(left_factor[0]), in_hbm(right_factor[0])],
        [HBM] * 3,
        [
            pltpu.VMEM((HALF, width), bf16),
            pltpu.VMEM((side, side), f32),
            pltpu.VMEM((side, side), f32),
            pltpu.SemaphoreType.DMA((3,)),
        ],
    )
    near = to_near(mine, "near")
    far = to_far(mine, "far")
    rest, train, weight = kernel_call(
        rest_kernel,
        [shape((HALF, width), bf16), shape(train.shape, bf16), shape((8, STEP), f32)],
        [in_hbm(layer_weight), layer_of, queries, train, lefts, rights],
        [SMEM, SMEM, HBM, HBM, VMEM, VMEM],
        [pltpu.VMEM((HALF, width), bf16), pltpu.SemaphoreType.DMA((1 + train.shape[0] // STEP,))],
    )
    score = functools.partial(call_scores, weight, train)

    def rows_of(*pieces):
        return [(piece, ((0, piece.shape[0]),)) for piece in pieces]

    mine_x = to_core(mine, "mine_x")
    rest_x = to_core(rest, "rest_x")
    near_x = to_core(near, "near_x")
    near_p = to_part(near, "near_p")
    far = after(far, near)
    cross = to_near(far, "cross")
    far_p = to_part(far, "far_p")
    far_x = to_core(far, "far_x")
    rest_x = after(rest_x, far)
    (early0,) = score(rows_of(mine, mine_x, rest, rest_x), stored=128)
    near_p = after(near_p, early0)
    near_px = to_core(near_p, "near_px")
    far_px = to_core(far_p, "far_px")
    cross_pa = to_part(cross[:CHUNK], "cross_pa")
    cross_pb = to_near(far_p[CHUNK:], "cross_pb")
    cross_x = to_core(cross, "cross_x")
    early1, send0, keep0 = score(
        rows_of(near, near_x, near_p, near_px, far, far_x, far_p, far_px),
        stored=128,
        early=[(early0, 0, 128)],
    )
    got0 = to_layer(send0, "got0")
    cross_pa, cross_pb = after(cross_pa, send0), after(cross_pb, send0)
    cross_pxa = to_core(cross_pa, "cross_pxa")
    cross_pxb = to_core(cross_pb, "cross_pxb")
    last = rows_of(cross, cross_x, cross_pa, cross_pb, cross_pxa, cross_pxb)
    n = train.shape[0]
    send1, keep1 = score(last, early=[(early1, 0, 128)], columns=(0, n // 2))
    got1 = to_layer(send1, "got1")
    early1 = after(early1, send1)
    send2, keep2 = score(last, early=[(early1, 0, 128)], columns=(n // 2, n))
    send2 = after(send2, got0)
    got2 = to_layer(send2, "got2")

    train_ids, query_ids = train_ids[None, :], query_ids[:, None]
    most = call_final(
        train_ids, query_ids, [keep0, got0], ((0, [(0, 1, 0, 0)]), (1, [(0, 1, 64, 0)]))
    )
    return call_final(
        train_ids,
        query_ids,
        [keep1, got1, keep2, got2],
        ((2, [(0, 1, 0, 0), (2, 3, 0, n // 2)]), (3, [(0, 1, 64, 0), (2, 3, 64, n // 2)])),
        most,
    )


def solution(mesh):
    placed = (
        P(("parts", "store"), "layer", None),
        P("store", "layer", None),
        P("layer", None, None),
        P("layer", None, None),
        P(),
        P("layer"),
        P(("parts", "store")),
        P("layer"),
    )
    sizes = tuple(mesh.shape[axis] for axis in AXES)
    return jax.shard_map(
        small if sizes == (PARTS, CHIPS * CORES, LAYERS) else general,
        mesh=mesh,
        in_specs=placed,
        out_specs=P("layer", ("parts", "store")),
        check_vma=False,
    )
```

```python
import functools

import jax
import jax.numpy as jnp
from jax import lax
from jax.experimental import pallas as pl
from jax.experimental.pallas import tpu as pltpu
from jax.sharding import PartitionSpec as P

AXES = ("parts", "store", "layer")
VMEM = pl.BlockSpec(memory_space=pltpu.VMEM)
SMEM = pl.BlockSpec(memory_space=pltpu.SMEM)
bf16, f32 = jnp.bfloat16, jnp.float32
LIMIT = 20 * 1024 * 1024


def preconditioned(query_grads, left_factor, right_factor):
    q_rows, slots, width = query_grads.shape
    side = left_factor.shape[1]
    mats = query_grads.astype(jnp.float32).reshape(q_rows, slots, side, side)
    half = jnp.einsum("lij,qljk->qlik", left_factor, mats, precision=lax.Precision.HIGHEST)
    full = jnp.einsum("qlik,lkm->qlim", half, right_factor, precision=lax.Precision.HIGHEST)
    return full.reshape(q_rows, slots, width).astype(jnp.bfloat16)


def general(
    train_grads,
    query_grads,
    left_factor,
    right_factor,
    layer_weight,
    layer_of,
    train_ids,
    query_ids,
):
    precond = preconditioned(query_grads, left_factor, right_factor)
    weight = jnp.take(layer_weight, layer_of[0])
    queries = lax.all_gather(precond, "store", axis=0, tiled=True)
    terms = weight * jnp.dot(
        queries[:, 0, :], train_grads[:, 0, :].T, preferred_element_type=jnp.float32
    )
    summed = lax.psum_scatter(terms, "layer", scatter_dimension=0, tiled=True)
    same = query_ids[:, None] == train_ids[None, :]
    return jnp.where(same, jnp.float32(0.0), summed)


PARTS, CHIPS, CORES, LAYERS = 2, 4, 2, 2
CHUNK = 16
HALF = 2 * CHUNK
STEP = 256
HBM = pl.BlockSpec(memory_space=pltpu.HBM)


def permute(value, name, target):
    pairs = []
    for p in range(PARTS):
        for z in range(CHIPS):
            for c in range(CORES):
                for l in range(LAYERS):
                    tp, tz, tc, tl = target(p, z, c, l)
                    source = ((p * CHIPS + z) * CORES + c) * LAYERS + l
                    pairs.append((source, ((tp * CHIPS + tz) * CORES + tc) * LAYERS + tl))
    with jax.named_scope(name):
        return lax.ppermute(value, AXES, pairs)


to_part = functools.partial(permute, target=lambda p, z, c, l: (1 - p, z, c, l))
to_core = functools.partial(permute, target=lambda p, z, c, l: (p, z, 1 - c, l))
to_layer = functools.partial(permute, target=lambda p, z, c, l: (p, z, c, 1 - l))
to_near = functools.partial(permute, target=lambda p, z, c, l: (p, z ^ 1, c, l))
to_far = functools.partial(permute, target=lambda p, z, c, l: (p, z ^ 3, c, l))


def after(value, *others):
    return lax.optimization_barrier((value, *others))[0]


def place():
    store = lax.axis_index("store")
    return lax.axis_index("parts"), store // CORES, store % CORES, lax.axis_index("layer")


def split(x, terms):
    out = []
    for _ in range(terms):
        term = x.astype(bf16)
        out.append(term)
        x = x - term.astype(f32)
    return out


def dot(a, b):
    return lax.dot_general(a, b, (((1,), (0,)), ((), ())), preferred_element_type=f32)


def iota(shape, dim):
    return lax.broadcasted_iota(jnp.int32, shape, dim)


def factors(left, right):
    r, c = iota((256, 64), 0), iota((256, 64), 1)
    pick = jnp.where(c == 4 * (r % 16) + (r // 16) % 4, 1.0, 0.0).astype(bf16)
    r, c = iota((64, 256), 0), iota((64, 256), 1)
    pick_t = jnp.where(r == 4 * (c % 16) + (c // 16) % 4, 1.0, 0.0).astype(bf16)
    block = iota((256, 256), 0) // 64 == iota((256, 256), 1) // 64
    lefts = [
        jnp.where(block, dot(dot(pick, term).astype(bf16), pick_t), 0.0).astype(bf16)
        for term in split(left, 2)
    ]
    row = jnp.concatenate([right, right], axis=1)
    tiled = jnp.concatenate([jnp.concatenate([row] * 4, axis=1)] * 4, axis=0)
    block = iota((256, 512), 0) // 64 == iota((256, 512), 1) // 128
    return lefts, split(jnp.where(block, tiled, 0.0), 2)


def precond_rows(q_ref, lefts, rights, out):
    for at in range(0, q_ref.shape[0], CHUNK):
        values = precond_chunk(q_ref[at : at + CHUNK, :], lefts, rights)
        for t, value in enumerate(values):
            out[at : at + CHUNK, t * 256 : (t + 1) * 256] = value


def precond_chunk(q, lefts, rights):
    tiles = q.shape[1] // 256
    r, c = iota((256, 256), 0), iota((256, 256), 1)
    swap = jnp.where((r // 16 == c % 16) & (r % 16 == c // 16), 1.0, 0.0).astype(bf16)
    x = jnp.concatenate([q[:, t * 256 : (t + 1) * 256] for t in range(tiles)], axis=0)
    x = dot(swap, x).astype(bf16)
    z = dot(x, rights[0]) + dot(x, rights[1])
    sets = []
    for first in range(0, 16, 4):
        rows = [
            z[query * 16 : (query + 1) * 16, s * 128 : (s + 1) * 128]
            for query in range(first, first + 4)
            for s in range(4)
        ]
        sets.append(jnp.concatenate(rows, axis=0))
    high, low = split(jnp.concatenate(sets, axis=1), 2)
    z = dot(lefts[0], high) + (dot(lefts[0], low) + dot(lefts[1], high))
    side = iota((16, 128), 1) < 64
    rows = []
    for first in range(4):
        for k in range(4):
            o = z[k * 64 : (k + 1) * 64, first * 128 : (first + 1) * 128]
            pair = [jnp.where(side, o[0:16], o[16:32]), jnp.where(side, o[32:48], o[48:64])]
            rows.append(jnp.concatenate(pair, axis=1))
    y = dot(swap, jnp.concatenate(rows, axis=0).astype(bf16)).astype(bf16)
    return [y[t * 16 : (t + 1) * 16] for t in range(tiles)]


def own_kernel(q_hbm, left_hbm, right_hbm, mine, lefts_ref, rights_ref, q_ref, left, right, sems):
    at = pl.multiple_of(lax.axis_index("parts") * HALF, HALF)
    copies = [
        pltpu.make_async_copy(source, target, sems.at[k])
        for k, (source, target) in enumerate(
            ((left_hbm, left), (right_hbm, right), (q_hbm.at[pl.ds(at, HALF), :], q_ref))
        )
    ]
    for copy in copies:
        copy.start()
    copies[0].wait()
    copies[1].wait()
    lefts, rights = factors(left[...], right[...])
    for k in range(2):
        lefts_ref[k] = lefts[k]
        rights_ref[k] = rights[k]
    copies[2].wait()
    precond_rows(q_ref, lefts, rights, mine)


def rest_kernel(
    weight_ref, layer_ref, q_hbm, train_hbm, lefts_ref, rights_ref, rest, train, weight, q_ref, sems
):
    at = pl.multiple_of((1 - lax.axis_index("parts")) * HALF, HALF)
    q_copy = pltpu.make_async_copy(q_hbm.at[pl.ds(at, HALF), :], q_ref, sems.at[0])
    q_copy.start()
    copies = []
    for k in range(train.shape[0] // STEP):
        here = pl.ds(k * STEP, STEP)
        copies.append(pltpu.make_async_copy(train_hbm.at[here, :], train.at[here, :], sems.at[1 + k]))
        copies[-1].start()
    weight[...] = jnp.full(weight.shape, weight_ref[layer_ref[0]])
    lefts, rights = [lefts_ref[0], lefts_ref[1]], [rights_ref[0], rights_ref[1]]
    q_copy.wait()
    precond_rows(q_ref, lefts, rights, rest)
    for copy in copies:
        copy.wait()


def score_kernel(weight_ref, train_ref, *refs, picks, stored, early, columns):
    inputs, refs = refs[: len(picks)], refs[len(picks) :]
    n_before = sum(taken for _, _, taken in early)
    before, outs = refs[:n_before], refs[n_before:]
    weight = weight_ref[0:1, :]
    queries = jnp.concatenate(
        [piece[at : at + n, :] for piece, rows in zip(inputs, picks) for at, n in rows], axis=0
    )
    _, z, _, layer = place()
    near_is_mine = z // 2 == layer
    for at in range(*columns, STEP):
        there, here = slice(at, at + STEP), slice(at - columns[0], at - columns[0] + STEP)
        value = lax.dot_general(
            train_ref[there, :], queries, (((1,), (1,)), ((), ())), preferred_element_type=f32
        )
        value = weight * value.T
        if stored:
            outs[0][:, here] = value[:stored]
        if early:
            send, keep = outs[-2:]
            old, given = [], list(before)
            for first, rows, taken in early:
                old.append(
                    given.pop(0)[first : first + rows, there] if taken else value[first : first + rows]
                )
            old, new = jnp.concatenate(old, axis=0), value[stored:]
            send[:, here] = jnp.where(near_is_mine, new, old).astype(send.dtype)
            keep[:, here] = jnp.where(near_is_mine, old, new)


def kernel_call(kernel, outs, inputs, specs=None, scratch=()):
    return pl.pallas_call(
        kernel,
        out_shape=outs,
        in_specs=specs or [VMEM] * len(inputs),
        out_specs=[VMEM] * len(outs) if isinstance(outs, list) else VMEM,
        scratch_shapes=scratch,
        compiler_params=pltpu.CompilerParams(vmem_limit_bytes=LIMIT),
    )(*inputs)


def call_scores(weight, train, inputs, stored=0, early=(), columns=None):
    columns = columns or (0, train.shape[0])
    n = columns[1] - columns[0]
    total = sum(count for _, rows in inputs for _, count in rows)
    others = [a for a, _ in inputs] + [a for a, _, _ in early if a is not None]
    outs = [jax.ShapeDtypeStruct((stored, n), f32)] if stored else []
    if early:
        outs += [jax.ShapeDtypeStruct((total - stored, n), t) for t in (bf16, f32)]
    return kernel_call(
        functools.partial(
            score_kernel,
            picks=[rows for _, rows in inputs],
            stored=stored,
            early=[(first, rows, a is not None) for a, first, rows in early],
            columns=columns,
        ),
        outs,
        [weight, train, *others],
    )


def final_kernel(train_ids, query_ids, *refs, groups, n_given):
    given, refs = refs[:n_given], refs[n_given:]
    *_, out, done, sems = refs
    part, z, core, layer = place()
    low = z % 2
    first = jnp.where(z // 2 == layer, low, 1 - low)
    copies = []
    for k, (which, terms) in enumerate(groups):
        block = first if which < 2 else 1 - first
        half = part if which % 2 == 0 else 1 - part
        for i, c in enumerate((core, 1 - core)):
            at = pl.multiple_of(((block * 2 + c) * 2 + half) * HALF, HALF)
            to = slice((2 * k + i) * HALF, (2 * k + i + 1) * HALF)
            ids = query_ids[pl.ds(at, HALF), :]
            for keep, got, row, column in terms:
                keep, got = given[keep], given[got]
                columns = slice(column, column + keep.shape[1])
                total = keep[row + i * HALF : row + (i + 1) * HALF, :]
                total = total + got[row + i * HALF : row + (i + 1) * HALF, :].astype(f32)
                same = ids == train_ids[:, columns]
                done[to, columns] = jnp.where(same, jnp.float32(0.0), total)
            copies.append(
                pltpu.make_async_copy(done.at[to, :], out.at[pl.ds(at, HALF), :], sems.at[2 * k + i])
            )
            copies[-1].start()
    for copy in copies:
        copy.wait()


def call_final(train_ids, query_ids, given, groups, before=None):
    rows, n = query_ids.shape[0], train_ids.shape[1]
    inputs = [train_ids, query_ids, *given] + ([] if before is None else [before])
    return pl.pallas_call(
        functools.partial(final_kernel, groups=groups, n_given=len(given)),
        out_shape=jax.ShapeDtypeStruct((rows, n), f32),
        in_specs=[VMEM] * (2 + len(given)) + ([] if before is None else [HBM]),
        out_specs=HBM,
        scratch_shapes=[
            pltpu.VMEM((2 * len(groups) * HALF, n), f32),
            pltpu.SemaphoreType.DMA((2 * len(groups),)),
        ],
        input_output_aliases={} if before is None else {len(inputs) - 1: 0},
        compiler_params=pltpu.CompilerParams(vmem_limit_bytes=LIMIT),
    )(*inputs)


def small(
    train_grads,
    query_grads,
    left_factor,
    right_factor,
    layer_weight,
    layer_of,
    train_ids,
    query_ids,
):
    in_hbm = lambda array: pltpu.with_memory_space_constraint(array, pltpu.HBM)
    train, queries = in_hbm(train_grads[:, 0, :]), in_hbm(query_grads[:, 0, :])
    width, side = queries.shape[1], left_factor.shape[1]
    shape = jax.ShapeDtypeStruct
    mine, lefts, rights = kernel_call(
        own_kernel,
        [shape((HALF, width), bf16), shape((2, 256, 256), bf16), shape((2, 256, 512), bf16)],
        [queries, in_hbm(left_factor[0]), in_hbm(right_factor[0])],
        [HBM] * 3,
        [
            pltpu.VMEM((HALF, width), bf16),
            pltpu.VMEM((side, side), f32),
            pltpu.VMEM((side, side), f32),
            pltpu.SemaphoreType.DMA((3,)),
        ],
    )
    near = to_near(mine, "near")
    far = to_far(mine, "far")
    rest, train, weight = kernel_call(
        rest_kernel,
        [shape((HALF, width), bf16), shape(train.shape, bf16), shape((8, STEP), f32)],
        [in_hbm(layer_weight), layer_of, queries, train, lefts, rights],
        [SMEM, SMEM, HBM, HBM, VMEM, VMEM],
        [pltpu.VMEM((HALF, width), bf16), pltpu.SemaphoreType.DMA((1 + train.shape[0] // STEP,))],
    )
    score = functools.partial(call_scores, weight, train)

    def rows_of(*pieces):
        return [(piece, ((0, piece.shape[0]),)) for piece in pieces]

    mine_x = to_core(mine, "mine_x")
    rest_x = to_core(rest, "rest_x")
    near_x = to_core(near, "near_x")
    near_p = to_part(near, "near_p")
    far = after(far, near)
    cross = to_near(far, "cross")
    far_p = to_part(far, "far_p")
    far_xa = to_core(far[:CHUNK], "far_xa")
    far_xb = to_core(far[CHUNK:], "far_xb")
    near_px = to_core(near_p, "near_px")
    (early,) = score(rows_of(mine, mine_x, rest, rest_x, near, near_x), stored=192)
    far_xb = after(far_xb, near_px)
    send0, keep0 = score(rows_of(far, far_xa, far_xb), early=[(early, 0, 64)])
    got0 = to_layer(send0, "got0")

    far_p, cross = after(far_p, send0), after(cross, send0)
    cross_p = to_near(far_p, "cross_p")
    far_px = to_core(far_p, "far_px")
    cross_x = to_core(cross, "cross_x")
    send1, keep1 = score(rows_of(far_p, far_px, cross, cross_x), early=[(early, 64, 128)])
    got1 = to_layer(send1, "got1")

    cross_p = after(cross_p, send1, got0)
    cross_px0 = to_core(cross_p[:CHUNK], "cross_px0")
    cross_px1 = to_core(cross_p[CHUNK:], "cross_px1")
    last = rows_of(near_p, near_px, cross_p, cross_px0, cross_px1)
    n, itself = train.shape[0], [(None, 0, 64)]
    _, send2, keep2 = score(last, stored=64, early=itself, columns=(0, n // 2))
    got2 = to_layer(send2, "got2")
    cross_p = after(cross_p, send2)
    last = rows_of(near_p, near_px, cross_p, cross_px0, cross_px1)
    _, send3, keep3 = score(last, stored=64, early=itself, columns=(n // 2, n))
    send3 = after(send3, got1)
    got3 = to_layer(send3, "got3")

    train_ids, query_ids = train_ids[None, :], query_ids[:, None]
    most = call_final(
        train_ids,
        query_ids,
        [keep0, got0, keep1, got1],
        ((0, [(0, 1, 0, 0)]), (1, [(2, 3, 0, 0)]), (2, [(2, 3, 64, 0)])),
    )
    return call_final(
        train_ids,
        query_ids,
        [keep2, got2, keep3, got3],
        ((3, [(0, 1, 0, 0), (2, 3, 0, n // 2)]),),
        most,
    )


def solution(mesh):
    placed = (
        P(("parts", "store"), "layer", None),
        P("store", "layer", None),
        P("layer", None, None),
        P("layer", None, None),
        P(),
        P("layer"),
        P(("parts", "store")),
        P("layer"),
    )
    sizes = tuple(mesh.shape[axis] for axis in AXES)
    return jax.shard_map(
        small if sizes == (PARTS, CHIPS * CORES, LAYERS) else general,
        mesh=mesh,
        in_specs=placed,
        out_specs=P("layer", ("parts", "store")),
        check_vma=False,
    )
```

```python
import functools

import jax
import jax.numpy as jnp
from jax import lax
from jax.experimental import pallas as pl
from jax.experimental.pallas import tpu as pltpu
from jax.sharding import PartitionSpec as P

AXES = ("parts", "store", "layer")
VMEM = pl.BlockSpec(memory_space=pltpu.VMEM)
SMEM = pl.BlockSpec(memory_space=pltpu.SMEM)
bf16, f32 = jnp.bfloat16, jnp.float32
LIMIT = 20 * 1024 * 1024


def preconditioned(query_grads, left_factor, right_factor):
    q_rows, slots, width = query_grads.shape
    side = left_factor.shape[1]
    mats = query_grads.astype(jnp.float32).reshape(q_rows, slots, side, side)
    half = jnp.einsum("lij,qljk->qlik", left_factor, mats, precision=lax.Precision.HIGHEST)
    full = jnp.einsum("qlik,lkm->qlim", half, right_factor, precision=lax.Precision.HIGHEST)
    return full.reshape(q_rows, slots, width).astype(jnp.bfloat16)


def general(
    train_grads,
    query_grads,
    left_factor,
    right_factor,
    layer_weight,
    layer_of,
    train_ids,
    query_ids,
):
    precond = preconditioned(query_grads, left_factor, right_factor)
    weight = jnp.take(layer_weight, layer_of[0])
    queries = lax.all_gather(precond, "store", axis=0, tiled=True)
    terms = weight * jnp.dot(
        queries[:, 0, :], train_grads[:, 0, :].T, preferred_element_type=jnp.float32
    )
    summed = lax.psum_scatter(terms, "layer", scatter_dimension=0, tiled=True)
    same = query_ids[:, None] == train_ids[None, :]
    return jnp.where(same, jnp.float32(0.0), summed)


PARTS, CHIPS, CORES, LAYERS = 2, 4, 2, 2
CHUNK = 16
HALF = 2 * CHUNK
STEP = 256
HBM = pl.BlockSpec(memory_space=pltpu.HBM)


def permute(value, name, target):
    pairs = []
    for p in range(PARTS):
        for z in range(CHIPS):
            for c in range(CORES):
                for l in range(LAYERS):
                    tp, tz, tc, tl = target(p, z, c, l)
                    source = ((p * CHIPS + z) * CORES + c) * LAYERS + l
                    pairs.append((source, ((tp * CHIPS + tz) * CORES + tc) * LAYERS + tl))
    with jax.named_scope(name):
        return lax.ppermute(value, AXES, pairs)


to_part = functools.partial(permute, target=lambda p, z, c, l: (1 - p, z, c, l))
to_core = functools.partial(permute, target=lambda p, z, c, l: (p, z, 1 - c, l))
to_layer = functools.partial(permute, target=lambda p, z, c, l: (p, z, c, 1 - l))
to_near = functools.partial(permute, target=lambda p, z, c, l: (p, z ^ 1, c, l))
to_far = functools.partial(permute, target=lambda p, z, c, l: (p, z ^ 3, c, l))


def after(value, *others):
    return lax.optimization_barrier((value, *others))[0]


def place():
    store = lax.axis_index("store")
    return lax.axis_index("parts"), store // CORES, store % CORES, lax.axis_index("layer")


def split(x, terms):
    out = []
    for _ in range(terms):
        term = x.astype(bf16)
        out.append(term)
        x = x - term.astype(f32)
    return out


def dot(a, b):
    return lax.dot_general(a, b, (((1,), (0,)), ((), ())), preferred_element_type=f32)


def iota(shape, dim):
    return lax.broadcasted_iota(jnp.int32, shape, dim)


def factors(left, right):
    r, c = iota((256, 64), 0), iota((256, 64), 1)
    pick = jnp.where(c == 4 * (r % 16) + (r // 16) % 4, 1.0, 0.0).astype(bf16)
    r, c = iota((64, 256), 0), iota((64, 256), 1)
    pick_t = jnp.where(r == 4 * (c % 16) + (c // 16) % 4, 1.0, 0.0).astype(bf16)
    block = iota((256, 256), 0) // 64 == iota((256, 256), 1) // 64
    lefts = [
        jnp.where(block, dot(dot(pick, term).astype(bf16), pick_t), 0.0).astype(bf16)
        for term in split(left, 2)
    ]
    row = jnp.concatenate([right, right], axis=1)
    tiled = jnp.concatenate([jnp.concatenate([row] * 4, axis=1)] * 4, axis=0)
    block = iota((256, 512), 0) // 64 == iota((256, 512), 1) // 128
    return lefts, split(jnp.where(block, tiled, 0.0), 2)


def precond_rows(q_ref, lefts, rights, out):
    for at in range(0, q_ref.shape[0], CHUNK):
        values = precond_chunk(q_ref[at : at + CHUNK, :], lefts, rights)
        for t, value in enumerate(values):
            out[at : at + CHUNK, t * 256 : (t + 1) * 256] = value


def precond_chunk(q, lefts, rights):
    tiles = q.shape[1] // 256
    r, c = iota((256, 256), 0), iota((256, 256), 1)
    swap = jnp.where((r // 16 == c % 16) & (r % 16 == c // 16), 1.0, 0.0).astype(bf16)
    x = jnp.concatenate([q[:, t * 256 : (t + 1) * 256] for t in range(tiles)], axis=0)
    x = dot(swap, x).astype(bf16)
    z = dot(x, rights[0]) + dot(x, rights[1])
    sets = []
    for first in range(0, 16, 4):
        rows = [
            z[query * 16 : (query + 1) * 16, s * 128 : (s + 1) * 128]
            for query in range(first, first + 4)
            for s in range(4)
        ]
        sets.append(jnp.concatenate(rows, axis=0))
    high, low = split(jnp.concatenate(sets, axis=1), 2)
    z = dot(lefts[0], high) + (dot(lefts[0], low) + dot(lefts[1], high))
    side = iota((16, 128), 1) < 64
    rows = []
    for first in range(4):
        for k in range(4):
            o = z[k * 64 : (k + 1) * 64, first * 128 : (first + 1) * 128]
            pair = [jnp.where(side, o[0:16], o[16:32]), jnp.where(side, o[32:48], o[48:64])]
            rows.append(jnp.concatenate(pair, axis=1))
    y = dot(swap, jnp.concatenate(rows, axis=0).astype(bf16)).astype(bf16)
    return [y[t * 16 : (t + 1) * 16] for t in range(tiles)]


def own_kernel(q_hbm, left_hbm, right_hbm, mine, lefts_ref, rights_ref, q_ref, left, right, sems):
    at = pl.multiple_of(lax.axis_index("parts") * HALF, HALF)
    copies = [
        pltpu.make_async_copy(source, target, sems.at[k])
        for k, (source, target) in enumerate(
            ((left_hbm, left), (right_hbm, right), (q_hbm.at[pl.ds(at, HALF), :], q_ref))
        )
    ]
    for copy in copies:
        copy.start()
    copies[0].wait()
    copies[1].wait()
    lefts, rights = factors(left[...], right[...])
    for k in range(2):
        lefts_ref[k] = lefts[k]
        rights_ref[k] = rights[k]
    copies[2].wait()
    precond_rows(q_ref, lefts, rights, mine)


def rest_kernel(
    weight_ref, layer_ref, q_hbm, train_hbm, lefts_ref, rights_ref, rest, train, weight, q_ref, sems
):
    at = pl.multiple_of((1 - lax.axis_index("parts")) * HALF, HALF)
    q_copy = pltpu.make_async_copy(q_hbm.at[pl.ds(at, HALF), :], q_ref, sems.at[0])
    q_copy.start()
    copies = []
    for k in range(train.shape[0] // STEP):
        here = pl.ds(k * STEP, STEP)
        copies.append(pltpu.make_async_copy(train_hbm.at[here, :], train.at[here, :], sems.at[1 + k]))
        copies[-1].start()
    weight[...] = jnp.full(weight.shape, weight_ref[layer_ref[0]])
    lefts, rights = [lefts_ref[0], lefts_ref[1]], [rights_ref[0], rights_ref[1]]
    q_copy.wait()
    precond_rows(q_ref, lefts, rights, rest)
    for copy in copies:
        copy.wait()


def score_kernel(weight_ref, train_ref, *refs, picks, stored, early, columns):
    inputs, refs = refs[: len(picks)], refs[len(picks) :]
    n_before = sum(taken for _, _, taken in early)
    before, outs = refs[:n_before], refs[n_before:]
    weight = weight_ref[0:1, :]
    queries = jnp.concatenate(
        [piece[at : at + n, :] for piece, rows in zip(inputs, picks) for at, n in rows], axis=0
    )
    _, z, _, layer = place()
    near_is_mine = z // 2 == layer
    for at in range(*columns, STEP):
        there, here = slice(at, at + STEP), slice(at - columns[0], at - columns[0] + STEP)
        value = lax.dot_general(
            train_ref[there, :], queries, (((1,), (1,)), ((), ())), preferred_element_type=f32
        )
        value = weight * value.T
        if stored:
            outs[0][:, here] = value[:stored]
        if early:
            send, keep = outs[-2:]
            old, given = [], list(before)
            for first, rows, taken in early:
                old.append(
                    given.pop(0)[first : first + rows, there] if taken else value[first : first + rows]
                )
            old, new = jnp.concatenate(old, axis=0), value[stored:]
            send[:, here] = jnp.where(near_is_mine, new, old).astype(send.dtype)
            keep[:, here] = jnp.where(near_is_mine, old, new)


def kernel_call(kernel, outs, inputs, specs=None, scratch=()):
    return pl.pallas_call(
        kernel,
        out_shape=outs,
        in_specs=specs or [VMEM] * len(inputs),
        out_specs=[VMEM] * len(outs) if isinstance(outs, list) else VMEM,
        scratch_shapes=scratch,
        compiler_params=pltpu.CompilerParams(vmem_limit_bytes=LIMIT),
    )(*inputs)


def call_scores(weight, train, inputs, stored=0, early=(), columns=None):
    columns = columns or (0, train.shape[0])
    n = columns[1] - columns[0]
    total = sum(count for _, rows in inputs for _, count in rows)
    others = [a for a, _ in inputs] + [a for a, _, _ in early if a is not None]
    outs = [jax.ShapeDtypeStruct((stored, n), f32)] if stored else []
    if early:
        outs += [jax.ShapeDtypeStruct((total - stored, n), t) for t in (bf16, f32)]
    return kernel_call(
        functools.partial(
            score_kernel,
            picks=[rows for _, rows in inputs],
            stored=stored,
            early=[(first, rows, a is not None) for a, first, rows in early],
            columns=columns,
        ),
        outs,
        [weight, train, *others],
    )


def final_kernel(train_ids, query_ids, *refs, groups, n_given):
    given, refs = refs[:n_given], refs[n_given:]
    *_, out, done, sems = refs
    part, z, core, layer = place()
    low = z % 2
    first = jnp.where(z // 2 == layer, low, 1 - low)
    copies = []
    for k, (which, keep, got, row, column) in enumerate(groups):
        block = first if which < 2 else 1 - first
        half = part if which % 2 == 0 else 1 - part
        keep, got = given[keep], given[got]
        columns = pl.ds(column, keep.shape[1])
        for i, c in enumerate((core, 1 - core)):
            at = pl.multiple_of(((block * 2 + c) * 2 + half) * HALF, HALF)
            here, j = slice(row + i * HALF, row + (i + 1) * HALF), 2 * k + i
            total = keep[here, :] + got[here, :].astype(f32)
            same = query_ids[pl.ds(at, HALF), :] == train_ids[:, columns]
            slot = done.at[j * HALF : (j + 1) * HALF, : keep.shape[1]]
            slot[...] = jnp.where(same, jnp.float32(0.0), total)
            copies.append(
                pltpu.make_async_copy(slot, out.at[pl.ds(at, HALF), columns], sems.at[j])
            )
            copies[-1].start()
    for copy in copies:
        copy.wait()


def call_final(train_ids, query_ids, given, groups, before=None):
    rows, n = query_ids.shape[0], train_ids.shape[1]
    inputs = [train_ids, query_ids, *given] + ([] if before is None else [before])
    return pl.pallas_call(
        functools.partial(final_kernel, groups=groups, n_given=len(given)),
        out_shape=jax.ShapeDtypeStruct((rows, n), f32),
        in_specs=[VMEM] * (2 + len(given)) + ([] if before is None else [HBM]),
        out_specs=HBM,
        scratch_shapes=[
            pltpu.VMEM((2 * len(groups) * HALF, max(a.shape[1] for a in given)), f32),
            pltpu.SemaphoreType.DMA((2 * len(groups),)),
        ],
        input_output_aliases={} if before is None else {len(inputs) - 1: 0},
        compiler_params=pltpu.CompilerParams(vmem_limit_bytes=LIMIT),
    )(*inputs)


def small(
    train_grads,
    query_grads,
    left_factor,
    right_factor,
    layer_weight,
    layer_of,
    train_ids,
    query_ids,
):
    in_hbm = lambda array: pltpu.with_memory_space_constraint(array, pltpu.HBM)
    train, queries = in_hbm(train_grads[:, 0, :]), in_hbm(query_grads[:, 0, :])
    width, side = queries.shape[1], left_factor.shape[1]
    shape = jax.ShapeDtypeStruct
    mine, lefts, rights = kernel_call(
        own_kernel,
        [shape((HALF, width), bf16), shape((2, 256, 256), bf16), shape((2, 256, 512), bf16)],
        [queries, in_hbm(left_factor[0]), in_hbm(right_factor[0])],
        [HBM] * 3,
        [
            pltpu.VMEM((HALF, width), bf16),
            pltpu.VMEM((side, side), f32),
            pltpu.VMEM((side, side), f32),
            pltpu.SemaphoreType.DMA((3,)),
        ],
    )
    near = to_near(mine, "near")
    far = to_far(mine, "far")
    rest, train, weight = kernel_call(
        rest_kernel,
        [shape((HALF, width), bf16), shape(train.shape, bf16), shape((8, STEP), f32)],
        [in_hbm(layer_weight), layer_of, queries, train, lefts, rights],
        [SMEM, SMEM, HBM, HBM, VMEM, VMEM],
        [pltpu.VMEM((HALF, width), bf16), pltpu.SemaphoreType.DMA((1 + train.shape[0] // STEP,))],
    )
    score = functools.partial(call_scores, weight, train)

    def rows_of(*pieces):
        return [(piece, ((0, piece.shape[0]),)) for piece in pieces]

    mine_x = to_core(mine, "mine_x")
    rest_x = to_core(rest, "rest_x")
    near_x = to_core(near, "near_x")
    near_p = to_part(near, "near_p")
    mine_x = after(mine_x, near_x)
    far = after(far, near)
    cross = to_near(far, "cross")
    far_p = to_part(far, "far_p")
    far_x = to_core(far, "far_x")
    rest_x = after(rest_x, far)
    (early0,) = score(rows_of(mine, mine_x, rest, rest_x), stored=128)
    near_p = after(near_p, early0)
    near_px = to_core(near_p, "near_px")

    far_px0 = to_core(far_p[:CHUNK], "far_px0")
    far_px1 = to_core(far_p[CHUNK:], "far_px1")
    cross_pa = to_part(after(cross[:CHUNK], far_x), "cross_pa")
    cross_pb = to_near(after(far_p[CHUNK:], far_x), "cross_pb")
    cross_x = to_core(cross, "cross_x")
    far_px1 = after(far_px1, cross_x)
    early1, send0, keep0 = score(
        rows_of(near, near_x, near_p, near_px, far, far_x, far_p, far_px0, far_px1),
        stored=128,
        early=[(early0, 0, 128)],
    )
    got0 = to_layer(send0, "got0")
    cross_pa, cross_pb = after(cross_pa, send0), after(cross_pb, send0)
    def by_columns(piece, name):
        parts = [to_core(part, name) for part in jnp.split(piece, 2, axis=1)]
        return jnp.concatenate(parts, axis=1)

    cross_pxa, cross_pxb = by_columns(cross_pa, "cross_pxa"), by_columns(cross_pb, "cross_pxb")
    last = rows_of(cross, cross_x, cross_pa, cross_pb, cross_pxa, cross_pxb)
    n = train.shape[0]
    cut = n * 3 // 4
    send1, keep1 = score(last, early=[(early1, 0, 128)], columns=(0, cut))
    got1 = to_layer(send1, "got1")
    early1 = after(early1, send1)
    send2, keep2 = score(last, early=[(early1, 0, 128)], columns=(cut, n))
    send2 = after(send2, got0)
    got2 = to_layer(send2, "got2")

    train_ids, query_ids = train_ids[None, :], query_ids[:, None]
    most = call_final(
        train_ids,
        query_ids,
        [keep0, got0, keep1, got1],
        ((0, 0, 1, 0, 0), (1, 0, 1, 64, 0), (2, 2, 3, 0, 0), (3, 2, 3, 64, 0)),
    )
    return call_final(
        train_ids, query_ids, [keep2, got2], ((2, 0, 1, 0, cut), (3, 0, 1, 64, cut)), most
    )


def solution(mesh):
    placed = (
        P(("parts", "store"), "layer", None),
        P("store", "layer", None),
        P("layer", None, None),
        P("layer", None, None),
        P(),
        P("layer"),
        P(("parts", "store")),
        P("layer"),
    )
    sizes = tuple(mesh.shape[axis] for axis in AXES)
    return jax.shard_map(
        small if sizes == (PARTS, CHIPS * CORES, LAYERS) else general,
        mesh=mesh,
        in_specs=placed,
        out_specs=P("layer", ("parts", "store")),
        check_vma=False,
    )
```

```python
import functools

import jax
import jax.numpy as jnp
from jax import lax
from jax.experimental import pallas as pl
from jax.experimental.pallas import tpu as pltpu
from jax.sharding import PartitionSpec as P

AXES = ("parts", "store", "layer")
VMEM = pl.BlockSpec(memory_space=pltpu.VMEM)
SMEM = pl.BlockSpec(memory_space=pltpu.SMEM)
bf16, f32 = jnp.bfloat16, jnp.float32
LIMIT = 20 * 1024 * 1024


def preconditioned(query_grads, left_factor, right_factor):
    q_rows, slots, width = query_grads.shape
    side = left_factor.shape[1]
    mats = query_grads.astype(jnp.float32).reshape(q_rows, slots, side, side)
    half = jnp.einsum("lij,qljk->qlik", left_factor, mats, precision=lax.Precision.HIGHEST)
    full = jnp.einsum("qlik,lkm->qlim", half, right_factor, precision=lax.Precision.HIGHEST)
    return full.reshape(q_rows, slots, width).astype(jnp.bfloat16)


def general(
    train_grads,
    query_grads,
    left_factor,
    right_factor,
    layer_weight,
    layer_of,
    train_ids,
    query_ids,
):
    precond = preconditioned(query_grads, left_factor, right_factor)
    weight = jnp.take(layer_weight, layer_of[0])
    queries = lax.all_gather(precond, "store", axis=0, tiled=True)
    terms = weight * jnp.dot(
        queries[:, 0, :], train_grads[:, 0, :].T, preferred_element_type=jnp.float32
    )
    summed = lax.psum_scatter(terms, "layer", scatter_dimension=0, tiled=True)
    same = query_ids[:, None] == train_ids[None, :]
    return jnp.where(same, jnp.float32(0.0), summed)


PARTS, CHIPS, CORES, LAYERS = 2, 4, 2, 2
CHUNK = 16
HALF = 2 * CHUNK
STEP = 256
HBM = pl.BlockSpec(memory_space=pltpu.HBM)


def permute(value, name, target):
    pairs = []
    for p in range(PARTS):
        for z in range(CHIPS):
            for c in range(CORES):
                for l in range(LAYERS):
                    tp, tz, tc, tl = target(p, z, c, l)
                    source = ((p * CHIPS + z) * CORES + c) * LAYERS + l
                    pairs.append((source, ((tp * CHIPS + tz) * CORES + tc) * LAYERS + tl))
    with jax.named_scope(name):
        return lax.ppermute(value, AXES, pairs)


to_part = functools.partial(permute, target=lambda p, z, c, l: (1 - p, z, c, l))
to_core = functools.partial(permute, target=lambda p, z, c, l: (p, z, 1 - c, l))
to_layer = functools.partial(permute, target=lambda p, z, c, l: (p, z, c, 1 - l))
to_near = functools.partial(permute, target=lambda p, z, c, l: (p, z ^ 1, c, l))
to_far = functools.partial(permute, target=lambda p, z, c, l: (p, z ^ 3, c, l))


def after(value, *others):
    return lax.optimization_barrier((value, *others))[0]


def place():
    store = lax.axis_index("store")
    return lax.axis_index("parts"), store // CORES, store % CORES, lax.axis_index("layer")


def split(x, terms):
    out = []
    for _ in range(terms):
        term = x.astype(bf16)
        out.append(term)
        x = x - term.astype(f32)
    return out


def dot(a, b):
    return lax.dot_general(a, b, (((1,), (0,)), ((), ())), preferred_element_type=f32)


def iota(shape, dim):
    return lax.broadcasted_iota(jnp.int32, shape, dim)


def factors(left, right):
    r, c = iota((256, 64), 0), iota((256, 64), 1)
    pick = jnp.where(c == 4 * (r % 16) + (r // 16) % 4, 1.0, 0.0).astype(bf16)
    r, c = iota((64, 256), 0), iota((64, 256), 1)
    pick_t = jnp.where(r == 4 * (c % 16) + (c // 16) % 4, 1.0, 0.0).astype(bf16)
    block = iota((256, 256), 0) // 64 == iota((256, 256), 1) // 64
    lefts = [
        jnp.where(block, dot(dot(pick, term).astype(bf16), pick_t), 0.0).astype(bf16)
        for term in split(left, 2)
    ]
    row = jnp.concatenate([right, right], axis=1)
    tiled = jnp.concatenate([jnp.concatenate([row] * 4, axis=1)] * 4, axis=0)
    block = iota((256, 512), 0) // 64 == iota((256, 512), 1) // 128
    return lefts, split(jnp.where(block, tiled, 0.0), 2)


def precond_rows(q_ref, lefts, rights, out):
    for at in range(0, q_ref.shape[0], CHUNK):
        values = precond_chunk(q_ref[at : at + CHUNK, :], lefts, rights)
        for t, value in enumerate(values):
            out[at : at + CHUNK, t * 256 : (t + 1) * 256] = value


def precond_chunk(q, lefts, rights):
    tiles = q.shape[1] // 256
    r, c = iota((256, 256), 0), iota((256, 256), 1)
    swap = jnp.where((r // 16 == c % 16) & (r % 16 == c // 16), 1.0, 0.0).astype(bf16)
    x = jnp.concatenate([q[:, t * 256 : (t + 1) * 256] for t in range(tiles)], axis=0)
    x = dot(swap, x).astype(bf16)
    z = dot(x, rights[0]) + dot(x, rights[1])
    sets = []
    for first in range(0, 16, 4):
        rows = [
            z[query * 16 : (query + 1) * 16, s * 128 : (s + 1) * 128]
            for query in range(first, first + 4)
            for s in range(4)
        ]
        sets.append(jnp.concatenate(rows, axis=0))
    high, low = split(jnp.concatenate(sets, axis=1), 2)
    z = dot(lefts[0], high) + (dot(lefts[0], low) + dot(lefts[1], high))
    side = iota((16, 128), 1) < 64
    rows = []
    for first in range(4):
        for k in range(4):
            o = z[k * 64 : (k + 1) * 64, first * 128 : (first + 1) * 128]
            pair = [jnp.where(side, o[0:16], o[16:32]), jnp.where(side, o[32:48], o[48:64])]
            rows.append(jnp.concatenate(pair, axis=1))
    y = dot(swap, jnp.concatenate(rows, axis=0).astype(bf16)).astype(bf16)
    return [y[t * 16 : (t + 1) * 16] for t in range(tiles)]


def own_kernel(q_hbm, left_hbm, right_hbm, mine, lefts_ref, rights_ref, q_ref, left, right, sems):
    at = pl.multiple_of(lax.axis_index("parts") * HALF, HALF)
    copies = [
        pltpu.make_async_copy(source, target, sems.at[k])
        for k, (source, target) in enumerate(
            ((left_hbm, left), (right_hbm, right), (q_hbm.at[pl.ds(at, HALF), :], q_ref))
        )
    ]
    for copy in copies:
        copy.start()
    copies[0].wait()
    copies[1].wait()
    lefts, rights = factors(left[...], right[...])
    for k in range(2):
        lefts_ref[k] = lefts[k]
        rights_ref[k] = rights[k]
    copies[2].wait()
    precond_rows(q_ref, lefts, rights, mine)


def rest_kernel(
    weight_ref, layer_ref, q_hbm, train_hbm, lefts_ref, rights_ref, rest, train, weight, q_ref, sems
):
    at = pl.multiple_of((1 - lax.axis_index("parts")) * HALF, HALF)
    q_copy = pltpu.make_async_copy(q_hbm.at[pl.ds(at, HALF), :], q_ref, sems.at[0])
    q_copy.start()
    copies = []
    for k in range(train.shape[0] // STEP):
        here = pl.ds(k * STEP, STEP)
        copies.append(pltpu.make_async_copy(train_hbm.at[here, :], train.at[here, :], sems.at[1 + k]))
        copies[-1].start()
    weight[...] = jnp.full(weight.shape, weight_ref[layer_ref[0]])
    lefts, rights = [lefts_ref[0], lefts_ref[1]], [rights_ref[0], rights_ref[1]]
    q_copy.wait()
    precond_rows(q_ref, lefts, rights, rest)
    for copy in copies:
        copy.wait()


def score_kernel(weight_ref, train_ref, *refs, picks, stored, early, columns):
    inputs, refs = refs[: len(picks)], refs[len(picks) :]
    n_before = sum(taken for _, _, taken in early)
    before, outs = refs[:n_before], refs[n_before:]
    weight = weight_ref[0:1, :]
    queries = jnp.concatenate(
        [piece[at : at + n, :] for piece, rows in zip(inputs, picks) for at, n in rows], axis=0
    )
    _, z, _, layer = place()
    near_is_mine = z // 2 == layer
    for at in range(*columns, STEP):
        there, here = slice(at, at + STEP), slice(at - columns[0], at - columns[0] + STEP)
        value = lax.dot_general(
            train_ref[there, :], queries, (((1,), (1,)), ((), ())), preferred_element_type=f32
        )
        value = weight * value.T
        if stored:
            outs[0][:, here] = value[:stored]
        if early:
            send, keep = outs[-2:]
            old, given = [], list(before)
            for first, rows, taken in early:
                old.append(
                    given.pop(0)[first : first + rows, there] if taken else value[first : first + rows]
                )
            old, new = jnp.concatenate(old, axis=0), value[stored:]
            send[:, here] = jnp.where(near_is_mine, new, old).astype(send.dtype)
            keep[:, here] = jnp.where(near_is_mine, old, new)


def kernel_call(kernel, outs, inputs, specs=None, scratch=()):
    return pl.pallas_call(
        kernel,
        out_shape=outs,
        in_specs=specs or [VMEM] * len(inputs),
        out_specs=[VMEM] * len(outs) if isinstance(outs, list) else VMEM,
        scratch_shapes=scratch,
        compiler_params=pltpu.CompilerParams(vmem_limit_bytes=LIMIT),
    )(*inputs)


def call_scores(weight, train, inputs, stored=0, early=(), columns=None):
    columns = columns or (0, train.shape[0])
    n = columns[1] - columns[0]
    total = sum(count for _, rows in inputs for _, count in rows)
    others = [a for a, _ in inputs] + [a for a, _, _ in early if a is not None]
    outs = [jax.ShapeDtypeStruct((stored, n), f32)] if stored else []
    if early:
        outs += [jax.ShapeDtypeStruct((total - stored, n), t) for t in (bf16, f32)]
    return kernel_call(
        functools.partial(
            score_kernel,
            picks=[rows for _, rows in inputs],
            stored=stored,
            early=[(first, rows, a is not None) for a, first, rows in early],
            columns=columns,
        ),
        outs,
        [weight, train, *others],
    )


def final_kernel(train_ids, query_ids, *refs, groups, n_given):
    given, refs = refs[:n_given], refs[n_given:]
    *_, out, done, sems = refs
    part, z, core, layer = place()
    low = z % 2
    first = jnp.where(z // 2 == layer, low, 1 - low)
    copies = []
    for k, (which, keep, got, row, column) in enumerate(groups):
        block = first if which < 2 else 1 - first
        half = part if which % 2 == 0 else 1 - part
        keep, got = given[keep], given[got]
        columns = pl.ds(column, keep.shape[1])
        for i, c in enumerate((core, 1 - core)):
            at = pl.multiple_of(((block * 2 + c) * 2 + half) * HALF, HALF)
            here, j = slice(row + i * HALF, row + (i + 1) * HALF), 2 * k + i
            total = keep[here, :] + got[here, :].astype(f32)
            same = query_ids[pl.ds(at, HALF), :] == train_ids[:, columns]
            slot = done.at[j * HALF : (j + 1) * HALF, : keep.shape[1]]
            slot[...] = jnp.where(same, jnp.float32(0.0), total)
            copies.append(
                pltpu.make_async_copy(slot, out.at[pl.ds(at, HALF), columns], sems.at[j])
            )
            copies[-1].start()
    for copy in copies:
        copy.wait()


def call_final(train_ids, query_ids, given, groups, before=None):
    rows, n = query_ids.shape[0], train_ids.shape[1]
    inputs = [train_ids, query_ids, *given] + ([] if before is None else [before])
    return pl.pallas_call(
        functools.partial(final_kernel, groups=groups, n_given=len(given)),
        out_shape=jax.ShapeDtypeStruct((rows, n), f32),
        in_specs=[VMEM] * (2 + len(given)) + ([] if before is None else [HBM]),
        out_specs=HBM,
        scratch_shapes=[
            pltpu.VMEM((2 * len(groups) * HALF, max(a.shape[1] for a in given)), f32),
            pltpu.SemaphoreType.DMA((2 * len(groups),)),
        ],
        input_output_aliases={} if before is None else {len(inputs) - 1: 0},
        compiler_params=pltpu.CompilerParams(vmem_limit_bytes=LIMIT),
    )(*inputs)


def small(
    train_grads,
    query_grads,
    left_factor,
    right_factor,
    layer_weight,
    layer_of,
    train_ids,
    query_ids,
):
    in_hbm = lambda array: pltpu.with_memory_space_constraint(array, pltpu.HBM)
    train, queries = in_hbm(train_grads[:, 0, :]), in_hbm(query_grads[:, 0, :])
    width, side = queries.shape[1], left_factor.shape[1]
    shape = jax.ShapeDtypeStruct
    mine, lefts, rights = kernel_call(
        own_kernel,
        [shape((HALF, width), bf16), shape((2, 256, 256), bf16), shape((2, 256, 512), bf16)],
        [queries, in_hbm(left_factor[0]), in_hbm(right_factor[0])],
        [HBM] * 3,
        [
            pltpu.VMEM((HALF, width), bf16),
            pltpu.VMEM((side, side), f32),
            pltpu.VMEM((side, side), f32),
            pltpu.SemaphoreType.DMA((3,)),
        ],
    )
    near = to_near(mine, "near")
    far = to_far(mine, "far")
    rest, train, weight = kernel_call(
        rest_kernel,
        [shape((HALF, width), bf16), shape(train.shape, bf16), shape((8, STEP), f32)],
        [in_hbm(layer_weight), layer_of, queries, train, lefts, rights],
        [SMEM, SMEM, HBM, HBM, VMEM, VMEM],
        [pltpu.VMEM((HALF, width), bf16), pltpu.SemaphoreType.DMA((1 + train.shape[0] // STEP,))],
    )
    score = functools.partial(call_scores, weight, train)

    def rows_of(*pieces):
        return [(piece, ((0, piece.shape[0]),)) for piece in pieces]

    mine_x = to_core(mine, "mine_x")
    rest_x = to_core(rest, "rest_x")
    near_x = to_core(near, "near_x")
    near_p = to_part(near, "near_p")
    far = after(far, near)
    cross = to_near(far, "cross")
    far_p = to_part(far, "far_p")
    far_x = to_core(far, "far_x")
    rest_x = after(rest_x, far)
    (early0,) = score(rows_of(mine, mine_x, rest, rest_x), stored=128)
    near_p = after(near_p, early0)
    near_px = to_core(near_p, "near_px")

    far_px0 = to_core(far_p[:CHUNK], "far_px0")
    far_px1 = to_core(far_p[CHUNK:], "far_px1")
    cross_pa = to_part(after(cross[:CHUNK], far_x, near_x), "cross_pa")
    cross_pb = to_near(after(far_p[CHUNK:], far_x, near_x), "cross_pb")
    cross_x = to_core(cross, "cross_x")
    far_px1 = after(far_px1, cross)
    early1, send0, keep0 = score(
        rows_of(near, near_x, near_p, near_px, far, far_x, far_p, far_px0, far_px1),
        stored=128,
        early=[(early0, 0, 128)],
    )
    got0 = to_layer(send0, "got0")
    cross_pa, cross_pb = after(cross_pa, send0), after(cross_pb, send0)
    def by_columns(piece, name):
        parts = [to_core(part, name) for part in jnp.split(piece, 2, axis=1)]
        return jnp.concatenate(parts, axis=1)

    cross_pxa, cross_pxb = by_columns(cross_pa, "cross_pxa"), by_columns(cross_pb, "cross_pxb")
    last = rows_of(cross, cross_x, cross_pa, cross_pb, cross_pxa, cross_pxb)
    n = train.shape[0]
    cut = n * 3 // 4
    send1, keep1 = score(last, early=[(early1, 0, 128)], columns=(0, cut))
    got1 = to_layer(send1, "got1")
    early1 = after(early1, send1)
    send2, keep2 = score(last, early=[(early1, 0, 128)], columns=(cut, n))
    send2 = after(send2, got0)
    got2 = to_layer(send2, "got2")

    train_ids, query_ids = train_ids[None, :], query_ids[:, None]
    most = call_final(
        train_ids,
        query_ids,
        [keep0, got0, keep1, got1],
        ((0, 0, 1, 0, 0), (1, 0, 1, 64, 0), (2, 2, 3, 0, 0), (3, 2, 3, 64, 0)),
    )
    return call_final(
        train_ids, query_ids, [keep2, got2], ((2, 0, 1, 0, cut), (3, 0, 1, 64, cut)), most
    )


def solution(mesh):
    placed = (
        P(("parts", "store"), "layer", None),
        P("store", "layer", None),
        P("layer", None, None),
        P("layer", None, None),
        P(),
        P("layer"),
        P(("parts", "store")),
        P("layer"),
    )
    sizes = tuple(mesh.shape[axis] for axis in AXES)
    return jax.shard_map(
        small if sizes == (PARTS, CHIPS * CORES, LAYERS) else general,
        mesh=mesh,
        in_specs=placed,
        out_specs=P("layer", ("parts", "store")),
        check_vma=False,
    )
```

```python
import functools

import jax
import jax.numpy as jnp
from jax import lax
from jax.experimental import pallas as pl
from jax.experimental.pallas import tpu as pltpu
from jax.sharding import PartitionSpec as P

AXES = ("parts", "store", "layer")
VMEM = pl.BlockSpec(memory_space=pltpu.VMEM)
SMEM = pl.BlockSpec(memory_space=pltpu.SMEM)
bf16, f32 = jnp.bfloat16, jnp.float32
LIMIT = 20 * 1024 * 1024


def preconditioned(query_grads, left_factor, right_factor):
    q_rows, slots, width = query_grads.shape
    side = left_factor.shape[1]
    mats = query_grads.astype(jnp.float32).reshape(q_rows, slots, side, side)
    half = jnp.einsum("lij,qljk->qlik", left_factor, mats, precision=lax.Precision.HIGHEST)
    full = jnp.einsum("qlik,lkm->qlim", half, right_factor, precision=lax.Precision.HIGHEST)
    return full.reshape(q_rows, slots, width).astype(jnp.bfloat16)


def general(
    train_grads,
    query_grads,
    left_factor,
    right_factor,
    layer_weight,
    layer_of,
    train_ids,
    query_ids,
):
    precond = preconditioned(query_grads, left_factor, right_factor)
    weight = jnp.take(layer_weight, layer_of[0])
    queries = lax.all_gather(precond, "store", axis=0, tiled=True)
    terms = weight * jnp.dot(
        queries[:, 0, :], train_grads[:, 0, :].T, preferred_element_type=jnp.float32
    )
    summed = lax.psum_scatter(terms, "layer", scatter_dimension=0, tiled=True)
    same = query_ids[:, None] == train_ids[None, :]
    return jnp.where(same, jnp.float32(0.0), summed)


PARTS, CHIPS, CORES, LAYERS = 2, 4, 2, 2
CHUNK = 16
HALF = 2 * CHUNK
STEP = 256
HBM = pl.BlockSpec(memory_space=pltpu.HBM)


def permute(value, name, target):
    pairs = []
    for p in range(PARTS):
        for z in range(CHIPS):
            for c in range(CORES):
                for l in range(LAYERS):
                    tp, tz, tc, tl = target(p, z, c, l)
                    source = ((p * CHIPS + z) * CORES + c) * LAYERS + l
                    pairs.append((source, ((tp * CHIPS + tz) * CORES + tc) * LAYERS + tl))
    with jax.named_scope(name):
        return lax.ppermute(value, AXES, pairs)


to_part = functools.partial(permute, target=lambda p, z, c, l: (1 - p, z, c, l))
to_core = functools.partial(permute, target=lambda p, z, c, l: (p, z, 1 - c, l))
to_layer = functools.partial(permute, target=lambda p, z, c, l: (p, z, c, 1 - l))
to_near = functools.partial(permute, target=lambda p, z, c, l: (p, z ^ 1, c, l))
to_far = functools.partial(permute, target=lambda p, z, c, l: (p, z ^ 3, c, l))


def after(value, *others):
    return lax.optimization_barrier((value, *others))[0]


def place():
    store = lax.axis_index("store")
    return lax.axis_index("parts"), store // CORES, store % CORES, lax.axis_index("layer")


def split(x, terms):
    out = []
    for _ in range(terms):
        term = x.astype(bf16)
        out.append(term)
        x = x - term.astype(f32)
    return out


def dot(a, b):
    return lax.dot_general(a, b, (((1,), (0,)), ((), ())), preferred_element_type=f32)


def iota(shape, dim):
    return lax.broadcasted_iota(jnp.int32, shape, dim)


def factors(left, right):
    r, c = iota((256, 64), 0), iota((256, 64), 1)
    pick = jnp.where(c == 4 * (r % 16) + (r // 16) % 4, 1.0, 0.0).astype(bf16)
    r, c = iota((64, 256), 0), iota((64, 256), 1)
    pick_t = jnp.where(r == 4 * (c % 16) + (c // 16) % 4, 1.0, 0.0).astype(bf16)
    block = iota((256, 256), 0) // 64 == iota((256, 256), 1) // 64
    lefts = [
        jnp.where(block, dot(dot(pick, term).astype(bf16), pick_t), 0.0).astype(bf16)
        for term in split(left, 2)
    ]
    row = jnp.concatenate([right, right], axis=1)
    tiled = jnp.concatenate([jnp.concatenate([row] * 4, axis=1)] * 4, axis=0)
    block = iota((256, 512), 0) // 64 == iota((256, 512), 1) // 128
    return lefts, split(jnp.where(block, tiled, 0.0), 2)


def precond_rows(q_ref, lefts, rights, out):
    for at in range(0, q_ref.shape[0], CHUNK):
        values = precond_chunk(q_ref[at : at + CHUNK, :], lefts, rights)
        for t, value in enumerate(values):
            out[at : at + CHUNK, t * 256 : (t + 1) * 256] = value


def precond_chunk(q, lefts, rights):
    tiles = q.shape[1] // 256
    r, c = iota((256, 256), 0), iota((256, 256), 1)
    swap = jnp.where((r // 16 == c % 16) & (r % 16 == c // 16), 1.0, 0.0).astype(bf16)
    x = jnp.concatenate([q[:, t * 256 : (t + 1) * 256] for t in range(tiles)], axis=0)
    x = dot(swap, x).astype(bf16)
    z = dot(x, rights[0]) + dot(x, rights[1])
    sets = []
    for first in range(0, 16, 4):
        rows = [
            z[query * 16 : (query + 1) * 16, s * 128 : (s + 1) * 128]
            for query in range(first, first + 4)
            for s in range(4)
        ]
        sets.append(jnp.concatenate(rows, axis=0))
    high, low = split(jnp.concatenate(sets, axis=1), 2)
    z = dot(lefts[0], high) + (dot(lefts[0], low) + dot(lefts[1], high))
    side = iota((16, 128), 1) < 64
    rows = []
    for first in range(4):
        for k in range(4):
            o = z[k * 64 : (k + 1) * 64, first * 128 : (first + 1) * 128]
            pair = [jnp.where(side, o[0:16], o[16:32]), jnp.where(side, o[32:48], o[48:64])]
            rows.append(jnp.concatenate(pair, axis=1))
    y = dot(swap, jnp.concatenate(rows, axis=0).astype(bf16)).astype(bf16)
    return [y[t * 16 : (t + 1) * 16] for t in range(tiles)]


def own_kernel(q_hbm, left_hbm, right_hbm, mine, lefts_ref, rights_ref, q_ref, left, right, sems):
    at = pl.multiple_of(lax.axis_index("parts") * HALF, HALF)
    copies = [
        pltpu.make_async_copy(source, target, sems.at[k])
        for k, (source, target) in enumerate(
            ((left_hbm, left), (right_hbm, right), (q_hbm.at[pl.ds(at, HALF), :], q_ref))
        )
    ]
    for copy in copies:
        copy.start()
    copies[0].wait()
    copies[1].wait()
    lefts, rights = factors(left[...], right[...])
    for k in range(2):
        lefts_ref[k] = lefts[k]
        rights_ref[k] = rights[k]
    copies[2].wait()
    precond_rows(q_ref, lefts, rights, mine)


def rest_kernel(
    weight_ref, layer_ref, q_hbm, train_hbm, lefts_ref, rights_ref, rest, train, weight, q_ref, sems
):
    at = pl.multiple_of((1 - lax.axis_index("parts")) * HALF, HALF)
    q_copy = pltpu.make_async_copy(q_hbm.at[pl.ds(at, HALF), :], q_ref, sems.at[0])
    q_copy.start()
    copies = []
    for k in range(train.shape[0] // STEP):
        here = pl.ds(k * STEP, STEP)
        copies.append(pltpu.make_async_copy(train_hbm.at[here, :], train.at[here, :], sems.at[1 + k]))
        copies[-1].start()
    weight[...] = jnp.full(weight.shape, weight_ref[layer_ref[0]])
    lefts, rights = [lefts_ref[0], lefts_ref[1]], [rights_ref[0], rights_ref[1]]
    q_copy.wait()
    precond_rows(q_ref, lefts, rights, rest)
    for copy in copies:
        copy.wait()


def score_kernel(weight_ref, train_ref, *refs, picks, stored, early, columns):
    inputs, refs = refs[: len(picks)], refs[len(picks) :]
    n_before = sum(taken for _, _, taken in early)
    before, outs = refs[:n_before], refs[n_before:]
    weight = weight_ref[0:1, :]
    queries = jnp.concatenate(
        [piece[at : at + n, :] for piece, rows in zip(inputs, picks) for at, n in rows], axis=0
    )
    _, z, _, layer = place()
    near_is_mine = z // 2 == layer
    for at in range(*columns, STEP):
        there, here = slice(at, at + STEP), slice(at - columns[0], at - columns[0] + STEP)
        value = lax.dot_general(
            train_ref[there, :], queries, (((1,), (1,)), ((), ())), preferred_element_type=f32
        )
        value = weight * value.T
        if stored:
            outs[0][:, here] = value[:stored]
        if early:
            send, keep = outs[-2:]
            old, given = [], list(before)
            for first, rows, taken in early:
                old.append(
                    given.pop(0)[first : first + rows, there] if taken else value[first : first + rows]
                )
            old, new = jnp.concatenate(old, axis=0), value[stored:]
            send[:, here] = jnp.where(near_is_mine, new, old).astype(send.dtype)
            keep[:, here] = jnp.where(near_is_mine, old, new)


def kernel_call(kernel, outs, inputs, specs=None, scratch=()):
    return pl.pallas_call(
        kernel,
        out_shape=outs,
        in_specs=specs or [VMEM] * len(inputs),
        out_specs=[VMEM] * len(outs) if isinstance(outs, list) else VMEM,
        scratch_shapes=scratch,
        compiler_params=pltpu.CompilerParams(vmem_limit_bytes=LIMIT),
    )(*inputs)


def call_scores(weight, train, inputs, stored=0, early=(), columns=None):
    columns = columns or (0, train.shape[0])
    n = columns[1] - columns[0]
    total = sum(count for _, rows in inputs for _, count in rows)
    others = [a for a, _ in inputs] + [a for a, _, _ in early if a is not None]
    outs = [jax.ShapeDtypeStruct((stored, n), f32)] if stored else []
    if early:
        outs += [jax.ShapeDtypeStruct((total - stored, n), t) for t in (bf16, f32)]
    return kernel_call(
        functools.partial(
            score_kernel,
            picks=[rows for _, rows in inputs],
            stored=stored,
            early=[(first, rows, a is not None) for a, first, rows in early],
            columns=columns,
        ),
        outs,
        [weight, train, *others],
    )


def final_kernel(train_ids, query_ids, *refs, groups, n_given):
    given, refs = refs[:n_given], refs[n_given:]
    *_, out, done, sems = refs
    part, z, core, layer = place()
    low = z % 2
    first = jnp.where(z // 2 == layer, low, 1 - low)
    copies = []
    for k, (which, keep, got, row, column) in enumerate(groups):
        block = first if which < 2 else 1 - first
        half = part if which % 2 == 0 else 1 - part
        keep, got = given[keep], given[got]
        columns = pl.ds(column, keep.shape[1])
        for i, c in enumerate((core, 1 - core)):
            at = pl.multiple_of(((block * 2 + c) * 2 + half) * HALF, HALF)
            here, j = slice(row + i * HALF, row + (i + 1) * HALF), 2 * k + i
            total = keep[here, :] + got[here, :].astype(f32)
            same = query_ids[pl.ds(at, HALF), :] == train_ids[:, columns]
            slot = done.at[j * HALF : (j + 1) * HALF, : keep.shape[1]]
            slot[...] = jnp.where(same, jnp.float32(0.0), total)
            copies.append(
                pltpu.make_async_copy(slot, out.at[pl.ds(at, HALF), columns], sems.at[j])
            )
            copies[-1].start()
    for copy in copies:
        copy.wait()


def call_final(train_ids, query_ids, given, groups, before=None):
    rows, n = query_ids.shape[0], train_ids.shape[1]
    inputs = [train_ids, query_ids, *given] + ([] if before is None else [before])
    return pl.pallas_call(
        functools.partial(final_kernel, groups=groups, n_given=len(given)),
        out_shape=jax.ShapeDtypeStruct((rows, n), f32),
        in_specs=[VMEM] * (2 + len(given)) + ([] if before is None else [HBM]),
        out_specs=HBM,
        scratch_shapes=[
            pltpu.VMEM((2 * len(groups) * HALF, max(a.shape[1] for a in given)), f32),
            pltpu.SemaphoreType.DMA((2 * len(groups),)),
        ],
        input_output_aliases={} if before is None else {len(inputs) - 1: 0},
        compiler_params=pltpu.CompilerParams(vmem_limit_bytes=LIMIT),
    )(*inputs)


def small(
    train_grads,
    query_grads,
    left_factor,
    right_factor,
    layer_weight,
    layer_of,
    train_ids,
    query_ids,
):
    in_hbm = lambda array: pltpu.with_memory_space_constraint(array, pltpu.HBM)
    train, queries = in_hbm(train_grads[:, 0, :]), in_hbm(query_grads[:, 0, :])
    width, side = queries.shape[1], left_factor.shape[1]
    shape = jax.ShapeDtypeStruct
    mine, lefts, rights = kernel_call(
        own_kernel,
        [shape((HALF, width), bf16), shape((2, 256, 256), bf16), shape((2, 256, 512), bf16)],
        [queries, in_hbm(left_factor[0]), in_hbm(right_factor[0])],
        [HBM] * 3,
        [
            pltpu.VMEM((HALF, width), bf16),
            pltpu.VMEM((side, side), f32),
            pltpu.VMEM((side, side), f32),
            pltpu.SemaphoreType.DMA((3,)),
        ],
    )
    near = to_near(mine, "near")
    far = to_far(mine, "far")
    rest, train, weight = kernel_call(
        rest_kernel,
        [shape((HALF, width), bf16), shape(train.shape, bf16), shape((8, STEP), f32)],
        [in_hbm(layer_weight), layer_of, queries, train, lefts, rights],
        [SMEM, SMEM, HBM, HBM, VMEM, VMEM],
        [pltpu.VMEM((HALF, width), bf16), pltpu.SemaphoreType.DMA((1 + train.shape[0] // STEP,))],
    )
    score = functools.partial(call_scores, weight, train)

    def rows_of(*pieces):
        return [(piece, ((0, piece.shape[0]),)) for piece in pieces]

    mine_x = to_core(after(mine, rest), "mine_x")
    rest_x = to_core(rest, "rest_x")
    near = after(near, rest)
    near_x = to_core(near, "near_x")
    near_p = to_part(near, "near_p")
    far = after(far, near)
    cross = to_near(far, "cross")
    far_p = to_part(far, "far_p")
    far_x = to_core(after(far, rest_x), "far_x")
    mine_x = after(mine_x, far)
    (early0,) = score(rows_of(mine, mine_x, rest, rest_x), stored=128)
    send0, keep0 = score(rows_of(far, far_x), early=[(early0, 0, 64)])
    got0 = to_layer(send0, "got0")

    near_p = after(near_p, early0)
    near_px = to_core(near_p, "near_px")
    far_p, cross = after(far_p, near_px, send0), after(cross, send0)
    far_px = to_core(far_p, "far_px")
    cross_pa = to_part(cross[:CHUNK], "cross_pa")
    cross_pb = to_near(far_p[CHUNK:], "cross_pb")
    cross_x = to_core(cross, "cross_x")
    early1, send1, keep1 = score(
        rows_of(near, near_x, near_p, near_px, far_p, far_px, cross, cross_x),
        stored=128,
        early=[(early0, 64, 64), (None, 0, 64)],
    )
    got1 = to_layer(send1, "got1")
    cross_pa, cross_pb = after(cross_pa, send1, got0), after(cross_pb, send1, got0)
    cross_pxa = to_core(cross_pa, "cross_pxa")
    cross_pxb = to_core(cross_pb, "cross_pxb")
    last = rows_of(cross_pa, cross_pb, cross_pxa, cross_pxb)
    n = train.shape[0]
    cut = n // 2
    send2, keep2 = score(last, early=[(early1, 64, 64)], columns=(0, cut))
    got2 = to_layer(send2, "got2")
    early1 = after(early1, send2)
    send3, keep3 = score(last, early=[(early1, 64, 64)], columns=(cut, n))
    send3 = after(send3, got1)
    got3 = to_layer(send3, "got3")

    train_ids, query_ids = train_ids[None, :], query_ids[:, None]
    most = call_final(
        train_ids,
        query_ids,
        [keep0, got0, keep1, got1],
        ((0, 0, 1, 0, 0), (1, 2, 3, 0, 0), (2, 2, 3, 64, 0)),
    )
    return call_final(
        train_ids,
        query_ids,
        [keep2, got2, keep3, got3],
        ((3, 0, 1, 0, 0), (3, 2, 3, 0, cut)),
        most,
    )


def solution(mesh):
    placed = (
        P(("parts", "store"), "layer", None),
        P("store", "layer", None),
        P("layer", None, None),
        P("layer", None, None),
        P(),
        P("layer"),
        P(("parts", "store")),
        P("layer"),
    )
    sizes = tuple(mesh.shape[axis] for axis in AXES)
    return jax.shard_map(
        small if sizes == (PARTS, CHIPS * CORES, LAYERS) else general,
        mesh=mesh,
        in_specs=placed,
        out_specs=P("layer", ("parts", "store")),
        check_vma=False,
    )
```

```python
import functools

import jax
import jax.numpy as jnp
from jax import lax
from jax.experimental import pallas as pl
from jax.experimental.pallas import tpu as pltpu
from jax.sharding import PartitionSpec as P

AXES = ("parts", "store", "layer")
VMEM = pl.BlockSpec(memory_space=pltpu.VMEM)
SMEM = pl.BlockSpec(memory_space=pltpu.SMEM)
bf16, f32 = jnp.bfloat16, jnp.float32
LIMIT = 20 * 1024 * 1024


def preconditioned(query_grads, left_factor, right_factor):
    q_rows, slots, width = query_grads.shape
    side = left_factor.shape[1]
    mats = query_grads.astype(jnp.float32).reshape(q_rows, slots, side, side)
    half = jnp.einsum("lij,qljk->qlik", left_factor, mats, precision=lax.Precision.HIGHEST)
    full = jnp.einsum("qlik,lkm->qlim", half, right_factor, precision=lax.Precision.HIGHEST)
    return full.reshape(q_rows, slots, width).astype(jnp.bfloat16)


def general(
    train_grads,
    query_grads,
    left_factor,
    right_factor,
    layer_weight,
    layer_of,
    train_ids,
    query_ids,
):
    precond = preconditioned(query_grads, left_factor, right_factor)
    weight = jnp.take(layer_weight, layer_of[0])
    queries = lax.all_gather(precond, "store", axis=0, tiled=True)
    terms = weight * jnp.dot(
        queries[:, 0, :], train_grads[:, 0, :].T, preferred_element_type=jnp.float32
    )
    summed = lax.psum_scatter(terms, "layer", scatter_dimension=0, tiled=True)
    same = query_ids[:, None] == train_ids[None, :]
    return jnp.where(same, jnp.float32(0.0), summed)


PARTS, CHIPS, CORES, LAYERS = 2, 4, 2, 2
CHUNK = 16
HALF = 2 * CHUNK
STEP = 256
HBM = pl.BlockSpec(memory_space=pltpu.HBM)


def permute(value, name, target):
    pairs = []
    for p in range(PARTS):
        for z in range(CHIPS):
            for c in range(CORES):
                for l in range(LAYERS):
                    tp, tz, tc, tl = target(p, z, c, l)
                    source = ((p * CHIPS + z) * CORES + c) * LAYERS + l
                    pairs.append((source, ((tp * CHIPS + tz) * CORES + tc) * LAYERS + tl))
    with jax.named_scope(name):
        return lax.ppermute(value, AXES, pairs)


to_part = functools.partial(permute, target=lambda p, z, c, l: (1 - p, z, c, l))
to_core = functools.partial(permute, target=lambda p, z, c, l: (p, z, 1 - c, l))
to_layer = functools.partial(permute, target=lambda p, z, c, l: (p, z, c, 1 - l))
to_near = functools.partial(permute, target=lambda p, z, c, l: (p, z ^ 1, c, l))
to_far = functools.partial(permute, target=lambda p, z, c, l: (p, z ^ 3, c, l))


def after(value, *others):
    return lax.optimization_barrier((value, *others))[0]


def place():
    store = lax.axis_index("store")
    return lax.axis_index("parts"), store // CORES, store % CORES, lax.axis_index("layer")


def split(x, terms):
    out = []
    for _ in range(terms):
        term = x.astype(bf16)
        out.append(term)
        x = x - term.astype(f32)
    return out


def dot(a, b):
    return lax.dot_general(a, b, (((1,), (0,)), ((), ())), preferred_element_type=f32)


def iota(shape, dim):
    return lax.broadcasted_iota(jnp.int32, shape, dim)


def factors(left, right):
    r, c = iota((256, 64), 0), iota((256, 64), 1)
    pick = jnp.where(c == 4 * (r % 16) + (r // 16) % 4, 1.0, 0.0).astype(bf16)
    r, c = iota((64, 256), 0), iota((64, 256), 1)
    pick_t = jnp.where(r == 4 * (c % 16) + (c // 16) % 4, 1.0, 0.0).astype(bf16)
    block = iota((256, 256), 0) // 64 == iota((256, 256), 1) // 64
    lefts = [
        jnp.where(block, dot(dot(pick, term).astype(bf16), pick_t), 0.0).astype(bf16)
        for term in split(left, 2)
    ]
    row = jnp.concatenate([right, right], axis=1)
    tiled = jnp.concatenate([jnp.concatenate([row] * 4, axis=1)] * 4, axis=0)
    block = iota((256, 512), 0) // 64 == iota((256, 512), 1) // 128
    return lefts, split(jnp.where(block, tiled, 0.0), 2)


def precond_rows(q_ref, lefts, rights, out):
    for at in range(0, q_ref.shape[0], CHUNK):
        values = precond_chunk(q_ref[at : at + CHUNK, :], lefts, rights)
        for t, value in enumerate(values):
            out[at : at + CHUNK, t * 256 : (t + 1) * 256] = value


def precond_chunk(q, lefts, rights):
    tiles = q.shape[1] // 256
    r, c = iota((256, 256), 0), iota((256, 256), 1)
    swap = jnp.where((r // 16 == c % 16) & (r % 16 == c // 16), 1.0, 0.0).astype(bf16)
    x = jnp.concatenate([q[:, t * 256 : (t + 1) * 256] for t in range(tiles)], axis=0)
    x = dot(swap, x).astype(bf16)
    z = dot(x, rights[0]) + dot(x, rights[1])
    sets = []
    for first in range(0, 16, 4):
        rows = [
            z[query * 16 : (query + 1) * 16, s * 128 : (s + 1) * 128]
            for query in range(first, first + 4)
            for s in range(4)
        ]
        sets.append(jnp.concatenate(rows, axis=0))
    high, low = split(jnp.concatenate(sets, axis=1), 2)
    z = dot(lefts[0], high) + (dot(lefts[0], low) + dot(lefts[1], high))
    side = iota((16, 128), 1) < 64
    rows = []
    for first in range(4):
        for k in range(4):
            o = z[k * 64 : (k + 1) * 64, first * 128 : (first + 1) * 128]
            pair = [jnp.where(side, o[0:16], o[16:32]), jnp.where(side, o[32:48], o[48:64])]
            rows.append(jnp.concatenate(pair, axis=1))
    y = dot(swap, jnp.concatenate(rows, axis=0).astype(bf16)).astype(bf16)
    return [y[t * 16 : (t + 1) * 16] for t in range(tiles)]


def own_kernel(q_hbm, left_hbm, right_hbm, mine, lefts_ref, rights_ref, q_ref, left, right, sems):
    at = pl.multiple_of(lax.axis_index("parts") * HALF, HALF)
    copies = [
        pltpu.make_async_copy(source, target, sems.at[k])
        for k, (source, target) in enumerate(
            ((left_hbm, left), (right_hbm, right), (q_hbm.at[pl.ds(at, HALF), :], q_ref))
        )
    ]
    for copy in copies:
        copy.start()
    copies[0].wait()
    copies[1].wait()
    lefts, rights = factors(left[...], right[...])
    for k in range(2):
        lefts_ref[k] = lefts[k]
        rights_ref[k] = rights[k]
    copies[2].wait()
    precond_rows(q_ref, lefts, rights, mine)


def rest_kernel(
    weight_ref, layer_ref, q_hbm, train_hbm, lefts_ref, rights_ref, rest, train, weight, q_ref, sems
):
    at = pl.multiple_of((1 - lax.axis_index("parts")) * HALF, HALF)
    q_copy = pltpu.make_async_copy(q_hbm.at[pl.ds(at, HALF), :], q_ref, sems.at[0])
    q_copy.start()
    copies = []
    for k in range(train.shape[0] // STEP):
        here = pl.ds(k * STEP, STEP)
        copies.append(pltpu.make_async_copy(train_hbm.at[here, :], train.at[here, :], sems.at[1 + k]))
        copies[-1].start()
    weight[...] = jnp.full(weight.shape, weight_ref[layer_ref[0]])
    lefts, rights = [lefts_ref[0], lefts_ref[1]], [rights_ref[0], rights_ref[1]]
    q_copy.wait()
    precond_rows(q_ref, lefts, rights, rest)
    for copy in copies:
        copy.wait()


def score_kernel(weight_ref, train_ref, *refs, picks, stored, early, columns):
    inputs, refs = refs[: len(picks)], refs[len(picks) :]
    n_before = sum(taken for _, _, taken in early)
    before, outs = refs[:n_before], refs[n_before:]
    weight = weight_ref[0:1, :]
    queries = jnp.concatenate(
        [piece[at : at + n, :] for piece, rows in zip(inputs, picks) for at, n in rows], axis=0
    )
    _, z, _, layer = place()
    near_is_mine = z // 2 == layer
    for at in range(*columns, STEP):
        there, here = slice(at, at + STEP), slice(at - columns[0], at - columns[0] + STEP)
        value = lax.dot_general(
            train_ref[there, :], queries, (((1,), (1,)), ((), ())), preferred_element_type=f32
        )
        value = weight * value.T
        if stored:
            outs[0][:, here] = value[:stored]
        if early:
            send, keep = outs[-2:]
            old, given = [], list(before)
            for first, rows, taken in early:
                old.append(
                    given.pop(0)[first : first + rows, there] if taken else value[first : first + rows]
                )
            old, new = jnp.concatenate(old, axis=0), value[stored:]
            send[:, here] = jnp.where(near_is_mine, new, old).astype(send.dtype)
            keep[:, here] = jnp.where(near_is_mine, old, new)


def kernel_call(kernel, outs, inputs, specs=None, scratch=()):
    return pl.pallas_call(
        kernel,
        out_shape=outs,
        in_specs=specs or [VMEM] * len(inputs),
        out_specs=[VMEM] * len(outs) if isinstance(outs, list) else VMEM,
        scratch_shapes=scratch,
        compiler_params=pltpu.CompilerParams(vmem_limit_bytes=LIMIT),
    )(*inputs)


def call_scores(weight, train, inputs, stored=0, early=(), columns=None):
    columns = columns or (0, train.shape[0])
    n = columns[1] - columns[0]
    total = sum(count for _, rows in inputs for _, count in rows)
    others = [a for a, _ in inputs] + [a for a, _, _ in early if a is not None]
    outs = [jax.ShapeDtypeStruct((stored, n), f32)] if stored else []
    if early:
        outs += [jax.ShapeDtypeStruct((total - stored, n), t) for t in (bf16, f32)]
    return kernel_call(
        functools.partial(
            score_kernel,
            picks=[rows for _, rows in inputs],
            stored=stored,
            early=[(first, rows, a is not None) for a, first, rows in early],
            columns=columns,
        ),
        outs,
        [weight, train, *others],
    )


def final_kernel(train_ids, query_ids, *refs, groups, n_given):
    given, refs = refs[:n_given], refs[n_given:]
    *_, out, done, sems = refs
    part, z, core, layer = place()
    low = z % 2
    first = jnp.where(z // 2 == layer, low, 1 - low)
    copies = []
    for k, (which, keep, got, row, column) in enumerate(groups):
        block = first if which < 2 else 1 - first
        half = part if which % 2 == 0 else 1 - part
        keep, got = given[keep], given[got]
        columns = pl.ds(column, keep.shape[1])
        for i, c in enumerate((core, 1 - core)):
            at = pl.multiple_of(((block * 2 + c) * 2 + half) * HALF, HALF)
            here, j = slice(row + i * HALF, row + (i + 1) * HALF), 2 * k + i
            total = keep[here, :] + got[here, :].astype(f32)
            same = query_ids[pl.ds(at, HALF), :] == train_ids[:, columns]
            slot = done.at[j * HALF : (j + 1) * HALF, : keep.shape[1]]
            slot[...] = jnp.where(same, jnp.float32(0.0), total)
            copies.append(
                pltpu.make_async_copy(slot, out.at[pl.ds(at, HALF), columns], sems.at[j])
            )
            copies[-1].start()
    for copy in copies:
        copy.wait()


def call_final(train_ids, query_ids, given, groups, before=None):
    rows, n = query_ids.shape[0], train_ids.shape[1]
    inputs = [train_ids, query_ids, *given] + ([] if before is None else [before])
    return pl.pallas_call(
        functools.partial(final_kernel, groups=groups, n_given=len(given)),
        out_shape=jax.ShapeDtypeStruct((rows, n), f32),
        in_specs=[VMEM] * (2 + len(given)) + ([] if before is None else [HBM]),
        out_specs=HBM,
        scratch_shapes=[
            pltpu.VMEM((2 * len(groups) * HALF, max(a.shape[1] for a in given)), f32),
            pltpu.SemaphoreType.DMA((2 * len(groups),)),
        ],
        input_output_aliases={} if before is None else {len(inputs) - 1: 0},
        compiler_params=pltpu.CompilerParams(vmem_limit_bytes=LIMIT),
    )(*inputs)


def small(
    train_grads,
    query_grads,
    left_factor,
    right_factor,
    layer_weight,
    layer_of,
    train_ids,
    query_ids,
):
    in_hbm = lambda array: pltpu.with_memory_space_constraint(array, pltpu.HBM)
    train, queries = in_hbm(train_grads[:, 0, :]), in_hbm(query_grads[:, 0, :])
    width, side = queries.shape[1], left_factor.shape[1]
    shape = jax.ShapeDtypeStruct
    mine, lefts, rights = kernel_call(
        own_kernel,
        [shape((HALF, width), bf16), shape((2, 256, 256), bf16), shape((2, 256, 512), bf16)],
        [queries, in_hbm(left_factor[0]), in_hbm(right_factor[0])],
        [HBM] * 3,
        [
            pltpu.VMEM((HALF, width), bf16),
            pltpu.VMEM((side, side), f32),
            pltpu.VMEM((side, side), f32),
            pltpu.SemaphoreType.DMA((3,)),
        ],
    )
    near = to_near(mine, "near")
    far = to_far(mine, "far")
    rest, train, weight = kernel_call(
        rest_kernel,
        [shape((HALF, width), bf16), shape(train.shape, bf16), shape((8, STEP), f32)],
        [in_hbm(layer_weight), layer_of, queries, train, lefts, rights],
        [SMEM, SMEM, HBM, HBM, VMEM, VMEM],
        [pltpu.VMEM((HALF, width), bf16), pltpu.SemaphoreType.DMA((1 + train.shape[0] // STEP,))],
    )
    score = functools.partial(call_scores, weight, train)

    def rows_of(*pieces):
        return [(piece, ((0, piece.shape[0]),)) for piece in pieces]

    mine_x = to_core(after(mine, rest), "mine_x")
    rest_x = to_core(rest, "rest_x")
    near = after(near, rest)
    near_x = to_core(near, "near_x")
    near_p = to_part(near, "near_p")
    far = after(far, near)
    cross = to_near(far, "cross")
    far_p = to_part(far, "far_p")
    far_x = to_core(after(far, rest_x), "far_x")
    mine_x = after(mine_x, far)
    (early0,) = score(rows_of(mine, mine_x, rest, rest_x), stored=128)
    send0, keep0 = score(rows_of(far, far_x), early=[(early0, 0, 64)])
    got0 = to_layer(send0, "got0")

    near_p = after(near_p, early0)
    near_px = to_core(near_p, "near_px")
    far_p, cross = after(far_p, near_px, send0), after(cross, send0)
    far_px = to_core(far_p, "far_px")
    cross_pa = to_part(cross[:CHUNK], "cross_pa")
    cross_pb = to_near(far_p[CHUNK:], "cross_pb")
    cross_x = to_core(cross, "cross_x")
    early1, send1, keep1 = score(
        rows_of(near, near_x, near_p, near_px, far_p, far_px, cross, cross_x),
        stored=128,
        early=[(early0, 64, 64), (None, 0, 64)],
    )
    got1 = to_layer(send1, "got1")
    cross_pa, cross_pb = after(cross_pa, send1, got0), after(cross_pb, send1, got0)
    cross_pxa = to_core(cross_pa, "cross_pxa")
    cross_pxb = to_core(cross_pb, "cross_pxb")
    last = rows_of(cross_pa, cross_pb, cross_pxa, cross_pxb)
    send2, keep2 = score(last, early=[(early1, 64, 64)])
    got2 = to_layer(send2, "got2")

    train_ids, query_ids = train_ids[None, :], query_ids[:, None]
    most = call_final(
        train_ids,
        query_ids,
        [keep0, got0, keep1, got1],
        ((0, 0, 1, 0, 0), (1, 2, 3, 0, 0), (2, 2, 3, 64, 0)),
    )
    return call_final(
        train_ids,
        query_ids,
        [keep2, got2],
        ((3, 0, 1, 0, 0),),
        most,
    )


def solution(mesh):
    placed = (
        P(("parts", "store"), "layer", None),
        P("store", "layer", None),
        P("layer", None, None),
        P("layer", None, None),
        P(),
        P("layer"),
        P(("parts", "store")),
        P("layer"),
    )
    sizes = tuple(mesh.shape[axis] for axis in AXES)
    return jax.shard_map(
        small if sizes == (PARTS, CHIPS * CORES, LAYERS) else general,
        mesh=mesh,
        in_specs=placed,
        out_specs=P("layer", ("parts", "store")),
        check_vma=False,
    )
```

```python
import functools

import jax
import jax.numpy as jnp
from jax import lax
from jax.experimental import pallas as pl
from jax.experimental.pallas import tpu as pltpu
from jax.sharding import PartitionSpec as P

AXES = ("parts", "store", "layer")
VMEM = pl.BlockSpec(memory_space=pltpu.VMEM)
SMEM = pl.BlockSpec(memory_space=pltpu.SMEM)
bf16, f32 = jnp.bfloat16, jnp.float32
LIMIT = 20 * 1024 * 1024


def preconditioned(query_grads, left_factor, right_factor):
    q_rows, slots, width = query_grads.shape
    side = left_factor.shape[1]
    mats = query_grads.astype(jnp.float32).reshape(q_rows, slots, side, side)
    half = jnp.einsum("lij,qljk->qlik", left_factor, mats, precision=lax.Precision.HIGHEST)
    full = jnp.einsum("qlik,lkm->qlim", half, right_factor, precision=lax.Precision.HIGHEST)
    return full.reshape(q_rows, slots, width).astype(jnp.bfloat16)


def general(
    train_grads,
    query_grads,
    left_factor,
    right_factor,
    layer_weight,
    layer_of,
    train_ids,
    query_ids,
):
    precond = preconditioned(query_grads, left_factor, right_factor)
    weight = jnp.take(layer_weight, layer_of[0])
    queries = lax.all_gather(precond, "store", axis=0, tiled=True)
    terms = weight * jnp.dot(
        queries[:, 0, :], train_grads[:, 0, :].T, preferred_element_type=jnp.float32
    )
    summed = lax.psum_scatter(terms, "layer", scatter_dimension=0, tiled=True)
    same = query_ids[:, None] == train_ids[None, :]
    return jnp.where(same, jnp.float32(0.0), summed)


PARTS, CHIPS, CORES, LAYERS = 2, 4, 2, 2
CHUNK = 16
HALF = 2 * CHUNK
STEP = 256
HBM = pl.BlockSpec(memory_space=pltpu.HBM)


def permute(value, name, target):
    pairs = []
    for p in range(PARTS):
        for z in range(CHIPS):
            for c in range(CORES):
                for l in range(LAYERS):
                    tp, tz, tc, tl = target(p, z, c, l)
                    source = ((p * CHIPS + z) * CORES + c) * LAYERS + l
                    pairs.append((source, ((tp * CHIPS + tz) * CORES + tc) * LAYERS + tl))
    with jax.named_scope(name):
        return lax.ppermute(value, AXES, pairs)


to_part = functools.partial(permute, target=lambda p, z, c, l: (1 - p, z, c, l))
to_core = functools.partial(permute, target=lambda p, z, c, l: (p, z, 1 - c, l))
to_layer = functools.partial(permute, target=lambda p, z, c, l: (p, z, c, 1 - l))
to_near = functools.partial(permute, target=lambda p, z, c, l: (p, z ^ 1, c, l))
to_far = functools.partial(permute, target=lambda p, z, c, l: (p, z ^ 3, c, l))


def after(value, *others):
    return lax.optimization_barrier((value, *others))[0]


def place():
    store = lax.axis_index("store")
    return lax.axis_index("parts"), store // CORES, store % CORES, lax.axis_index("layer")


def split(x, terms):
    out = []
    for _ in range(terms):
        term = x.astype(bf16)
        out.append(term)
        x = x - term.astype(f32)
    return out


def dot(a, b):
    return lax.dot_general(a, b, (((1,), (0,)), ((), ())), preferred_element_type=f32)


def iota(shape, dim):
    return lax.broadcasted_iota(jnp.int32, shape, dim)


def factors(left, right):
    r, c = iota((256, 64), 0), iota((256, 64), 1)
    pick = jnp.where(c == 4 * (r % 16) + (r // 16) % 4, 1.0, 0.0).astype(bf16)
    r, c = iota((64, 256), 0), iota((64, 256), 1)
    pick_t = jnp.where(r == 4 * (c % 16) + (c // 16) % 4, 1.0, 0.0).astype(bf16)
    block = iota((256, 256), 0) // 64 == iota((256, 256), 1) // 64
    lefts = [
        jnp.where(block, dot(dot(pick, term).astype(bf16), pick_t), 0.0).astype(bf16)
        for term in split(left, 2)
    ]
    row = jnp.concatenate([right, right], axis=1)
    tiled = jnp.concatenate([jnp.concatenate([row] * 4, axis=1)] * 4, axis=0)
    block = iota((256, 512), 0) // 64 == iota((256, 512), 1) // 128
    return lefts, split(jnp.where(block, tiled, 0.0), 2)


def precond_rows(q_ref, lefts, rights, out):
    for at in range(0, q_ref.shape[0], CHUNK):
        values = precond_chunk(q_ref[at : at + CHUNK, :], lefts, rights)
        for t, value in enumerate(values):
            out[at : at + CHUNK, t * 256 : (t + 1) * 256] = value


def precond_chunk(q, lefts, rights):
    tiles = q.shape[1] // 256
    r, c = iota((256, 256), 0), iota((256, 256), 1)
    swap = jnp.where((r // 16 == c % 16) & (r % 16 == c // 16), 1.0, 0.0).astype(bf16)
    x = jnp.concatenate([q[:, t * 256 : (t + 1) * 256] for t in range(tiles)], axis=0)
    x = dot(swap, x).astype(bf16)
    z = dot(x, rights[0]) + dot(x, rights[1])
    sets = []
    for first in range(0, 16, 4):
        rows = [
            z[query * 16 : (query + 1) * 16, s * 128 : (s + 1) * 128]
            for query in range(first, first + 4)
            for s in range(4)
        ]
        sets.append(jnp.concatenate(rows, axis=0))
    high, low = split(jnp.concatenate(sets, axis=1), 2)
    z = dot(lefts[0], high) + (dot(lefts[0], low) + dot(lefts[1], high))
    side = iota((16, 128), 1) < 64
    rows = []
    for first in range(4):
        for k in range(4):
            o = z[k * 64 : (k + 1) * 64, first * 128 : (first + 1) * 128]
            pair = [jnp.where(side, o[0:16], o[16:32]), jnp.where(side, o[32:48], o[48:64])]
            rows.append(jnp.concatenate(pair, axis=1))
    y = dot(swap, jnp.concatenate(rows, axis=0).astype(bf16)).astype(bf16)
    return [y[t * 16 : (t + 1) * 16] for t in range(tiles)]


def own_kernel(q_hbm, left_hbm, right_hbm, mine, lefts_ref, rights_ref, q_ref, left, right, sems):
    at = pl.multiple_of(lax.axis_index("parts") * HALF, HALF)
    copies = [
        pltpu.make_async_copy(source, target, sems.at[k])
        for k, (source, target) in enumerate(
            ((left_hbm, left), (right_hbm, right), (q_hbm.at[pl.ds(at, HALF), :], q_ref))
        )
    ]
    for copy in copies:
        copy.start()
    copies[0].wait()
    copies[1].wait()
    lefts, rights = factors(left[...], right[...])
    for k in range(2):
        lefts_ref[k] = lefts[k]
        rights_ref[k] = rights[k]
    copies[2].wait()
    precond_rows(q_ref, lefts, rights, mine)


def rest_kernel(
    weight_ref, layer_ref, q_hbm, train_hbm, lefts_ref, rights_ref, rest, train, weight, q_ref, sems
):
    at = pl.multiple_of((1 - lax.axis_index("parts")) * HALF, HALF)
    q_copy = pltpu.make_async_copy(q_hbm.at[pl.ds(at, HALF), :], q_ref, sems.at[0])
    q_copy.start()
    copies = []
    for k in range(train.shape[0] // STEP):
        here = pl.ds(k * STEP, STEP)
        copies.append(pltpu.make_async_copy(train_hbm.at[here, :], train.at[here, :], sems.at[1 + k]))
        copies[-1].start()
    weight[...] = jnp.full(weight.shape, weight_ref[layer_ref[0]])
    lefts, rights = [lefts_ref[0], lefts_ref[1]], [rights_ref[0], rights_ref[1]]
    q_copy.wait()
    precond_rows(q_ref, lefts, rights, rest)
    for copy in copies:
        copy.wait()


def score_kernel(weight_ref, train_ref, *refs, picks, stored, early, columns):
    inputs, refs = refs[: len(picks)], refs[len(picks) :]
    n_before = sum(taken for _, _, taken in early)
    before, outs = refs[:n_before], refs[n_before:]
    weight = weight_ref[0:1, :]
    queries = jnp.concatenate(
        [piece[at : at + n, :] for piece, rows in zip(inputs, picks) for at, n in rows], axis=0
    )
    _, z, _, layer = place()
    near_is_mine = z // 2 == layer
    for at in range(*columns, STEP):
        there, here = slice(at, at + STEP), slice(at - columns[0], at - columns[0] + STEP)
        value = lax.dot_general(
            train_ref[there, :], queries, (((1,), (1,)), ((), ())), preferred_element_type=f32
        )
        value = weight * value.T
        if stored:
            outs[0][:, here] = value[:stored]
        if early:
            send, keep = outs[-2:]
            old, given = [], list(before)
            for first, rows, taken in early:
                old.append(
                    given.pop(0)[first : first + rows, there] if taken else value[first : first + rows]
                )
            old, new = jnp.concatenate(old, axis=0), value[stored:]
            send[:, here] = jnp.where(near_is_mine, new, old).astype(send.dtype)
            keep[:, here] = jnp.where(near_is_mine, old, new)


def kernel_call(kernel, outs, inputs, specs=None, scratch=()):
    return pl.pallas_call(
        kernel,
        out_shape=outs,
        in_specs=specs or [VMEM] * len(inputs),
        out_specs=[VMEM] * len(outs) if isinstance(outs, list) else VMEM,
        scratch_shapes=scratch,
        compiler_params=pltpu.CompilerParams(vmem_limit_bytes=LIMIT),
    )(*inputs)


def call_scores(weight, train, inputs, stored=0, early=(), columns=None):
    columns = columns or (0, train.shape[0])
    n = columns[1] - columns[0]
    total = sum(count for _, rows in inputs for _, count in rows)
    others = [a for a, _ in inputs] + [a for a, _, _ in early if a is not None]
    outs = [jax.ShapeDtypeStruct((stored, n), f32)] if stored else []
    if early:
        outs += [jax.ShapeDtypeStruct((total - stored, n), t) for t in (bf16, f32)]
    return kernel_call(
        functools.partial(
            score_kernel,
            picks=[rows for _, rows in inputs],
            stored=stored,
            early=[(first, rows, a is not None) for a, first, rows in early],
            columns=columns,
        ),
        outs,
        [weight, train, *others],
    )


def final_kernel(train_ids, query_ids, *refs, groups, n_given):
    given, refs = refs[:n_given], refs[n_given:]
    *_, out, done, sems = refs
    part, z, core, layer = place()
    low = z % 2
    first = jnp.where(z // 2 == layer, low, 1 - low)
    copies = []
    for k, (which, keep, got, row, column) in enumerate(groups):
        block = first if which < 2 else 1 - first
        half = part if which % 2 == 0 else 1 - part
        keep, got = given[keep], given[got]
        columns = pl.ds(column, keep.shape[1])
        for i, c in enumerate((core, 1 - core)):
            at = pl.multiple_of(((block * 2 + c) * 2 + half) * HALF, HALF)
            here, j = slice(row + i * HALF, row + (i + 1) * HALF), 2 * k + i
            total = keep[here, :] + got[here, :].astype(f32)
            same = query_ids[pl.ds(at, HALF), :] == train_ids[:, columns]
            slot = done.at[j * HALF : (j + 1) * HALF, : keep.shape[1]]
            slot[...] = jnp.where(same, jnp.float32(0.0), total)
            copies.append(
                pltpu.make_async_copy(slot, out.at[pl.ds(at, HALF), columns], sems.at[j])
            )
            copies[-1].start()
    for copy in copies:
        copy.wait()


def call_final(train_ids, query_ids, given, groups, before=None):
    rows, n = query_ids.shape[0], train_ids.shape[1]
    inputs = [train_ids, query_ids, *given] + ([] if before is None else [before])
    return pl.pallas_call(
        functools.partial(final_kernel, groups=groups, n_given=len(given)),
        out_shape=jax.ShapeDtypeStruct((rows, n), f32),
        in_specs=[VMEM] * (2 + len(given)) + ([] if before is None else [HBM]),
        out_specs=HBM,
        scratch_shapes=[
            pltpu.VMEM((2 * len(groups) * HALF, max(a.shape[1] for a in given)), f32),
            pltpu.SemaphoreType.DMA((2 * len(groups),)),
        ],
        input_output_aliases={} if before is None else {len(inputs) - 1: 0},
        compiler_params=pltpu.CompilerParams(vmem_limit_bytes=LIMIT),
    )(*inputs)


def small(
    train_grads,
    query_grads,
    left_factor,
    right_factor,
    layer_weight,
    layer_of,
    train_ids,
    query_ids,
):
    in_hbm = lambda array: pltpu.with_memory_space_constraint(array, pltpu.HBM)
    train, queries = in_hbm(train_grads[:, 0, :]), in_hbm(query_grads[:, 0, :])
    width, side = queries.shape[1], left_factor.shape[1]
    shape = jax.ShapeDtypeStruct
    mine, lefts, rights = kernel_call(
        own_kernel,
        [shape((HALF, width), bf16), shape((2, 256, 256), bf16), shape((2, 256, 512), bf16)],
        [queries, in_hbm(left_factor[0]), in_hbm(right_factor[0])],
        [HBM] * 3,
        [
            pltpu.VMEM((HALF, width), bf16),
            pltpu.VMEM((side, side), f32),
            pltpu.VMEM((side, side), f32),
            pltpu.SemaphoreType.DMA((3,)),
        ],
    )
    near = to_near(mine, "near")
    far = to_far(mine, "far")
    rest, train, weight = kernel_call(
        rest_kernel,
        [shape((HALF, width), bf16), shape(train.shape, bf16), shape((8, STEP), f32)],
        [in_hbm(layer_weight), layer_of, queries, train, lefts, rights],
        [SMEM, SMEM, HBM, HBM, VMEM, VMEM],
        [pltpu.VMEM((HALF, width), bf16), pltpu.SemaphoreType.DMA((1 + train.shape[0] // STEP,))],
    )
    score = functools.partial(call_scores, weight, train)

    def rows_of(*pieces):
        return [(piece, ((0, piece.shape[0]),)) for piece in pieces]

    mine_x = to_core(after(mine, rest), "mine_x")
    rest_x = to_core(rest, "rest_x")
    near = after(near, rest)
    near_x = to_core(near, "near_x")
    near_p = to_part(near, "near_p")
    far = after(far, near)
    cross = to_near(far, "cross")
    far_p = to_part(far, "far_p")
    far_x = to_core(after(far, rest_x, mine_x), "far_x")
    mine_x = after(mine_x, far)
    early0, send0, keep0 = score(
        rows_of(mine, mine_x, rest, rest_x, far, far_x), stored=128, early=[(None, 0, 64)]
    )
    got0 = to_layer(send0, "got0")

    near_px = to_core(near_p, "near_px")
    far_p, cross = after(far_p, near_px, near_x, send0), after(cross, send0)
    far_px0 = to_core(far_p[:CHUNK], "far_px0")
    far_px1 = to_core(far_p[CHUNK:], "far_px1")
    cross_x = to_core(cross, "cross_x")
    cross_pa = to_part(after(cross[:CHUNK], cross_x), "cross_pa")
    cross_pb = to_near(far_p[CHUNK:], "cross_pb")
    cross_x = after(cross_x, got0)
    early1, send1, keep1 = score(
        rows_of(near, near_x, near_p, near_px, far_p, far_px0, far_px1, cross, cross_x),
        stored=128,
        early=[(early0, 64, 64), (None, 0, 64)],
    )
    got1 = to_layer(send1, "got1")
    cross_pa, cross_pb = after(cross_pa, send1, got0), after(cross_pb, send1, got0)
    cross_pxa = to_core(cross_pa, "cross_pxa")
    cross_pxb = to_core(cross_pb, "cross_pxb")
    last = rows_of(cross_pa, cross_pb, cross_pxa, cross_pxb)
    send2, keep2 = score(last, early=[(early1, 64, 64)])
    got2 = to_layer(send2, "got2")

    train_ids, query_ids = train_ids[None, :], query_ids[:, None]
    most = call_final(
        train_ids,
        query_ids,
        [keep0, got0, keep1, got1],
        ((0, 0, 1, 0, 0), (1, 2, 3, 0, 0), (2, 2, 3, 64, 0)),
    )
    return call_final(
        train_ids,
        query_ids,
        [keep2, got2],
        ((3, 0, 1, 0, 0),),
        most,
    )


def solution(mesh):
    placed = (
        P(("parts", "store"), "layer", None),
        P("store", "layer", None),
        P("layer", None, None),
        P("layer", None, None),
        P(),
        P("layer"),
        P(("parts", "store")),
        P("layer"),
    )
    sizes = tuple(mesh.shape[axis] for axis in AXES)
    return jax.shard_map(
        small if sizes == (PARTS, CHIPS * CORES, LAYERS) else general,
        mesh=mesh,
        in_specs=placed,
        out_specs=P("layer", ("parts", "store")),
        check_vma=False,
    )
```

```python
import functools

import jax
import jax.numpy as jnp
from jax import lax
from jax.experimental import pallas as pl
from jax.experimental.pallas import tpu as pltpu
from jax.sharding import PartitionSpec as P

AXES = ("parts", "store", "layer")
VMEM = pl.BlockSpec(memory_space=pltpu.VMEM)
SMEM = pl.BlockSpec(memory_space=pltpu.SMEM)
bf16, f32 = jnp.bfloat16, jnp.float32
LIMIT = 20 * 1024 * 1024


def preconditioned(query_grads, left_factor, right_factor):
    q_rows, slots, width = query_grads.shape
    side = left_factor.shape[1]
    mats = query_grads.astype(jnp.float32).reshape(q_rows, slots, side, side)
    half = jnp.einsum("lij,qljk->qlik", left_factor, mats, precision=lax.Precision.HIGHEST)
    full = jnp.einsum("qlik,lkm->qlim", half, right_factor, precision=lax.Precision.HIGHEST)
    return full.reshape(q_rows, slots, width).astype(jnp.bfloat16)


def general(
    train_grads,
    query_grads,
    left_factor,
    right_factor,
    layer_weight,
    layer_of,
    train_ids,
    query_ids,
):
    precond = preconditioned(query_grads, left_factor, right_factor)
    weight = jnp.take(layer_weight, layer_of[0])
    queries = lax.all_gather(precond, "store", axis=0, tiled=True)
    terms = weight * jnp.dot(
        queries[:, 0, :], train_grads[:, 0, :].T, preferred_element_type=jnp.float32
    )
    summed = lax.psum_scatter(terms, "layer", scatter_dimension=0, tiled=True)
    same = query_ids[:, None] == train_ids[None, :]
    return jnp.where(same, jnp.float32(0.0), summed)


PARTS, CHIPS, CORES, LAYERS = 2, 4, 2, 2
CHUNK = 16
HALF = 2 * CHUNK
STEP = 256
HBM = pl.BlockSpec(memory_space=pltpu.HBM)


def permute(value, name, target):
    pairs = []
    for p in range(PARTS):
        for z in range(CHIPS):
            for c in range(CORES):
                for l in range(LAYERS):
                    tp, tz, tc, tl = target(p, z, c, l)
                    source = ((p * CHIPS + z) * CORES + c) * LAYERS + l
                    pairs.append((source, ((tp * CHIPS + tz) * CORES + tc) * LAYERS + tl))
    with jax.named_scope(name):
        return lax.ppermute(value, AXES, pairs)


to_part = functools.partial(permute, target=lambda p, z, c, l: (1 - p, z, c, l))
to_core = functools.partial(permute, target=lambda p, z, c, l: (p, z, 1 - c, l))
to_layer = functools.partial(permute, target=lambda p, z, c, l: (p, z, c, 1 - l))
to_near = functools.partial(permute, target=lambda p, z, c, l: (p, z ^ 1, c, l))
to_middle = functools.partial(permute, target=lambda p, z, c, l: (p, z ^ 3 if 0 < z < 3 else z, c, l))


def after(value, *others):
    return lax.optimization_barrier((value, *others))[0]


def place():
    store = lax.axis_index("store")
    return lax.axis_index("parts"), store // CORES, store % CORES, lax.axis_index("layer")


def split(x, terms):
    out = []
    for _ in range(terms):
        term = x.astype(bf16)
        out.append(term)
        x = x - term.astype(f32)
    return out


def dot(a, b):
    return lax.dot_general(a, b, (((1,), (0,)), ((), ())), preferred_element_type=f32)


def iota(shape, dim):
    return lax.broadcasted_iota(jnp.int32, shape, dim)


def factors(left, right):
    r, c = iota((256, 64), 0), iota((256, 64), 1)
    pick = jnp.where(c == 4 * (r % 16) + (r // 16) % 4, 1.0, 0.0).astype(bf16)
    r, c = iota((64, 256), 0), iota((64, 256), 1)
    pick_t = jnp.where(r == 4 * (c % 16) + (c // 16) % 4, 1.0, 0.0).astype(bf16)
    block = iota((256, 256), 0) // 64 == iota((256, 256), 1) // 64
    lefts = [
        jnp.where(block, dot(dot(pick, term).astype(bf16), pick_t), 0.0).astype(bf16)
        for term in split(left, 2)
    ]
    row = jnp.concatenate([right, right], axis=1)
    tiled = jnp.concatenate([jnp.concatenate([row] * 4, axis=1)] * 4, axis=0)
    block = iota((256, 512), 0) // 64 == iota((256, 512), 1) // 128
    return lefts, split(jnp.where(block, tiled, 0.0), 2)


def precond_rows(q_ref, lefts, rights, out):
    for at in range(0, q_ref.shape[0], CHUNK):
        values = precond_chunk(q_ref[at : at + CHUNK, :], lefts, rights)
        for t, value in enumerate(values):
            out[at : at + CHUNK, t * 256 : (t + 1) * 256] = value


def precond_chunk(q, lefts, rights):
    tiles = q.shape[1] // 256
    r, c = iota((256, 256), 0), iota((256, 256), 1)
    swap = jnp.where((r // 16 == c % 16) & (r % 16 == c // 16), 1.0, 0.0).astype(bf16)
    x = jnp.concatenate([q[:, t * 256 : (t + 1) * 256] for t in range(tiles)], axis=0)
    x = dot(swap, x).astype(bf16)
    z = dot(x, rights[0]) + dot(x, rights[1])
    sets = []
    for first in range(0, 16, 4):
        rows = [
            z[query * 16 : (query + 1) * 16, s * 128 : (s + 1) * 128]
            for query in range(first, first + 4)
            for s in range(4)
        ]
        sets.append(jnp.concatenate(rows, axis=0))
    high, low = split(jnp.concatenate(sets, axis=1), 2)
    z = dot(lefts[0], high) + (dot(lefts[0], low) + dot(lefts[1], high))
    side = iota((16, 128), 1) < 64
    rows = []
    for first in range(4):
        for k in range(4):
            o = z[k * 64 : (k + 1) * 64, first * 128 : (first + 1) * 128]
            pair = [jnp.where(side, o[0:16], o[16:32]), jnp.where(side, o[32:48], o[48:64])]
            rows.append(jnp.concatenate(pair, axis=1))
    y = dot(swap, jnp.concatenate(rows, axis=0).astype(bf16)).astype(bf16)
    return [y[t * 16 : (t + 1) * 16] for t in range(tiles)]


def own_kernel(q_hbm, left_hbm, right_hbm, mine, lefts_ref, rights_ref, q_ref, left, right, sems):
    at = pl.multiple_of(lax.axis_index("parts") * HALF, HALF)
    copies = [
        pltpu.make_async_copy(source, target, sems.at[k])
        for k, (source, target) in enumerate(
            ((left_hbm, left), (right_hbm, right), (q_hbm.at[pl.ds(at, HALF), :], q_ref))
        )
    ]
    for copy in copies:
        copy.start()
    copies[0].wait()
    copies[1].wait()
    lefts, rights = factors(left[...], right[...])
    for k in range(2):
        lefts_ref[k] = lefts[k]
        rights_ref[k] = rights[k]
    copies[2].wait()
    precond_rows(q_ref, lefts, rights, mine)


def rest_kernel(
    weight_ref, layer_ref, q_hbm, train_hbm, lefts_ref, rights_ref, rest, train, weight, q_ref, sems
):
    at = pl.multiple_of((1 - lax.axis_index("parts")) * HALF, HALF)
    q_copy = pltpu.make_async_copy(q_hbm.at[pl.ds(at, HALF), :], q_ref, sems.at[0])
    q_copy.start()
    copies = []
    for k in range(train.shape[0] // STEP):
        here = pl.ds(k * STEP, STEP)
        copies.append(pltpu.make_async_copy(train_hbm.at[here, :], train.at[here, :], sems.at[1 + k]))
        copies[-1].start()
    weight[...] = jnp.full(weight.shape, weight_ref[layer_ref[0]])
    lefts, rights = [lefts_ref[0], lefts_ref[1]], [rights_ref[0], rights_ref[1]]
    q_copy.wait()
    precond_rows(q_ref, lefts, rights, rest)
    for copy in copies:
        copy.wait()


def score_kernel(weight_ref, train_ref, *refs, picks, stored, early, columns):
    inputs, refs = refs[: len(picks)], refs[len(picks) :]
    n_before = sum(taken for _, _, taken in early)
    before, outs = refs[:n_before], refs[n_before:]
    weight = weight_ref[0:1, :]
    queries = jnp.concatenate(
        [piece[at : at + n, :] for piece, rows in zip(inputs, picks) for at, n in rows], axis=0
    )
    _, z, _, layer = place()
    near_is_mine = z // 2 == layer
    for at in range(*columns, STEP):
        there, here = slice(at, at + STEP), slice(at - columns[0], at - columns[0] + STEP)
        value = lax.dot_general(
            train_ref[there, :], queries, (((1,), (1,)), ((), ())), preferred_element_type=f32
        )
        value = weight * value.T
        if stored:
            outs[0][:, here] = value[:stored]
        if early:
            send, keep = outs[-2:]
            old, given = [], list(before)
            for first, rows, taken in early:
                old.append(
                    given.pop(0)[first : first + rows, there] if taken else value[first : first + rows]
                )
            old, new = jnp.concatenate(old, axis=0), value[stored:]
            send[:, here] = jnp.where(near_is_mine, new, old).astype(send.dtype)
            keep[:, here] = jnp.where(near_is_mine, old, new)


def kernel_call(kernel, outs, inputs, specs=None, scratch=()):
    return pl.pallas_call(
        kernel,
        out_shape=outs,
        in_specs=specs or [VMEM] * len(inputs),
        out_specs=[VMEM] * len(outs) if isinstance(outs, list) else VMEM,
        scratch_shapes=scratch,
        compiler_params=pltpu.CompilerParams(vmem_limit_bytes=LIMIT),
    )(*inputs)


def call_scores(weight, train, inputs, stored=0, early=(), columns=None):
    columns = columns or (0, train.shape[0])
    n = columns[1] - columns[0]
    total = sum(count for _, rows in inputs for _, count in rows)
    others = [a for a, _ in inputs] + [a for a, _, _ in early if a is not None]
    outs = [jax.ShapeDtypeStruct((stored, n), f32)] if stored else []
    if early:
        outs += [jax.ShapeDtypeStruct((total - stored, n), t) for t in (bf16, f32)]
    return kernel_call(
        functools.partial(
            score_kernel,
            picks=[rows for _, rows in inputs],
            stored=stored,
            early=[(first, rows, a is not None) for a, first, rows in early],
            columns=columns,
        ),
        outs,
        [weight, train, *others],
    )


def final_kernel(train_ids, query_ids, *refs, groups, n_given):
    given, refs = refs[:n_given], refs[n_given:]
    *_, out, done, sems = refs
    part, z, core, layer = place()
    low = z % 2
    inner = (z + 1) // 2 == 1
    first = jnp.where((z // 2 == layer) | ~inner, low, 1 - low)
    copies = []
    for k, (which, keep, got, row, column) in enumerate(groups):
        block = first if which < 2 else 1 - first
        half = part if which % 2 == 0 else 1 - part
        keep, got = given[keep], given[got]
        columns = pl.ds(column, keep.shape[1])
        for i, c in enumerate((core, 1 - core)):
            at = pl.multiple_of(((block * 2 + c) * 2 + half) * HALF, HALF)
            here, j = slice(row + i * HALF, row + (i + 1) * HALF), 2 * k + i
            total = keep[here, :] + got[here, :].astype(f32)
            same = query_ids[pl.ds(at, HALF), :] == train_ids[:, columns]
            slot = done.at[j * HALF : (j + 1) * HALF, : keep.shape[1]]
            slot[...] = jnp.where(same, jnp.float32(0.0), total)
            copies.append(
                pltpu.make_async_copy(slot, out.at[pl.ds(at, HALF), columns], sems.at[j])
            )
            copies[-1].start()
    for copy in copies:
        copy.wait()


def call_final(train_ids, query_ids, given, groups, before=None):
    rows, n = query_ids.shape[0], train_ids.shape[1]
    inputs = [train_ids, query_ids, *given] + ([] if before is None else [before])
    return pl.pallas_call(
        functools.partial(final_kernel, groups=groups, n_given=len(given)),
        out_shape=jax.ShapeDtypeStruct((rows, n), f32),
        in_specs=[VMEM] * (2 + len(given)) + ([] if before is None else [HBM]),
        out_specs=HBM,
        scratch_shapes=[
            pltpu.VMEM((2 * len(groups) * HALF, max(a.shape[1] for a in given)), f32),
            pltpu.SemaphoreType.DMA((2 * len(groups),)),
        ],
        input_output_aliases={} if before is None else {len(inputs) - 1: 0},
        compiler_params=pltpu.CompilerParams(vmem_limit_bytes=LIMIT),
    )(*inputs)


def small(
    train_grads,
    query_grads,
    left_factor,
    right_factor,
    layer_weight,
    layer_of,
    train_ids,
    query_ids,
):
    in_hbm = lambda array: pltpu.with_memory_space_constraint(array, pltpu.HBM)
    train, queries = in_hbm(train_grads[:, 0, :]), in_hbm(query_grads[:, 0, :])
    width, side = queries.shape[1], left_factor.shape[1]
    shape = jax.ShapeDtypeStruct
    mine, lefts, rights = kernel_call(
        own_kernel,
        [shape((HALF, width), bf16), shape((2, 256, 256), bf16), shape((2, 256, 512), bf16)],
        [queries, in_hbm(left_factor[0]), in_hbm(right_factor[0])],
        [HBM] * 3,
        [
            pltpu.VMEM((HALF, width), bf16),
            pltpu.VMEM((side, side), f32),
            pltpu.VMEM((side, side), f32),
            pltpu.SemaphoreType.DMA((3,)),
        ],
    )
    near = to_near(mine, "near")
    middle = to_middle(mine, "middle")
    rest, train, weight = kernel_call(
        rest_kernel,
        [shape((HALF, width), bf16), shape(train.shape, bf16), shape((8, STEP), f32)],
        [in_hbm(layer_weight), layer_of, queries, train, lefts, rights],
        [SMEM, SMEM, HBM, HBM, VMEM, VMEM],
        [pltpu.VMEM((HALF, width), bf16), pltpu.SemaphoreType.DMA((1 + train.shape[0] // STEP,))],
    )
    score = functools.partial(call_scores, weight, train)

    def rows_of(*pieces):
        return [(piece, ((0, piece.shape[0]),)) for piece in pieces]

    mine_x = to_core(after(mine, rest), "mine_x")
    rest_x = to_core(rest, "rest_x")
    near = after(near, rest)
    near_p = to_part(near, "near_p")
    middle_near = to_middle(near, "middle_near")
    outward = to_near(after(middle, near), "outward")
    inner = (place()[1] + 1) // 2 == 1
    near_x = to_core(near, "near_x")
    far = jnp.where(inner, middle, outward)
    far_p = to_part(far, "far_p")
    outward_near = to_near(after(middle_near, far), "outward_near")
    cross = jnp.where(inner, middle_near, outward_near)
    far_x = to_core(after(far, rest_x), "far_x")
    (early0,) = score(rows_of(mine, mine_x, rest, rest_x), stored=128)
    send0, keep0 = score(rows_of(far, far_x), early=[(early0, 0, 64)])
    got0 = to_layer(send0, "got0")

    near_p = after(near_p, early0)
    near_px = to_core(near_p, "near_px")
    far_p, cross = after(far_p, near_px, send0), after(cross, send0)
    far_px = to_core(far_p, "far_px")
    cross_p = to_part(cross, "cross_p")
    cross_x = to_core(cross, "cross_x")
    early1, send1, keep1 = score(
        rows_of(near, near_x, near_p, near_px, far_p, far_px, cross, cross_x),
        stored=128,
        early=[(early0, 64, 64), (None, 0, 64)],
    )
    got1 = to_layer(send1, "got1")
    cross_p = after(cross_p, send1, got0)
    cross_pxa = to_core(cross_p[:CHUNK], "cross_pxa")
    cross_pxb = to_core(cross_p[CHUNK:], "cross_pxb")
    last = rows_of(cross_p, cross_pxa, cross_pxb)
    send2, keep2 = score(last, early=[(early1, 64, 64)])
    got2 = to_layer(send2, "got2")

    train_ids, query_ids = train_ids[None, :], query_ids[:, None]
    most = call_final(
        train_ids,
        query_ids,
        [keep0, got0, keep1, got1],
        ((0, 0, 1, 0, 0), (1, 2, 3, 0, 0), (2, 2, 3, 64, 0)),
    )
    return call_final(
        train_ids,
        query_ids,
        [keep2, got2],
        ((3, 0, 1, 0, 0),),
        most,
    )


def solution(mesh):
    placed = (
        P(("parts", "store"), "layer", None),
        P("store", "layer", None),
        P("layer", None, None),
        P("layer", None, None),
        P(),
        P("layer"),
        P(("parts", "store")),
        P("layer"),
    )
    sizes = tuple(mesh.shape[axis] for axis in AXES)
    return jax.shard_map(
        small if sizes == (PARTS, CHIPS * CORES, LAYERS) else general,
        mesh=mesh,
        in_specs=placed,
        out_specs=P("layer", ("parts", "store")),
        check_vma=False,
    )
```

```python
import functools

import jax
import jax.numpy as jnp
from jax import lax
from jax.experimental import pallas as pl
from jax.experimental.pallas import tpu as pltpu
from jax.sharding import PartitionSpec as P

AXES = ("parts", "store", "layer")
VMEM = pl.BlockSpec(memory_space=pltpu.VMEM)
SMEM = pl.BlockSpec(memory_space=pltpu.SMEM)
bf16, f32 = jnp.bfloat16, jnp.float32
LIMIT = 20 * 1024 * 1024


def preconditioned(query_grads, left_factor, right_factor):
    q_rows, slots, width = query_grads.shape
    side = left_factor.shape[1]
    mats = query_grads.astype(jnp.float32).reshape(q_rows, slots, side, side)
    half = jnp.einsum("lij,qljk->qlik", left_factor, mats, precision=lax.Precision.HIGHEST)
    full = jnp.einsum("qlik,lkm->qlim", half, right_factor, precision=lax.Precision.HIGHEST)
    return full.reshape(q_rows, slots, width).astype(jnp.bfloat16)


def general(
    train_grads,
    query_grads,
    left_factor,
    right_factor,
    layer_weight,
    layer_of,
    train_ids,
    query_ids,
):
    precond = preconditioned(query_grads, left_factor, right_factor)
    weight = jnp.take(layer_weight, layer_of[0])
    queries = lax.all_gather(precond, "store", axis=0, tiled=True)
    terms = weight * jnp.dot(
        queries[:, 0, :], train_grads[:, 0, :].T, preferred_element_type=jnp.float32
    )
    summed = lax.psum_scatter(terms, "layer", scatter_dimension=0, tiled=True)
    same = query_ids[:, None] == train_ids[None, :]
    return jnp.where(same, jnp.float32(0.0), summed)


PARTS, CHIPS, CORES, LAYERS = 2, 4, 2, 2
CHUNK = 16
HALF = 2 * CHUNK
STEP = 256
HBM = pl.BlockSpec(memory_space=pltpu.HBM)


def permute(value, name, target):
    pairs = []
    for p in range(PARTS):
        for z in range(CHIPS):
            for c in range(CORES):
                for l in range(LAYERS):
                    tp, tz, tc, tl = target(p, z, c, l)
                    source = ((p * CHIPS + z) * CORES + c) * LAYERS + l
                    pairs.append((source, ((tp * CHIPS + tz) * CORES + tc) * LAYERS + tl))
    with jax.named_scope(name):
        return lax.ppermute(value, AXES, pairs)


to_part = functools.partial(permute, target=lambda p, z, c, l: (1 - p, z, c, l))
to_core = functools.partial(permute, target=lambda p, z, c, l: (p, z, 1 - c, l))
to_layer = functools.partial(permute, target=lambda p, z, c, l: (p, z, c, 1 - l))
to_near = functools.partial(permute, target=lambda p, z, c, l: (p, z ^ 1, c, l))
to_far = functools.partial(permute, target=lambda p, z, c, l: (p, z ^ 3, c, l))


def after(value, *others):
    return lax.optimization_barrier((value, *others))[0]


def place():
    store = lax.axis_index("store")
    return lax.axis_index("parts"), store // CORES, store % CORES, lax.axis_index("layer")


def split(x, terms):
    out = []
    for _ in range(terms):
        term = x.astype(bf16)
        out.append(term)
        x = x - term.astype(f32)
    return out


def dot(a, b):
    return lax.dot_general(a, b, (((1,), (0,)), ((), ())), preferred_element_type=f32)


def iota(shape, dim):
    return lax.broadcasted_iota(jnp.int32, shape, dim)


def factors(left, right):
    r, c = iota((256, 64), 0), iota((256, 64), 1)
    pick = jnp.where(c == 4 * (r % 16) + (r // 16) % 4, 1.0, 0.0).astype(bf16)
    r, c = iota((64, 256), 0), iota((64, 256), 1)
    pick_t = jnp.where(r == 4 * (c % 16) + (c // 16) % 4, 1.0, 0.0).astype(bf16)
    block = iota((256, 256), 0) // 64 == iota((256, 256), 1) // 64
    lefts = [
        jnp.where(block, dot(dot(pick, term).astype(bf16), pick_t), 0.0).astype(bf16)
        for term in split(left, 2)
    ]
    row = jnp.concatenate([right, right], axis=1)
    tiled = jnp.concatenate([jnp.concatenate([row] * 4, axis=1)] * 4, axis=0)
    block = iota((256, 512), 0) // 64 == iota((256, 512), 1) // 128
    return lefts, split(jnp.where(block, tiled, 0.0), 2)


def precond_rows(q_ref, lefts, rights, out):
    rows, width = q_ref.shape
    tiles, chunks = width // 256, range(rows // CHUNK)
    side_by_side = functools.partial(jnp.concatenate, axis=1)
    r, c = iota((256, 256), 0), iota((256, 256), 1)
    swap = jnp.where((r // 16 == c % 16) & (r % 16 == c // 16), 1.0, 0.0).astype(bf16)

    def of_chunk(k):
        q = q_ref[k * CHUNK : (k + 1) * CHUNK, :]
        return jnp.concatenate([q[:, t * 256 : (t + 1) * 256] for t in range(tiles)], axis=0)

    x = dot(swap, side_by_side([of_chunk(k) for k in chunks])).astype(bf16)
    x = jnp.concatenate([x[:, k * 256 : (k + 1) * 256] for k in chunks], axis=0)
    z = dot(x, rights[0]) + dot(x, rights[1])
    sets = []
    for first in range(0, rows, 4):
        pieces = [
            z[query * 16 : (query + 1) * 16, s * 128 : (s + 1) * 128]
            for query in range(first, first + 4)
            for s in range(4)
        ]
        sets.append(jnp.concatenate(pieces, axis=0))
    high, low = split(side_by_side(sets), 2)
    z = dot(lefts[0], high) + (dot(lefts[0], low) + dot(lefts[1], high))
    side = iota((16, 128), 1) < 64
    y = []
    for query in range(rows):
        k, group = query % 4, query // 4
        o = z[k * 64 : (k + 1) * 64, group * 128 : (group + 1) * 128]
        pair = [jnp.where(side, o[0:16], o[16:32]), jnp.where(side, o[32:48], o[48:64])]
        y.append(side_by_side(pair))
    y = [jnp.concatenate(y[k * CHUNK : (k + 1) * CHUNK], axis=0) for k in chunks]
    y = dot(swap, side_by_side(y).astype(bf16)).astype(bf16)
    for k in chunks:
        for t in range(tiles):
            value = y[t * 16 : (t + 1) * 16, k * 256 : (k + 1) * 256]
            out[k * CHUNK : (k + 1) * CHUNK, t * 256 : (t + 1) * 256] = value


def own_kernel(q_hbm, left_hbm, right_hbm, mine, lefts_ref, rights_ref, q_ref, left, right, sems):
    at = pl.multiple_of(lax.axis_index("parts") * HALF, HALF)
    copies = [
        pltpu.make_async_copy(source, target, sems.at[k])
        for k, (source, target) in enumerate(
            ((left_hbm, left), (right_hbm, right), (q_hbm.at[pl.ds(at, HALF), :], q_ref))
        )
    ]
    for copy in copies:
        copy.start()
    copies[0].wait()
    copies[1].wait()
    lefts, rights = factors(left[...], right[...])
    for k in range(2):
        lefts_ref[k] = lefts[k]
        rights_ref[k] = rights[k]
    copies[2].wait()
    precond_rows(q_ref, lefts, rights, mine)


def rest_kernel(
    weight_ref, layer_ref, q_hbm, train_hbm, lefts_ref, rights_ref, rest, train, weight, q_ref, sems
):
    at = pl.multiple_of((1 - lax.axis_index("parts")) * HALF, HALF)
    q_copy = pltpu.make_async_copy(q_hbm.at[pl.ds(at, HALF), :], q_ref, sems.at[0])
    q_copy.start()
    copies = []
    for k in range(train.shape[0] // STEP):
        here = pl.ds(k * STEP, STEP)
        copies.append(pltpu.make_async_copy(train_hbm.at[here, :], train.at[here, :], sems.at[1 + k]))
        copies[-1].start()
    weight[...] = jnp.full(weight.shape, weight_ref[layer_ref[0]])
    lefts, rights = [lefts_ref[0], lefts_ref[1]], [rights_ref[0], rights_ref[1]]
    q_copy.wait()
    precond_rows(q_ref, lefts, rights, rest)
    for copy in copies:
        copy.wait()


def score_kernel(weight_ref, train_ref, *refs, picks, stored, early, columns):
    inputs, refs = refs[: len(picks)], refs[len(picks) :]
    n_before = sum(taken for _, _, taken in early)
    before, outs = refs[:n_before], refs[n_before:]
    weight = weight_ref[0:1, :]
    queries = jnp.concatenate(
        [piece[at : at + n, :] for piece, rows in zip(inputs, picks) for at, n in rows], axis=0
    )
    _, z, _, layer = place()
    near_is_mine = z // 2 == layer
    for at in range(*columns, STEP):
        there, here = slice(at, at + STEP), slice(at - columns[0], at - columns[0] + STEP)
        value = lax.dot_general(
            train_ref[there, :], queries, (((1,), (1,)), ((), ())), preferred_element_type=f32
        )
        value = weight * value.T
        if stored:
            outs[0][:, here] = value[:stored]
        if early:
            send, keep = outs[-2:]
            old, given = [], list(before)
            for first, rows, taken in early:
                old.append(
                    given.pop(0)[first : first + rows, there] if taken else value[first : first + rows]
                )
            old, new = jnp.concatenate(old, axis=0), value[stored:]
            send[:, here] = jnp.where(near_is_mine, new, old).astype(send.dtype)
            keep[:, here] = jnp.where(near_is_mine, old, new)


def kernel_call(kernel, outs, inputs, specs=None, scratch=()):
    return pl.pallas_call(
        kernel,
        out_shape=outs,
        in_specs=specs or [VMEM] * len(inputs),
        out_specs=[VMEM] * len(outs) if isinstance(outs, list) else VMEM,
        scratch_shapes=scratch,
        compiler_params=pltpu.CompilerParams(vmem_limit_bytes=LIMIT),
    )(*inputs)


def call_scores(weight, train, inputs, stored=0, early=(), columns=None):
    columns = columns or (0, train.shape[0])
    n = columns[1] - columns[0]
    total = sum(count for _, rows in inputs for _, count in rows)
    others = [a for a, _ in inputs] + [a for a, _, _ in early if a is not None]
    outs = [jax.ShapeDtypeStruct((stored, n), f32)] if stored else []
    if early:
        outs += [jax.ShapeDtypeStruct((total - stored, n), t) for t in (bf16, f32)]
    return kernel_call(
        functools.partial(
            score_kernel,
            picks=[rows for _, rows in inputs],
            stored=stored,
            early=[(first, rows, a is not None) for a, first, rows in early],
            columns=columns,
        ),
        outs,
        [weight, train, *others],
    )


def final_kernel(train_ids, query_ids, *refs, groups, n_given):
    given, refs = refs[:n_given], refs[n_given:]
    *_, out, done, sems = refs
    part, z, core, layer = place()
    low = z % 2
    first = jnp.where(z // 2 == layer, low, 1 - low)
    copies = []
    for k, (which, keep, got, row, column) in enumerate(groups):
        block = first if which < 2 else 1 - first
        half = part if which % 2 == 0 else 1 - part
        keep, got = given[keep], given[got]
        columns = pl.ds(column, keep.shape[1])
        for i, c in enumerate((core, 1 - core)):
            at = pl.multiple_of(((block * 2 + c) * 2 + half) * HALF, HALF)
            here, j = slice(row + i * HALF, row + (i + 1) * HALF), 2 * k + i
            total = keep[here, :] + got[here, :].astype(f32)
            same = query_ids[pl.ds(at, HALF), :] == train_ids[:, columns]
            slot = done.at[j * HALF : (j + 1) * HALF, : keep.shape[1]]
            slot[...] = jnp.where(same, jnp.float32(0.0), total)
            copies.append(
                pltpu.make_async_copy(slot, out.at[pl.ds(at, HALF), columns], sems.at[j])
            )
            copies[-1].start()
    for copy in copies:
        copy.wait()


def call_final(train_ids, query_ids, given, groups, before=None):
    rows, n = query_ids.shape[0], train_ids.shape[1]
    inputs = [train_ids, query_ids, *given] + ([] if before is None else [before])
    return pl.pallas_call(
        functools.partial(final_kernel, groups=groups, n_given=len(given)),
        out_shape=jax.ShapeDtypeStruct((rows, n), f32),
        in_specs=[VMEM] * (2 + len(given)) + ([] if before is None else [HBM]),
        out_specs=HBM,
        scratch_shapes=[
            pltpu.VMEM((2 * len(groups) * HALF, max(a.shape[1] for a in given)), f32),
            pltpu.SemaphoreType.DMA((2 * len(groups),)),
        ],
        input_output_aliases={} if before is None else {len(inputs) - 1: 0},
        compiler_params=pltpu.CompilerParams(vmem_limit_bytes=LIMIT),
    )(*inputs)


def small(
    train_grads,
    query_grads,
    left_factor,
    right_factor,
    layer_weight,
    layer_of,
    train_ids,
    query_ids,
):
    in_hbm = lambda array: pltpu.with_memory_space_constraint(array, pltpu.HBM)
    train, queries = in_hbm(train_grads[:, 0, :]), in_hbm(query_grads[:, 0, :])
    width, side = queries.shape[1], left_factor.shape[1]
    shape = jax.ShapeDtypeStruct
    mine, lefts, rights = kernel_call(
        own_kernel,
        [shape((HALF, width), bf16), shape((2, 256, 256), bf16), shape((2, 256, 512), bf16)],
        [queries, in_hbm(left_factor[0]), in_hbm(right_factor[0])],
        [HBM] * 3,
        [
            pltpu.VMEM((HALF, width), bf16),
            pltpu.VMEM((side, side), f32),
            pltpu.VMEM((side, side), f32),
            pltpu.SemaphoreType.DMA((3,)),
        ],
    )
    near = to_near(mine, "near")
    far = to_far(mine, "far")
    rest, train, weight = kernel_call(
        rest_kernel,
        [shape((HALF, width), bf16), shape(train.shape, bf16), shape((8, STEP), f32)],
        [in_hbm(layer_weight), layer_of, queries, train, lefts, rights],
        [SMEM, SMEM, HBM, HBM, VMEM, VMEM],
        [pltpu.VMEM((HALF, width), bf16), pltpu.SemaphoreType.DMA((1 + train.shape[0] // STEP,))],
    )
    score = functools.partial(call_scores, weight, train)

    def rows_of(*pieces):
        return [(piece, ((0, piece.shape[0]),)) for piece in pieces]

    mine_x = to_core(after(mine, rest), "mine_x")
    rest_x = to_core(rest, "rest_x")
    near = after(near, rest)
    near_x = to_core(near, "near_x")
    near_p = to_part(near, "near_p")
    far = after(far, near)
    cross = to_near(far, "cross")
    far_p = to_part(far, "far_p")
    far_x = to_core(after(far, rest_x), "far_x")
    mine_x = after(mine_x, far)
    (early0,) = score(rows_of(mine, mine_x, rest, rest_x), stored=128)
    send0, keep0 = score(rows_of(far, far_x), early=[(early0, 0, 64)])
    got0 = to_layer(send0, "got0")

    near_p = after(near_p, early0)
    near_px = to_core(near_p, "near_px")
    far_p, cross = after(far_p, near_px, send0), after(cross, send0)
    far_px = to_core(far_p, "far_px")
    cross_pa = to_part(cross[:CHUNK], "cross_pa")
    cross_pb = to_near(far_p[CHUNK:], "cross_pb")
    cross_x = to_core(cross, "cross_x")
    early1, send1, keep1 = score(
        rows_of(near, near_x, near_p, near_px, far_p, far_px, cross, cross_x),
        stored=128,
        early=[(early0, 64, 64), (None, 0, 64)],
    )
    got1 = to_layer(send1, "got1")
    cross_pa, cross_pb = after(cross_pa, send1, got0), after(cross_pb, send1, got0)
    cross_pxa = to_core(cross_pa, "cross_pxa")
    cross_pxb = to_core(cross_pb, "cross_pxb")
    last = rows_of(cross_pa, cross_pb, cross_pxa, cross_pxb)
    send2, keep2 = score(last, early=[(early1, 64, 64)])
    got2 = to_layer(send2, "got2")

    train_ids, query_ids = train_ids[None, :], query_ids[:, None]
    most = call_final(
        train_ids,
        query_ids,
        [keep0, got0, keep1, got1],
        ((0, 0, 1, 0, 0), (1, 2, 3, 0, 0), (2, 2, 3, 64, 0)),
    )
    return call_final(
        train_ids,
        query_ids,
        [keep2, got2],
        ((3, 0, 1, 0, 0),),
        most,
    )


def solution(mesh):
    placed = (
        P(("parts", "store"), "layer", None),
        P("store", "layer", None),
        P("layer", None, None),
        P("layer", None, None),
        P(),
        P("layer"),
        P(("parts", "store")),
        P("layer"),
    )
    sizes = tuple(mesh.shape[axis] for axis in AXES)
    return jax.shard_map(
        small if sizes == (PARTS, CHIPS * CORES, LAYERS) else general,
        mesh=mesh,
        in_specs=placed,
        out_specs=P("layer", ("parts", "store")),
        check_vma=False,
    )
```

```python
import functools

import jax
import jax.numpy as jnp
from jax import lax
from jax.experimental import pallas as pl
from jax.experimental.pallas import tpu as pltpu
from jax.sharding import PartitionSpec as P

AXES = ("parts", "store", "layer")
VMEM = pl.BlockSpec(memory_space=pltpu.VMEM)
SMEM = pl.BlockSpec(memory_space=pltpu.SMEM)
bf16, f32 = jnp.bfloat16, jnp.float32
LIMIT = 20 * 1024 * 1024


def preconditioned(query_grads, left_factor, right_factor):
    q_rows, slots, width = query_grads.shape
    side = left_factor.shape[1]
    mats = query_grads.astype(jnp.float32).reshape(q_rows, slots, side, side)
    half = jnp.einsum("lij,qljk->qlik", left_factor, mats, precision=lax.Precision.HIGHEST)
    full = jnp.einsum("qlik,lkm->qlim", half, right_factor, precision=lax.Precision.HIGHEST)
    return full.reshape(q_rows, slots, width).astype(jnp.bfloat16)


def general(
    train_grads,
    query_grads,
    left_factor,
    right_factor,
    layer_weight,
    layer_of,
    train_ids,
    query_ids,
):
    precond = preconditioned(query_grads, left_factor, right_factor)
    weight = jnp.take(layer_weight, layer_of[0])
    queries = lax.all_gather(precond, "store", axis=0, tiled=True)
    terms = weight * jnp.dot(
        queries[:, 0, :], train_grads[:, 0, :].T, preferred_element_type=jnp.float32
    )
    summed = lax.psum_scatter(terms, "layer", scatter_dimension=0, tiled=True)
    same = query_ids[:, None] == train_ids[None, :]
    return jnp.where(same, jnp.float32(0.0), summed)


PARTS, CHIPS, CORES, LAYERS = 2, 4, 2, 2
CHUNK = 16
HALF = 2 * CHUNK
STEP = 256
HBM = pl.BlockSpec(memory_space=pltpu.HBM)


def permute(value, name, target):
    pairs = []
    for p in range(PARTS):
        for z in range(CHIPS):
            for c in range(CORES):
                for l in range(LAYERS):
                    tp, tz, tc, tl = target(p, z, c, l)
                    source = ((p * CHIPS + z) * CORES + c) * LAYERS + l
                    pairs.append((source, ((tp * CHIPS + tz) * CORES + tc) * LAYERS + tl))
    with jax.named_scope(name):
        return lax.ppermute(value, AXES, pairs)


to_part = functools.partial(permute, target=lambda p, z, c, l: (1 - p, z, c, l))
to_core = functools.partial(permute, target=lambda p, z, c, l: (p, z, 1 - c, l))
to_layer = functools.partial(permute, target=lambda p, z, c, l: (p, z, c, 1 - l))
to_near = functools.partial(permute, target=lambda p, z, c, l: (p, z ^ 1, c, l))
to_far = functools.partial(permute, target=lambda p, z, c, l: (p, z ^ 3, c, l))


def after(value, *others):
    return lax.optimization_barrier((value, *others))[0]


def place():
    store = lax.axis_index("store")
    return lax.axis_index("parts"), store // CORES, store % CORES, lax.axis_index("layer")


def split(x, terms):
    out = []
    for _ in range(terms):
        term = x.astype(bf16)
        out.append(term)
        x = x - term.astype(f32)
    return out


def dot(a, b):
    return lax.dot_general(a, b, (((1,), (0,)), ((), ())), preferred_element_type=f32)


def iota(shape, dim):
    return lax.broadcasted_iota(jnp.int32, shape, dim)


def factors(left, right):
    r, c = iota((256, 64), 0), iota((256, 64), 1)
    pick = jnp.where(c == 4 * (r % 16) + (r // 16) % 4, 1.0, 0.0).astype(bf16)
    r, c = iota((64, 256), 0), iota((64, 256), 1)
    pick_t = jnp.where(r == 4 * (c % 16) + (c // 16) % 4, 1.0, 0.0).astype(bf16)
    block = iota((256, 256), 0) // 64 == iota((256, 256), 1) // 64
    lefts = [
        jnp.where(block, dot(dot(pick, term).astype(bf16), pick_t), 0.0).astype(bf16)
        for term in split(left, 2)
    ]
    row = jnp.concatenate([right, right], axis=1)
    tiled = jnp.concatenate([jnp.concatenate([row] * 4, axis=1)] * 4, axis=0)
    block = iota((256, 512), 0) // 64 == iota((256, 512), 1) // 128
    return lefts, split(jnp.where(block, tiled, 0.0), 2)


def precond_rows(q_ref, lefts, rights, out):
    rows, width = q_ref.shape
    tiles, chunks = width // 256, range(rows // CHUNK)
    side_by_side = functools.partial(jnp.concatenate, axis=1)
    r, c = iota((256, 256), 0), iota((256, 256), 1)
    swap = jnp.where((r // 16 == c % 16) & (r % 16 == c // 16), 1.0, 0.0).astype(bf16)

    def of_chunk(k):
        q = q_ref[k * CHUNK : (k + 1) * CHUNK, :]
        return jnp.concatenate([q[:, t * 256 : (t + 1) * 256] for t in range(tiles)], axis=0)

    x = dot(swap, side_by_side([of_chunk(k) for k in chunks])).astype(bf16)
    x = jnp.concatenate([x[:, k * 256 : (k + 1) * 256] for k in chunks], axis=0)
    z = dot(x, rights[0]) + dot(x, rights[1])
    sets = []
    for first in range(0, rows, 4):
        pieces = [
            z[query * 16 : (query + 1) * 16, s * 128 : (s + 1) * 128]
            for query in range(first, first + 4)
            for s in range(4)
        ]
        sets.append(jnp.concatenate(pieces, axis=0))
    high, low = split(side_by_side(sets), 2)
    z = dot(lefts[0], high) + (dot(lefts[0], low) + dot(lefts[1], high))
    side = iota((16, 128), 1) < 64
    y = []
    for query in range(rows):
        k, group = query % 4, query // 4
        o = z[k * 64 : (k + 1) * 64, group * 128 : (group + 1) * 128]
        pair = [jnp.where(side, o[0:16], o[16:32]), jnp.where(side, o[32:48], o[48:64])]
        y.append(side_by_side(pair))
    y = [jnp.concatenate(y[k * CHUNK : (k + 1) * CHUNK], axis=0) for k in chunks]
    y = dot(swap, side_by_side(y).astype(bf16)).astype(bf16)
    for k in chunks:
        for t in range(tiles):
            value = y[t * 16 : (t + 1) * 16, k * 256 : (k + 1) * 256]
            out[k * CHUNK : (k + 1) * CHUNK, t * 256 : (t + 1) * 256] = value


def own_kernel(q_hbm, left_hbm, right_hbm, mine, lefts_ref, rights_ref, q_ref, left, right, sems):
    at = pl.multiple_of(lax.axis_index("parts") * HALF, HALF)
    copies = [
        pltpu.make_async_copy(source, target, sems.at[k])
        for k, (source, target) in enumerate(
            ((left_hbm, left), (right_hbm, right), (q_hbm.at[pl.ds(at, HALF), :], q_ref))
        )
    ]
    for copy in copies:
        copy.start()
    copies[0].wait()
    copies[1].wait()
    lefts, rights = factors(left[...], right[...])
    for k in range(2):
        lefts_ref[k] = lefts[k]
        rights_ref[k] = rights[k]
    copies[2].wait()
    precond_rows(q_ref, lefts, rights, mine)


def rest_kernel(
    weight_ref, layer_ref, q_hbm, train_hbm, lefts_ref, rights_ref, rest, train, weight, q_ref, sems
):
    at = pl.multiple_of((1 - lax.axis_index("parts")) * HALF, HALF)
    q_copy = pltpu.make_async_copy(q_hbm.at[pl.ds(at, HALF), :], q_ref, sems.at[0])
    q_copy.start()
    copies = []
    for k in range(train.shape[0] // STEP):
        here = pl.ds(k * STEP, STEP)
        copies.append(pltpu.make_async_copy(train_hbm.at[here, :], train.at[here, :], sems.at[1 + k]))
        copies[-1].start()
    weight[...] = jnp.full(weight.shape, weight_ref[layer_ref[0]])
    lefts, rights = [lefts_ref[0], lefts_ref[1]], [rights_ref[0], rights_ref[1]]
    q_copy.wait()
    precond_rows(q_ref, lefts, rights, rest)
    for copy in copies:
        copy.wait()


def score_kernel(weight_ref, train_ref, *refs, picks, stored, early, columns):
    inputs, refs = refs[: len(picks)], refs[len(picks) :]
    n_before = sum(taken for _, _, taken in early)
    before, outs = refs[:n_before], refs[n_before:]
    weight = weight_ref[0:1, :]
    queries = jnp.concatenate(
        [piece[at : at + n, :] for piece, rows in zip(inputs, picks) for at, n in rows], axis=0
    )
    _, z, _, layer = place()
    near_is_mine = z // 2 == layer
    for at in range(*columns, STEP):
        there, here = slice(at, at + STEP), slice(at - columns[0], at - columns[0] + STEP)
        value = lax.dot_general(
            train_ref[there, :], queries, (((1,), (1,)), ((), ())), preferred_element_type=f32
        )
        value = weight * value.T
        if stored:
            outs[0][:, here] = value[:stored]
        if early:
            send, keep = outs[-2:]
            old, given = [], list(before)
            for first, rows, taken in early:
                old.append(
                    given.pop(0)[first : first + rows, there] if taken else value[first : first + rows]
                )
            old, new = jnp.concatenate(old, axis=0), value[stored:]
            send[:, here] = jnp.where(near_is_mine, new, old).astype(send.dtype)
            keep[:, here] = jnp.where(near_is_mine, old, new)


def kernel_call(kernel, outs, inputs, specs=None, scratch=()):
    return pl.pallas_call(
        kernel,
        out_shape=outs,
        in_specs=specs or [VMEM] * len(inputs),
        out_specs=[VMEM] * len(outs) if isinstance(outs, list) else VMEM,
        scratch_shapes=scratch,
        compiler_params=pltpu.CompilerParams(vmem_limit_bytes=LIMIT),
    )(*inputs)


def call_scores(weight, train, inputs, stored=0, early=(), columns=None, sent=bf16):
    columns = columns or (0, train.shape[0])
    n = columns[1] - columns[0]
    total = sum(count for _, rows in inputs for _, count in rows)
    others = [a for a, _ in inputs] + [a for a, _, _ in early if a is not None]
    outs = [jax.ShapeDtypeStruct((stored, n), f32)] if stored else []
    if early:
        outs += [jax.ShapeDtypeStruct((total - stored, n), t) for t in (sent, f32)]
    return kernel_call(
        functools.partial(
            score_kernel,
            picks=[rows for _, rows in inputs],
            stored=stored,
            early=[(first, rows, a is not None) for a, first, rows in early],
            columns=columns,
        ),
        outs,
        [weight, train, *others],
    )


def final_kernel(train_ids, query_ids, *refs, groups, n_given):
    given, refs = refs[:n_given], refs[n_given:]
    *_, out, done, sems = refs
    part, z, core, layer = place()
    low = z % 2
    first = jnp.where(z // 2 == layer, low, 1 - low)
    copies = []
    for k, (which, keep, got, row, column) in enumerate(groups):
        block = first if which < 2 else 1 - first
        half = part if which % 2 == 0 else 1 - part
        keep, got = given[keep], given[got]
        columns = pl.ds(column, keep.shape[1])
        for i, c in enumerate((core, 1 - core)):
            at = pl.multiple_of(((block * 2 + c) * 2 + half) * HALF, HALF)
            here, j = slice(row + i * HALF, row + (i + 1) * HALF), 2 * k + i
            total = keep[here, :] + got[here, :].astype(f32)
            same = query_ids[pl.ds(at, HALF), :] == train_ids[:, columns]
            slot = done.at[j * HALF : (j + 1) * HALF, : keep.shape[1]]
            slot[...] = jnp.where(same, jnp.float32(0.0), total)
            copies.append(
                pltpu.make_async_copy(slot, out.at[pl.ds(at, HALF), columns], sems.at[j])
            )
            copies[-1].start()
    for copy in copies:
        copy.wait()


def call_final(train_ids, query_ids, given, groups, before=None):
    rows, n = query_ids.shape[0], train_ids.shape[1]
    inputs = [train_ids, query_ids, *given] + ([] if before is None else [before])
    return pl.pallas_call(
        functools.partial(final_kernel, groups=groups, n_given=len(given)),
        out_shape=jax.ShapeDtypeStruct((rows, n), f32),
        in_specs=[VMEM] * (2 + len(given)) + ([] if before is None else [HBM]),
        out_specs=HBM,
        scratch_shapes=[
            pltpu.VMEM((2 * len(groups) * HALF, max(a.shape[1] for a in given)), f32),
            pltpu.SemaphoreType.DMA((2 * len(groups),)),
        ],
        input_output_aliases={} if before is None else {len(inputs) - 1: 0},
        compiler_params=pltpu.CompilerParams(vmem_limit_bytes=LIMIT),
    )(*inputs)


def small(
    train_grads,
    query_grads,
    left_factor,
    right_factor,
    layer_weight,
    layer_of,
    train_ids,
    query_ids,
):
    in_hbm = lambda array: pltpu.with_memory_space_constraint(array, pltpu.HBM)
    train, queries = in_hbm(train_grads[:, 0, :]), in_hbm(query_grads[:, 0, :])
    width, side = queries.shape[1], left_factor.shape[1]
    shape = jax.ShapeDtypeStruct
    mine, lefts, rights = kernel_call(
        own_kernel,
        [shape((HALF, width), bf16), shape((2, 256, 256), bf16), shape((2, 256, 512), bf16)],
        [queries, in_hbm(left_factor[0]), in_hbm(right_factor[0])],
        [HBM] * 3,
        [
            pltpu.VMEM((HALF, width), bf16),
            pltpu.VMEM((side, side), f32),
            pltpu.VMEM((side, side), f32),
            pltpu.SemaphoreType.DMA((3,)),
        ],
    )
    near = to_near(mine, "near")
    far = to_far(mine, "far")
    rest, train, weight = kernel_call(
        rest_kernel,
        [shape((HALF, width), bf16), shape(train.shape, bf16), shape((8, STEP), f32)],
        [in_hbm(layer_weight), layer_of, queries, train, lefts, rights],
        [SMEM, SMEM, HBM, HBM, VMEM, VMEM],
        [pltpu.VMEM((HALF, width), bf16), pltpu.SemaphoreType.DMA((1 + train.shape[0] // STEP,))],
    )
    score = functools.partial(call_scores, weight, train)

    def rows_of(*pieces):
        return [(piece, ((0, piece.shape[0]),)) for piece in pieces]

    mine_x = to_core(after(mine, rest), "mine_x")
    rest_x = to_core(rest, "rest_x")
    near = after(near, rest)
    near_x = to_core(near, "near_x")
    near_p = to_part(near, "near_p")
    far = after(far, near)
    cross = to_near(far, "cross")
    far_p = to_part(far, "far_p")
    far_x = to_core(after(far, rest_x), "far_x")
    mine_x = after(mine_x, far)
    (early0,) = score(rows_of(mine, mine_x, rest, rest_x), stored=128)
    send0, keep0 = score(rows_of(far, far_x), early=[(early0, 0, 64)], sent=f32)
    got0 = to_layer(send0, "got0")

    near_p = after(near_p, early0)
    near_px = to_core(near_p, "near_px")
    far_p, cross = after(far_p, near_px, send0), after(cross, send0)
    far_px0 = to_core(far_p[:CHUNK], "far_px0")
    far_px1 = to_core(far_p[CHUNK:], "far_px1")
    cross_pa = to_part(cross[:CHUNK], "cross_pa")
    cross_pb = to_near(far_p[CHUNK:], "cross_pb")
    cross_x = to_core(cross, "cross_x")
    early1, send1, keep1 = score(
        rows_of(near, near_x, near_p, near_px, far_p, far_px0, far_px1, cross, cross_x),
        stored=128,
        early=[(early0, 64, 64), (None, 0, 64)],
    )
    got1 = to_layer(send1, "got1")
    cross_pa, cross_pb = after(cross_pa, send1, got0), after(cross_pb, send1, got0)
    cross_pxa = to_core(cross_pa, "cross_pxa")
    cross_pxb = to_core(cross_pb, "cross_pxb")
    last = rows_of(cross_pa, cross_pb, cross_pxa, cross_pxb)
    send2, keep2 = score(last, early=[(early1, 64, 64)])
    got2 = to_layer(send2, "got2")

    train_ids, query_ids = train_ids[None, :], query_ids[:, None]
    most = call_final(
        train_ids,
        query_ids,
        [keep0, got0, keep1, got1],
        ((0, 0, 1, 0, 0), (1, 2, 3, 0, 0), (2, 2, 3, 64, 0)),
    )
    return call_final(
        train_ids,
        query_ids,
        [keep2, got2],
        ((3, 0, 1, 0, 0),),
        most,
    )


def solution(mesh):
    placed = (
        P(("parts", "store"), "layer", None),
        P("store", "layer", None),
        P("layer", None, None),
        P("layer", None, None),
        P(),
        P("layer"),
        P(("parts", "store")),
        P("layer"),
    )
    sizes = tuple(mesh.shape[axis] for axis in AXES)
    return jax.shard_map(
        small if sizes == (PARTS, CHIPS * CORES, LAYERS) else general,
        mesh=mesh,
        in_specs=placed,
        out_specs=P("layer", ("parts", "store")),
        check_vma=False,
    )
```

```python
import functools

import jax
import jax.numpy as jnp
from jax import lax
from jax.experimental import pallas as pl
from jax.experimental.pallas import tpu as pltpu
from jax.sharding import PartitionSpec as P

AXES = ("parts", "store", "layer")
VMEM = pl.BlockSpec(memory_space=pltpu.VMEM)
SMEM = pl.BlockSpec(memory_space=pltpu.SMEM)
bf16, f32 = jnp.bfloat16, jnp.float32
LIMIT = 20 * 1024 * 1024


def preconditioned(query_grads, left_factor, right_factor):
    q_rows, slots, width = query_grads.shape
    side = left_factor.shape[1]
    mats = query_grads.astype(jnp.float32).reshape(q_rows, slots, side, side)
    half = jnp.einsum("lij,qljk->qlik", left_factor, mats, precision=lax.Precision.HIGHEST)
    full = jnp.einsum("qlik,lkm->qlim", half, right_factor, precision=lax.Precision.HIGHEST)
    return full.reshape(q_rows, slots, width).astype(jnp.bfloat16)


def general(
    train_grads,
    query_grads,
    left_factor,
    right_factor,
    layer_weight,
    layer_of,
    train_ids,
    query_ids,
):
    precond = preconditioned(query_grads, left_factor, right_factor)
    weight = jnp.take(layer_weight, layer_of[0])
    queries = lax.all_gather(precond, "store", axis=0, tiled=True)
    terms = weight * jnp.dot(
        queries[:, 0, :], train_grads[:, 0, :].T, preferred_element_type=jnp.float32
    )
    summed = lax.psum_scatter(terms, "layer", scatter_dimension=0, tiled=True)
    same = query_ids[:, None] == train_ids[None, :]
    return jnp.where(same, jnp.float32(0.0), summed)


PARTS, CHIPS, CORES, LAYERS = 2, 4, 2, 2
CHUNK = 16
HALF = 2 * CHUNK
STEP = 256
HBM = pl.BlockSpec(memory_space=pltpu.HBM)


def permute(value, name, target):
    pairs = []
    for p in range(PARTS):
        for z in range(CHIPS):
            for c in range(CORES):
                for l in range(LAYERS):
                    tp, tz, tc, tl = target(p, z, c, l)
                    source = ((p * CHIPS + z) * CORES + c) * LAYERS + l
                    pairs.append((source, ((tp * CHIPS + tz) * CORES + tc) * LAYERS + tl))
    with jax.named_scope(name):
        return lax.ppermute(value, AXES, pairs)


to_part = functools.partial(permute, target=lambda p, z, c, l: (1 - p, z, c, l))
to_core = functools.partial(permute, target=lambda p, z, c, l: (p, z, 1 - c, l))
to_layer = functools.partial(permute, target=lambda p, z, c, l: (p, z, c, 1 - l))
to_near = functools.partial(permute, target=lambda p, z, c, l: (p, z ^ 1, c, l))
to_far = functools.partial(permute, target=lambda p, z, c, l: (p, z ^ 3, c, l))


def after(value, *others):
    return lax.optimization_barrier((value, *others))[0]


def place():
    store = lax.axis_index("store")
    return lax.axis_index("parts"), store // CORES, store % CORES, lax.axis_index("layer")


def split(x, terms):
    out = []
    for _ in range(terms):
        term = x.astype(bf16)
        out.append(term)
        x = x - term.astype(f32)
    return out


def dot(a, b):
    return lax.dot_general(a, b, (((1,), (0,)), ((), ())), preferred_element_type=f32)


def iota(shape, dim):
    return lax.broadcasted_iota(jnp.int32, shape, dim)


def factors(left, right):
    r, c = iota((256, 64), 0), iota((256, 64), 1)
    pick = jnp.where(c == 4 * (r % 16) + (r // 16) % 4, 1.0, 0.0).astype(bf16)
    r, c = iota((64, 256), 0), iota((64, 256), 1)
    pick_t = jnp.where(r == 4 * (c % 16) + (c // 16) % 4, 1.0, 0.0).astype(bf16)
    block = iota((256, 256), 0) // 64 == iota((256, 256), 1) // 64
    lefts = [
        jnp.where(block, dot(dot(pick, term).astype(bf16), pick_t), 0.0).astype(bf16)
        for term in split(left, 2)
    ]
    row = jnp.concatenate([right, right], axis=1)
    tiled = jnp.concatenate([jnp.concatenate([row] * 4, axis=1)] * 4, axis=0)
    block = iota((256, 512), 0) // 64 == iota((256, 512), 1) // 128
    return lefts, split(jnp.where(block, tiled, 0.0), 2)


def precond_rows(q_ref, lefts, rights, out):
    rows, width = q_ref.shape
    tiles, chunks = width // 256, range(rows // CHUNK)
    side_by_side = functools.partial(jnp.concatenate, axis=1)
    r, c = iota((256, 256), 0), iota((256, 256), 1)
    swap = jnp.where((r // 16 == c % 16) & (r % 16 == c // 16), 1.0, 0.0).astype(bf16)

    def of_chunk(k):
        q = q_ref[k * CHUNK : (k + 1) * CHUNK, :]
        return jnp.concatenate([q[:, t * 256 : (t + 1) * 256] for t in range(tiles)], axis=0)

    x = dot(swap, side_by_side([of_chunk(k) for k in chunks])).astype(bf16)
    x = jnp.concatenate([x[:, k * 256 : (k + 1) * 256] for k in chunks], axis=0)
    z = dot(x, rights[0]) + dot(x, rights[1])
    sets = []
    for first in range(0, rows, 4):
        pieces = [
            z[query * 16 : (query + 1) * 16, s * 128 : (s + 1) * 128]
            for query in range(first, first + 4)
            for s in range(4)
        ]
        sets.append(jnp.concatenate(pieces, axis=0))
    high, low = split(side_by_side(sets), 2)
    z = dot(lefts[0], high) + (dot(lefts[0], low) + dot(lefts[1], high))
    side = iota((16, 128), 1) < 64
    y = []
    for query in range(rows):
        k, group = query % 4, query // 4
        o = z[k * 64 : (k + 1) * 64, group * 128 : (group + 1) * 128]
        pair = [jnp.where(side, o[0:16], o[16:32]), jnp.where(side, o[32:48], o[48:64])]
        y.append(side_by_side(pair))
    y = [jnp.concatenate(y[k * CHUNK : (k + 1) * CHUNK], axis=0) for k in chunks]
    y = dot(swap, side_by_side(y).astype(bf16)).astype(bf16)
    for k in chunks:
        for t in range(tiles):
            value = y[t * 16 : (t + 1) * 16, k * 256 : (k + 1) * 256]
            out[k * CHUNK : (k + 1) * CHUNK, t * 256 : (t + 1) * 256] = value


def own_kernel(q_hbm, left_hbm, right_hbm, mine, lefts_ref, rights_ref, q_ref, left, right, sems):
    at = pl.multiple_of(lax.axis_index("parts") * HALF, HALF)
    copies = [
        pltpu.make_async_copy(source, target, sems.at[k])
        for k, (source, target) in enumerate(
            ((left_hbm, left), (right_hbm, right), (q_hbm.at[pl.ds(at, HALF), :], q_ref))
        )
    ]
    for copy in copies:
        copy.start()
    copies[0].wait()
    copies[1].wait()
    lefts, rights = factors(left[...], right[...])
    for k in range(2):
        lefts_ref[k] = lefts[k]
        rights_ref[k] = rights[k]
    copies[2].wait()
    precond_rows(q_ref, lefts, rights, mine)


def rest_kernel(
    weight_ref, layer_ref, q_hbm, train_hbm, lefts_ref, rights_ref, rest, train, weight, q_ref, sems
):
    at = pl.multiple_of((1 - lax.axis_index("parts")) * HALF, HALF)
    q_copy = pltpu.make_async_copy(q_hbm.at[pl.ds(at, HALF), :], q_ref, sems.at[0])
    q_copy.start()
    copies = []
    for k in range(train.shape[0] // STEP):
        here = pl.ds(k * STEP, STEP)
        copies.append(pltpu.make_async_copy(train_hbm.at[here, :], train.at[here, :], sems.at[1 + k]))
        copies[-1].start()
    weight[...] = jnp.full(weight.shape, weight_ref[layer_ref[0]])
    lefts, rights = [lefts_ref[0], lefts_ref[1]], [rights_ref[0], rights_ref[1]]
    q_copy.wait()
    precond_rows(q_ref, lefts, rights, rest)
    for copy in copies:
        copy.wait()


def score_kernel(weight_ref, train_ref, *refs, picks, stored, early, columns):
    inputs, refs = refs[: len(picks)], refs[len(picks) :]
    n_before = sum(taken for _, _, taken in early)
    before, outs = refs[:n_before], refs[n_before:]
    weight = weight_ref[0:1, :]
    queries = jnp.concatenate(
        [piece[at : at + n, :] for piece, rows in zip(inputs, picks) for at, n in rows], axis=0
    )
    _, z, _, layer = place()
    near_is_mine = z // 2 == layer
    for at in range(*columns, STEP):
        there, here = slice(at, at + STEP), slice(at - columns[0], at - columns[0] + STEP)
        value = lax.dot_general(
            train_ref[there, :], queries, (((1,), (1,)), ((), ())), preferred_element_type=f32
        )
        value = weight * value.T
        if stored:
            outs[0][:, here] = value[:stored]
        if early:
            send, keep = outs[-2:]
            old, given = [], list(before)
            for first, rows, taken in early:
                old.append(
                    given.pop(0)[first : first + rows, there] if taken else value[first : first + rows]
                )
            old, new = jnp.concatenate(old, axis=0), value[stored:]
            send[:, here] = jnp.where(near_is_mine, new, old).astype(send.dtype)
            keep[:, here] = jnp.where(near_is_mine, old, new)


def kernel_call(kernel, outs, inputs, specs=None, scratch=()):
    return pl.pallas_call(
        kernel,
        out_shape=outs,
        in_specs=specs or [VMEM] * len(inputs),
        out_specs=[VMEM] * len(outs) if isinstance(outs, list) else VMEM,
        scratch_shapes=scratch,
        compiler_params=pltpu.CompilerParams(vmem_limit_bytes=LIMIT),
    )(*inputs)


def call_scores(weight, train, inputs, stored=0, early=(), columns=None):
    columns = columns or (0, train.shape[0])
    n = columns[1] - columns[0]
    total = sum(count for _, rows in inputs for _, count in rows)
    others = [a for a, _ in inputs] + [a for a, _, _ in early if a is not None]
    outs = [jax.ShapeDtypeStruct((stored, n), f32)] if stored else []
    if early:
        outs += [jax.ShapeDtypeStruct((total - stored, n), t) for t in (bf16, f32)]
    return kernel_call(
        functools.partial(
            score_kernel,
            picks=[rows for _, rows in inputs],
            stored=stored,
            early=[(first, rows, a is not None) for a, first, rows in early],
            columns=columns,
        ),
        outs,
        [weight, train, *others],
    )


def final_kernel(train_ids, query_ids, *refs, groups, n_given):
    given, refs = refs[:n_given], refs[n_given:]
    *_, out, done, sems = refs
    part, z, core, layer = place()
    low = z % 2
    first = jnp.where(z // 2 == layer, low, 1 - low)
    copies = []
    for k, (which, keep, got, row, column) in enumerate(groups):
        block = first if which < 2 else 1 - first
        half = part if which % 2 == 0 else 1 - part
        keep, got = given[keep], given[got]
        columns = pl.ds(column, keep.shape[1])
        for i, c in enumerate((core, 1 - core)):
            at = pl.multiple_of(((block * 2 + c) * 2 + half) * HALF, HALF)
            here, j = slice(row + i * HALF, row + (i + 1) * HALF), 2 * k + i
            total = keep[here, :] + got[here, :].astype(f32)
            same = query_ids[pl.ds(at, HALF), :] == train_ids[:, columns]
            slot = done.at[j * HALF : (j + 1) * HALF, : keep.shape[1]]
            slot[...] = jnp.where(same, jnp.float32(0.0), total)
            copies.append(
                pltpu.make_async_copy(slot, out.at[pl.ds(at, HALF), columns], sems.at[j])
            )
            copies[-1].start()
    for copy in copies:
        copy.wait()


def call_final(train_ids, query_ids, given, groups, before=None):
    rows, n = query_ids.shape[0], train_ids.shape[1]
    inputs = [train_ids, query_ids, *given] + ([] if before is None else [before])
    return pl.pallas_call(
        functools.partial(final_kernel, groups=groups, n_given=len(given)),
        out_shape=jax.ShapeDtypeStruct((rows, n), f32),
        in_specs=[VMEM] * (2 + len(given)) + ([] if before is None else [HBM]),
        out_specs=HBM,
        scratch_shapes=[
            pltpu.VMEM((2 * len(groups) * HALF, max(a.shape[1] for a in given)), f32),
            pltpu.SemaphoreType.DMA((2 * len(groups),)),
        ],
        input_output_aliases={} if before is None else {len(inputs) - 1: 0},
        compiler_params=pltpu.CompilerParams(vmem_limit_bytes=LIMIT),
    )(*inputs)


def small(
    train_grads,
    query_grads,
    left_factor,
    right_factor,
    layer_weight,
    layer_of,
    train_ids,
    query_ids,
):
    in_hbm = lambda array: pltpu.with_memory_space_constraint(array, pltpu.HBM)
    train, queries = in_hbm(train_grads[:, 0, :]), in_hbm(query_grads[:, 0, :])
    width, side = queries.shape[1], left_factor.shape[1]
    shape = jax.ShapeDtypeStruct
    mine, lefts, rights = kernel_call(
        own_kernel,
        [shape((HALF, width), bf16), shape((2, 256, 256), bf16), shape((2, 256, 512), bf16)],
        [queries, in_hbm(left_factor[0]), in_hbm(right_factor[0])],
        [HBM] * 3,
        [
            pltpu.VMEM((HALF, width), bf16),
            pltpu.VMEM((side, side), f32),
            pltpu.VMEM((side, side), f32),
            pltpu.SemaphoreType.DMA((3,)),
        ],
    )
    near = to_near(mine, "near")
    far = to_far(mine, "far")
    rest, train, weight = kernel_call(
        rest_kernel,
        [shape((HALF, width), bf16), shape(train.shape, bf16), shape((8, STEP), f32)],
        [in_hbm(layer_weight), layer_of, queries, train, lefts, rights],
        [SMEM, SMEM, HBM, HBM, VMEM, VMEM],
        [pltpu.VMEM((HALF, width), bf16), pltpu.SemaphoreType.DMA((1 + train.shape[0] // STEP,))],
    )
    score = functools.partial(call_scores, weight, train)

    def rows_of(*pieces):
        return [(piece, ((0, piece.shape[0]),)) for piece in pieces]

    mine_x = to_core(after(mine, rest), "mine_x")
    rest_x = to_core(rest, "rest_x")
    near = after(near, rest)
    near_x = to_core(near, "near_x")
    near_p = to_part(near, "near_p")
    far = after(far, near)
    cross = to_near(far, "cross")
    far_p = to_part(far, "far_p")
    far_x = to_core(after(far, rest_x), "far_x")
    mine_x = after(mine_x, far)
    (early0,) = score(rows_of(mine, mine_x, rest, rest_x), stored=128)
    send0, keep0 = score(rows_of(far, far_x), early=[(early0, 0, 64)])
    got0 = to_layer(send0, "got0")

    near_p = after(near_p, early0)
    near_px = to_core(near_p, "near_px")
    far_p, cross = after(far_p, near_px, send0), after(cross, send0)
    far_px = to_core(far_p, "far_px")
    cross_pa = to_part(cross[:CHUNK], "cross_pa")
    cross_pb = to_near(far_p[CHUNK:], "cross_pb")
    cross_x = to_core(cross, "cross_x")
    early1, send1, keep1 = score(
        rows_of(near, near_x, near_p, near_px, far_p, far_px, cross, cross_x),
        stored=128,
        early=[(early0, 64, 64), (None, 0, 64)],
    )
    got1 = to_layer(send1, "got1")
    cross_pa, cross_pb = after(cross_pa, send1, got0), after(cross_pb, send1, got0)
    cross_pxa = to_core(cross_pa, "cross_pxa")
    cross_pxb = to_core(cross_pb, "cross_pxb")
    last = rows_of(cross_pa, cross_pb, cross_pxa, cross_pxb)
    n = train.shape[0]
    cut = n * 3 // 4
    send2, keep2 = score(last, early=[(early1, 64, 64)], columns=(0, cut))
    got2 = to_layer(send2, "got2")
    early1 = after(early1, send2)
    send3, keep3 = score(last, early=[(early1, 64, 64)], columns=(cut, n))
    send3 = after(send3, got1)
    got3 = to_layer(send3, "got3")

    train_ids, query_ids = train_ids[None, :], query_ids[:, None]
    most = call_final(
        train_ids,
        query_ids,
        [keep0, got0, keep1, got1],
        ((0, 0, 1, 0, 0), (1, 2, 3, 0, 0), (2, 2, 3, 64, 0)),
    )
    return call_final(
        train_ids,
        query_ids,
        [keep2, got2, keep3, got3],
        ((3, 0, 1, 0, 0), (3, 2, 3, 0, cut)),
        most,
    )


def solution(mesh):
    placed = (
        P(("parts", "store"), "layer", None),
        P("store", "layer", None),
        P("layer", None, None),
        P("layer", None, None),
        P(),
        P("layer"),
        P(("parts", "store")),
        P("layer"),
    )
    sizes = tuple(mesh.shape[axis] for axis in AXES)
    return jax.shard_map(
        small if sizes == (PARTS, CHIPS * CORES, LAYERS) else general,
        mesh=mesh,
        in_specs=placed,
        out_specs=P("layer", ("parts", "store")),
        check_vma=False,
    )
```

```python
import functools

import jax
import jax.numpy as jnp
from jax import lax
from jax.experimental import pallas as pl
from jax.experimental.pallas import tpu as pltpu
from jax.sharding import PartitionSpec as P

AXES = ("parts", "store", "layer")
VMEM = pl.BlockSpec(memory_space=pltpu.VMEM)
SMEM = pl.BlockSpec(memory_space=pltpu.SMEM)
bf16, f32 = jnp.bfloat16, jnp.float32
LIMIT = 20 * 1024 * 1024


def preconditioned(query_grads, left_factor, right_factor):
    q_rows, slots, width = query_grads.shape
    side = left_factor.shape[1]
    mats = query_grads.astype(jnp.float32).reshape(q_rows, slots, side, side)
    half = jnp.einsum("lij,qljk->qlik", left_factor, mats, precision=lax.Precision.HIGHEST)
    full = jnp.einsum("qlik,lkm->qlim", half, right_factor, precision=lax.Precision.HIGHEST)
    return full.reshape(q_rows, slots, width).astype(jnp.bfloat16)


def general(
    train_grads,
    query_grads,
    left_factor,
    right_factor,
    layer_weight,
    layer_of,
    train_ids,
    query_ids,
):
    precond = preconditioned(query_grads, left_factor, right_factor)
    weight = jnp.take(layer_weight, layer_of[0])
    queries = lax.all_gather(precond, "store", axis=0, tiled=True)
    terms = weight * jnp.dot(
        queries[:, 0, :], train_grads[:, 0, :].T, preferred_element_type=jnp.float32
    )
    summed = lax.psum_scatter(terms, "layer", scatter_dimension=0, tiled=True)
    same = query_ids[:, None] == train_ids[None, :]
    return jnp.where(same, jnp.float32(0.0), summed)


PARTS, CHIPS, CORES, LAYERS = 2, 4, 2, 2
CHUNK = 16
HALF = 2 * CHUNK
STEP = 256
HBM = pl.BlockSpec(memory_space=pltpu.HBM)


def permute(value, name, target):
    pairs = []
    for p in range(PARTS):
        for z in range(CHIPS):
            for c in range(CORES):
                for l in range(LAYERS):
                    tp, tz, tc, tl = target(p, z, c, l)
                    source = ((p * CHIPS + z) * CORES + c) * LAYERS + l
                    pairs.append((source, ((tp * CHIPS + tz) * CORES + tc) * LAYERS + tl))
    with jax.named_scope(name):
        return lax.ppermute(value, AXES, pairs)


to_part = functools.partial(permute, target=lambda p, z, c, l: (1 - p, z, c, l))
to_core = functools.partial(permute, target=lambda p, z, c, l: (p, z, 1 - c, l))
to_layer = functools.partial(permute, target=lambda p, z, c, l: (p, z, c, 1 - l))
to_near = functools.partial(permute, target=lambda p, z, c, l: (p, z ^ 1, c, l))
to_far = functools.partial(permute, target=lambda p, z, c, l: (p, z ^ 3, c, l))


def after(value, *others):
    return lax.optimization_barrier((value, *others))[0]


def place():
    store = lax.axis_index("store")
    return lax.axis_index("parts"), store // CORES, store % CORES, lax.axis_index("layer")


def split(x, terms):
    out = []
    for _ in range(terms):
        term = x.astype(bf16)
        out.append(term)
        x = x - term.astype(f32)
    return out


def dot(a, b):
    return lax.dot_general(a, b, (((1,), (0,)), ((), ())), preferred_element_type=f32)


def iota(shape, dim):
    return lax.broadcasted_iota(jnp.int32, shape, dim)


def factors(left, right):
    r, c = iota((256, 64), 0), iota((256, 64), 1)
    pick = jnp.where(c == 4 * (r % 16) + (r // 16) % 4, 1.0, 0.0).astype(bf16)
    r, c = iota((64, 256), 0), iota((64, 256), 1)
    pick_t = jnp.where(r == 4 * (c % 16) + (c // 16) % 4, 1.0, 0.0).astype(bf16)
    block = iota((256, 256), 0) // 64 == iota((256, 256), 1) // 64
    lefts = [
        jnp.where(block, dot(dot(pick, term).astype(bf16), pick_t), 0.0).astype(bf16)
        for term in split(left, 2)
    ]
    row = jnp.concatenate([right, right], axis=1)
    tiled = jnp.concatenate([jnp.concatenate([row] * 4, axis=1)] * 4, axis=0)
    block = iota((256, 512), 0) // 64 == iota((256, 512), 1) // 128
    return lefts, split(jnp.where(block, tiled, 0.0), 2)


def precond_rows(q_ref, lefts, rights, out):
    rows, width = q_ref.shape
    tiles, chunks = width // 256, range(rows // CHUNK)
    side_by_side = functools.partial(jnp.concatenate, axis=1)
    r, c = iota((256, 256), 0), iota((256, 256), 1)
    swap = jnp.where((r // 16 == c % 16) & (r % 16 == c // 16), 1.0, 0.0).astype(bf16)

    def of_chunk(k):
        q = q_ref[k * CHUNK : (k + 1) * CHUNK, :]
        return jnp.concatenate([q[:, t * 256 : (t + 1) * 256] for t in range(tiles)], axis=0)

    x = dot(swap, side_by_side([of_chunk(k) for k in chunks])).astype(bf16)
    x = jnp.concatenate([x[:, k * 256 : (k + 1) * 256] for k in chunks], axis=0)
    z = dot(x, rights[0]) + dot(x, rights[1])
    sets = []
    for first in range(0, rows, 4):
        pieces = [
            z[query * 16 : (query + 1) * 16, s * 128 : (s + 1) * 128]
            for query in range(first, first + 4)
            for s in range(4)
        ]
        sets.append(jnp.concatenate(pieces, axis=0))
    high, low = split(side_by_side(sets), 2)
    z = dot(lefts[0], high) + (dot(lefts[0], low) + dot(lefts[1], high))
    side = iota((16, 128), 1) < 64
    y = []
    for query in range(rows):
        k, group = query % 4, query // 4
        o = z[k * 64 : (k + 1) * 64, group * 128 : (group + 1) * 128]
        pair = [jnp.where(side, o[0:16], o[16:32]), jnp.where(side, o[32:48], o[48:64])]
        y.append(side_by_side(pair))
    y = [jnp.concatenate(y[k * CHUNK : (k + 1) * CHUNK], axis=0) for k in chunks]
    y = dot(swap, side_by_side(y).astype(bf16)).astype(bf16)
    for k in chunks:
        for t in range(tiles):
            value = y[t * 16 : (t + 1) * 16, k * 256 : (k + 1) * 256]
            out[k * CHUNK : (k + 1) * CHUNK, t * 256 : (t + 1) * 256] = value


def own_kernel(q_hbm, left_hbm, right_hbm, mine, lefts_ref, rights_ref, q_ref, left, right, sems):
    at = pl.multiple_of(lax.axis_index("parts") * HALF, HALF)
    copies = [
        pltpu.make_async_copy(source, target, sems.at[k])
        for k, (source, target) in enumerate(
            ((left_hbm, left), (right_hbm, right), (q_hbm.at[pl.ds(at, HALF), :], q_ref))
        )
    ]
    for copy in copies:
        copy.start()
    copies[0].wait()
    copies[1].wait()
    lefts, rights = factors(left[...], right[...])
    for k in range(2):
        lefts_ref[k] = lefts[k]
        rights_ref[k] = rights[k]
    copies[2].wait()
    precond_rows(q_ref, lefts, rights, mine)


def rest_kernel(
    weight_ref, layer_ref, q_hbm, train_hbm, lefts_ref, rights_ref, rest, train, weight, q_ref, sems
):
    at = pl.multiple_of((1 - lax.axis_index("parts")) * HALF, HALF)
    q_copy = pltpu.make_async_copy(q_hbm.at[pl.ds(at, HALF), :], q_ref, sems.at[0])
    q_copy.start()
    copies = []
    for k in range(train.shape[0] // STEP):
        here = pl.ds(k * STEP, STEP)
        copies.append(pltpu.make_async_copy(train_hbm.at[here, :], train.at[here, :], sems.at[1 + k]))
        copies[-1].start()
    weight[...] = jnp.full(weight.shape, weight_ref[layer_ref[0]])
    lefts, rights = [lefts_ref[0], lefts_ref[1]], [rights_ref[0], rights_ref[1]]
    q_copy.wait()
    precond_rows(q_ref, lefts, rights, rest)
    for copy in copies:
        copy.wait()


def score_kernel(weight_ref, train_ref, *refs, picks, stored, early, columns):
    inputs, refs = refs[: len(picks)], refs[len(picks) :]
    n_before = sum(taken for _, _, taken in early)
    before, outs = refs[:n_before], refs[n_before:]
    weight = weight_ref[0:1, :]
    queries = jnp.concatenate(
        [piece[at : at + n, :] for piece, rows in zip(inputs, picks) for at, n in rows], axis=0
    )
    _, z, _, layer = place()
    near_is_mine = z // 2 == layer
    for at in range(*columns, STEP):
        there, here = slice(at, at + STEP), slice(at - columns[0], at - columns[0] + STEP)
        value = lax.dot_general(
            train_ref[there, :], queries, (((1,), (1,)), ((), ())), preferred_element_type=f32
        )
        value = weight * value.T
        if stored:
            outs[0][:, here] = value[:stored]
        if early:
            send, keep = outs[-2:]
            old, given = [], list(before)
            for first, rows, taken in early:
                old.append(
                    given.pop(0)[first : first + rows, there] if taken else value[first : first + rows]
                )
            old, new = jnp.concatenate(old, axis=0), value[stored:]
            send[:, here] = jnp.where(near_is_mine, new, old).astype(send.dtype)
            keep[:, here] = jnp.where(near_is_mine, old, new)


def kernel_call(kernel, outs, inputs, specs=None, scratch=()):
    return pl.pallas_call(
        kernel,
        out_shape=outs,
        in_specs=specs or [VMEM] * len(inputs),
        out_specs=[VMEM] * len(outs) if isinstance(outs, list) else VMEM,
        scratch_shapes=scratch,
        compiler_params=pltpu.CompilerParams(vmem_limit_bytes=LIMIT),
    )(*inputs)


def call_scores(weight, train, inputs, stored=0, early=(), columns=None):
    columns = columns or (0, train.shape[0])
    n = columns[1] - columns[0]
    total = sum(count for _, rows in inputs for _, count in rows)
    others = [a for a, _ in inputs] + [a for a, _, _ in early if a is not None]
    outs = [jax.ShapeDtypeStruct((stored, n), f32)] if stored else []
    if early:
        outs += [jax.ShapeDtypeStruct((total - stored, n), t) for t in (bf16, f32)]
    return kernel_call(
        functools.partial(
            score_kernel,
            picks=[rows for _, rows in inputs],
            stored=stored,
            early=[(first, rows, a is not None) for a, first, rows in early],
            columns=columns,
        ),
        outs,
        [weight, train, *others],
    )


def final_kernel(train_ids, query_ids, *refs, groups, n_given):
    given, refs = refs[:n_given], refs[n_given:]
    *_, out, done, sems = refs
    part, z, core, layer = place()
    low = z % 2
    first = jnp.where(z // 2 == layer, low, 1 - low)
    copies = []
    for k, (which, keep, got, row, column) in enumerate(groups):
        block = first if which < 2 else 1 - first
        half = part if which % 2 == 0 else 1 - part
        keep, got = given[keep], given[got]
        columns = pl.ds(column, keep.shape[1])
        for i, c in enumerate((core, 1 - core)):
            at = pl.multiple_of(((block * 2 + c) * 2 + half) * HALF, HALF)
            here, j = slice(row + i * HALF, row + (i + 1) * HALF), 2 * k + i
            total = keep[here, :] + got[here, :].astype(f32)
            same = query_ids[pl.ds(at, HALF), :] == train_ids[:, columns]
            slot = done.at[j * HALF : (j + 1) * HALF, : keep.shape[1]]
            slot[...] = jnp.where(same, jnp.float32(0.0), total)
            copies.append(
                pltpu.make_async_copy(slot, out.at[pl.ds(at, HALF), columns], sems.at[j])
            )
            copies[-1].start()
    for copy in copies:
        copy.wait()


def call_final(train_ids, query_ids, given, groups, before=None):
    rows, n = query_ids.shape[0], train_ids.shape[1]
    inputs = [train_ids, query_ids, *given] + ([] if before is None else [before])
    return pl.pallas_call(
        functools.partial(final_kernel, groups=groups, n_given=len(given)),
        out_shape=jax.ShapeDtypeStruct((rows, n), f32),
        in_specs=[VMEM] * (2 + len(given)) + ([] if before is None else [HBM]),
        out_specs=HBM,
        scratch_shapes=[
            pltpu.VMEM((2 * len(groups) * HALF, max(a.shape[1] for a in given)), f32),
            pltpu.SemaphoreType.DMA((2 * len(groups),)),
        ],
        input_output_aliases={} if before is None else {len(inputs) - 1: 0},
        compiler_params=pltpu.CompilerParams(vmem_limit_bytes=LIMIT),
    )(*inputs)


def small(
    train_grads,
    query_grads,
    left_factor,
    right_factor,
    layer_weight,
    layer_of,
    train_ids,
    query_ids,
):
    in_hbm = lambda array: pltpu.with_memory_space_constraint(array, pltpu.HBM)
    train, queries = in_hbm(train_grads[:, 0, :]), in_hbm(query_grads[:, 0, :])
    width, side = queries.shape[1], left_factor.shape[1]
    shape = jax.ShapeDtypeStruct
    mine, lefts, rights = kernel_call(
        own_kernel,
        [shape((HALF, width), bf16), shape((2, 256, 256), bf16), shape((2, 256, 512), bf16)],
        [queries, in_hbm(left_factor[0]), in_hbm(right_factor[0])],
        [HBM] * 3,
        [
            pltpu.VMEM((HALF, width), bf16),
            pltpu.VMEM((side, side), f32),
            pltpu.VMEM((side, side), f32),
            pltpu.SemaphoreType.DMA((3,)),
        ],
    )
    near = to_near(mine, "near")
    far = to_far(mine, "far")
    rest, train, weight = kernel_call(
        rest_kernel,
        [shape((HALF, width), bf16), shape(train.shape, bf16), shape((8, STEP), f32)],
        [in_hbm(layer_weight), layer_of, queries, train, lefts, rights],
        [SMEM, SMEM, HBM, HBM, VMEM, VMEM],
        [pltpu.VMEM((HALF, width), bf16), pltpu.SemaphoreType.DMA((1 + train.shape[0] // STEP,))],
    )
    score = functools.partial(call_scores, weight, train)

    def rows_of(*pieces):
        return [(piece, ((0, piece.shape[0]),)) for piece in pieces]

    mine_x = to_core(after(mine, rest), "mine_x")
    rest_x = to_core(rest, "rest_x")
    near = after(near, rest)
    near_x = to_core(near, "near_x")
    near_p = to_part(near, "near_p")
    far = after(far, near)
    cross = to_near(far, "cross")
    far_p = to_part(far, "far_p")
    far_x = to_core(after(far, rest_x), "far_x")
    mine_x = after(mine_x, far)
    (early0,) = score(rows_of(mine, mine_x, rest, rest_x), stored=128)
    send0, keep0 = score(rows_of(far, far_x), early=[(early0, 0, 64)])
    got0 = to_layer(send0, "got0")

    near_p = after(near_p, early0)
    near_px = to_core(near_p, "near_px")
    far_p, cross = after(far_p, near_px, send0), after(cross, send0)
    far_px = to_core(far_p, "far_px")
    cross_p = to_near(far_p, "cross_p")
    cross_x = to_core(cross, "cross_x")
    early1, send1, keep1 = score(
        rows_of(near, near_x, near_p, near_px, far_p, far_px, cross, cross_x),
        stored=128,
        early=[(early0, 64, 64), (None, 0, 64)],
    )
    got1 = to_layer(send1, "got1")
    cross_p = after(cross_p, send1, got0)
    cross_pxa = to_core(cross_p[:CHUNK], "cross_pxa")
    cross_pxb = to_core(cross_p[CHUNK:], "cross_pxb")
    last = rows_of(cross_p, cross_pxa, cross_pxb)
    send2, keep2 = score(last, early=[(early1, 64, 64)])
    got2 = to_layer(send2, "got2")

    train_ids, query_ids = train_ids[None, :], query_ids[:, None]
    most = call_final(
        train_ids,
        query_ids,
        [keep0, got0, keep1, got1],
        ((0, 0, 1, 0, 0), (1, 2, 3, 0, 0), (2, 2, 3, 64, 0)),
    )
    return call_final(
        train_ids,
        query_ids,
        [keep2, got2],
        ((3, 0, 1, 0, 0),),
        most,
    )


def solution(mesh):
    placed = (
        P(("parts", "store"), "layer", None),
        P("store", "layer", None),
        P("layer", None, None),
        P("layer", None, None),
        P(),
        P("layer"),
        P(("parts", "store")),
        P("layer"),
    )
    sizes = tuple(mesh.shape[axis] for axis in AXES)
    return jax.shard_map(
        small if sizes == (PARTS, CHIPS * CORES, LAYERS) else general,
        mesh=mesh,
        in_specs=placed,
        out_specs=P("layer", ("parts", "store")),
        check_vma=False,
    )
```

```python
import functools

import jax
import jax.numpy as jnp
from jax import lax
from jax.experimental import pallas as pl
from jax.experimental.pallas import tpu as pltpu
from jax.sharding import PartitionSpec as P

AXES = ("parts", "store", "layer")
VMEM = pl.BlockSpec(memory_space=pltpu.VMEM)
SMEM = pl.BlockSpec(memory_space=pltpu.SMEM)
bf16, f32 = jnp.bfloat16, jnp.float32
LIMIT = 20 * 1024 * 1024


def preconditioned(query_grads, left_factor, right_factor):
    q_rows, slots, width = query_grads.shape
    side = left_factor.shape[1]
    mats = query_grads.astype(jnp.float32).reshape(q_rows, slots, side, side)
    half = jnp.einsum("lij,qljk->qlik", left_factor, mats, precision=lax.Precision.HIGHEST)
    full = jnp.einsum("qlik,lkm->qlim", half, right_factor, precision=lax.Precision.HIGHEST)
    return full.reshape(q_rows, slots, width).astype(jnp.bfloat16)


def general(
    train_grads,
    query_grads,
    left_factor,
    right_factor,
    layer_weight,
    layer_of,
    train_ids,
    query_ids,
):
    precond = preconditioned(query_grads, left_factor, right_factor)
    weight = jnp.take(layer_weight, layer_of[0])
    queries = lax.all_gather(precond, "store", axis=0, tiled=True)
    terms = weight * jnp.dot(
        queries[:, 0, :], train_grads[:, 0, :].T, preferred_element_type=jnp.float32
    )
    summed = lax.psum_scatter(terms, "layer", scatter_dimension=0, tiled=True)
    same = query_ids[:, None] == train_ids[None, :]
    return jnp.where(same, jnp.float32(0.0), summed)


PARTS, CHIPS, CORES, LAYERS = 2, 4, 2, 2
CHUNK = 16
HALF = 2 * CHUNK
STEP = 256
HBM = pl.BlockSpec(memory_space=pltpu.HBM)


def permute(value, name, target):
    pairs = []
    for p in range(PARTS):
        for z in range(CHIPS):
            for c in range(CORES):
                for l in range(LAYERS):
                    tp, tz, tc, tl = target(p, z, c, l)
                    source = ((p * CHIPS + z) * CORES + c) * LAYERS + l
                    pairs.append((source, ((tp * CHIPS + tz) * CORES + tc) * LAYERS + tl))
    with jax.named_scope(name):
        return lax.ppermute(value, AXES, pairs)


to_part = functools.partial(permute, target=lambda p, z, c, l: (1 - p, z, c, l))
to_core = functools.partial(permute, target=lambda p, z, c, l: (p, z, 1 - c, l))
to_layer = functools.partial(permute, target=lambda p, z, c, l: (p, z, c, 1 - l))
to_near = functools.partial(permute, target=lambda p, z, c, l: (p, z ^ 1, c, l))
to_far = functools.partial(permute, target=lambda p, z, c, l: (p, z ^ 3, c, l))


def after(value, *others):
    return lax.optimization_barrier((value, *others))[0]


def place():
    store = lax.axis_index("store")
    return lax.axis_index("parts"), store // CORES, store % CORES, lax.axis_index("layer")


def split(x, terms):
    out = []
    for _ in range(terms):
        term = x.astype(bf16)
        out.append(term)
        x = x - term.astype(f32)
    return out


def dot(a, b):
    return lax.dot_general(a, b, (((1,), (0,)), ((), ())), preferred_element_type=f32)


def iota(shape, dim):
    return lax.broadcasted_iota(jnp.int32, shape, dim)


def factors(left, right):
    r, c = iota((256, 64), 0), iota((256, 64), 1)
    pick = jnp.where(c == 4 * (r % 16) + (r // 16) % 4, 1.0, 0.0).astype(bf16)
    r, c = iota((64, 256), 0), iota((64, 256), 1)
    pick_t = jnp.where(r == 4 * (c % 16) + (c // 16) % 4, 1.0, 0.0).astype(bf16)
    block = iota((256, 256), 0) // 64 == iota((256, 256), 1) // 64
    lefts = [
        jnp.where(block, dot(dot(pick, term).astype(bf16), pick_t), 0.0).astype(bf16)
        for term in split(left, 2)
    ]
    row = jnp.concatenate([right, right], axis=1)
    tiled = jnp.concatenate([jnp.concatenate([row] * 4, axis=1)] * 4, axis=0)
    block = iota((256, 512), 0) // 64 == iota((256, 512), 1) // 128
    return lefts, split(jnp.where(block, tiled, 0.0), 2)


def precond_rows(q_ref, lefts, rights, out):
    rows, width = q_ref.shape
    tiles, chunks = width // 256, range(rows // CHUNK)
    side_by_side = functools.partial(jnp.concatenate, axis=1)
    r, c = iota((256, 256), 0), iota((256, 256), 1)
    swap = jnp.where((r // 16 == c % 16) & (r % 16 == c // 16), 1.0, 0.0).astype(bf16)

    def of_chunk(k):
        q = q_ref[k * CHUNK : (k + 1) * CHUNK, :]
        return jnp.concatenate([q[:, t * 256 : (t + 1) * 256] for t in range(tiles)], axis=0)

    x = dot(swap, side_by_side([of_chunk(k) for k in chunks])).astype(bf16)
    x = jnp.concatenate([x[:, k * 256 : (k + 1) * 256] for k in chunks], axis=0)
    z = dot(x, rights[0]) + dot(x, rights[1])
    sets = []
    for first in range(0, rows, 4):
        pieces = [
            z[query * 16 : (query + 1) * 16, s * 128 : (s + 1) * 128]
            for query in range(first, first + 4)
            for s in range(4)
        ]
        sets.append(jnp.concatenate(pieces, axis=0))
    high, low = split(side_by_side(sets), 2)
    z = dot(lefts[0], high) + (dot(lefts[0], low) + dot(lefts[1], high))
    side = iota((16, 128), 1) < 64
    y = []
    for query in range(rows):
        k, group = query % 4, query // 4
        o = z[k * 64 : (k + 1) * 64, group * 128 : (group + 1) * 128]
        pair = [jnp.where(side, o[0:16], o[16:32]), jnp.where(side, o[32:48], o[48:64])]
        y.append(side_by_side(pair))
    y = [jnp.concatenate(y[k * CHUNK : (k + 1) * CHUNK], axis=0) for k in chunks]
    y = dot(swap, side_by_side(y).astype(bf16)).astype(bf16)
    for k in chunks:
        for t in range(tiles):
            value = y[t * 16 : (t + 1) * 16, k * 256 : (k + 1) * 256]
            out[k * CHUNK : (k + 1) * CHUNK, t * 256 : (t + 1) * 256] = value


def own_kernel(q_hbm, left_hbm, right_hbm, mine, lefts_ref, rights_ref, q_ref, left, right, sems):
    at = pl.multiple_of(lax.axis_index("parts") * HALF, HALF)
    copies = [
        pltpu.make_async_copy(source, target, sems.at[k])
        for k, (source, target) in enumerate(
            ((left_hbm, left), (right_hbm, right), (q_hbm.at[pl.ds(at, HALF), :], q_ref))
        )
    ]
    for copy in copies:
        copy.start()
    copies[0].wait()
    copies[1].wait()
    lefts, rights = factors(left[...], right[...])
    for k in range(2):
        lefts_ref[k] = lefts[k]
        rights_ref[k] = rights[k]
    copies[2].wait()
    precond_rows(q_ref, lefts, rights, mine)


def rest_kernel(
    weight_ref, layer_ref, q_hbm, train_hbm, lefts_ref, rights_ref, rest, train, weight, q_ref, sems
):
    at = pl.multiple_of((1 - lax.axis_index("parts")) * HALF, HALF)
    q_copy = pltpu.make_async_copy(q_hbm.at[pl.ds(at, HALF), :], q_ref, sems.at[0])
    q_copy.start()
    copies = []
    for k in range(train.shape[0] // STEP):
        here = pl.ds(k * STEP, STEP)
        copies.append(pltpu.make_async_copy(train_hbm.at[here, :], train.at[here, :], sems.at[1 + k]))
        copies[-1].start()
    weight[...] = jnp.full(weight.shape, weight_ref[layer_ref[0]])
    lefts, rights = [lefts_ref[0], lefts_ref[1]], [rights_ref[0], rights_ref[1]]
    q_copy.wait()
    precond_rows(q_ref, lefts, rights, rest)
    for copy in copies:
        copy.wait()


def score_kernel(weight_ref, train_ref, *refs, picks, stored, early, columns):
    inputs, refs = refs[: len(picks)], refs[len(picks) :]
    n_before = sum(taken for _, _, taken in early)
    before, outs = refs[:n_before], refs[n_before:]
    weight = weight_ref[0:1, :]
    queries = jnp.concatenate(
        [piece[at : at + n, :] for piece, rows in zip(inputs, picks) for at, n in rows], axis=0
    )
    _, z, _, layer = place()
    near_is_mine = z // 2 == layer
    for at in range(*columns, STEP):
        there, here = slice(at, at + STEP), slice(at - columns[0], at - columns[0] + STEP)
        value = lax.dot_general(
            train_ref[there, :], queries, (((1,), (1,)), ((), ())), preferred_element_type=f32
        )
        value = weight * value.T
        if stored:
            outs[0][:, here] = value[:stored]
        if early:
            send, keep = outs[-2:]
            old, given = [], list(before)
            for first, rows, taken in early:
                old.append(
                    given.pop(0)[first : first + rows, there] if taken else value[first : first + rows]
                )
            old, new = jnp.concatenate(old, axis=0), value[stored:]
            send[:, here] = jnp.where(near_is_mine, new, old).astype(send.dtype)
            keep[:, here] = jnp.where(near_is_mine, old, new)


def kernel_call(kernel, outs, inputs, specs=None, scratch=()):
    return pl.pallas_call(
        kernel,
        out_shape=outs,
        in_specs=specs or [VMEM] * len(inputs),
        out_specs=[VMEM] * len(outs) if isinstance(outs, list) else VMEM,
        scratch_shapes=scratch,
        compiler_params=pltpu.CompilerParams(vmem_limit_bytes=LIMIT),
    )(*inputs)


def call_scores(weight, train, inputs, stored=0, early=(), columns=None):
    columns = columns or (0, train.shape[0])
    n = columns[1] - columns[0]
    total = sum(count for _, rows in inputs for _, count in rows)
    others = [a for a, _ in inputs] + [a for a, _, _ in early if a is not None]
    outs = [jax.ShapeDtypeStruct((stored, n), f32)] if stored else []
    if early:
        outs += [jax.ShapeDtypeStruct((total - stored, n), t) for t in (bf16, f32)]
    return kernel_call(
        functools.partial(
            score_kernel,
            picks=[rows for _, rows in inputs],
            stored=stored,
            early=[(first, rows, a is not None) for a, first, rows in early],
            columns=columns,
        ),
        outs,
        [weight, train, *others],
    )


def final_kernel(train_ids, query_ids, *refs, groups, n_given):
    given, refs = refs[:n_given], refs[n_given:]
    *_, out, done, sems = refs
    part, z, core, layer = place()
    low = z % 2
    first = jnp.where(z // 2 == layer, low, 1 - low)
    copies = []
    for k, (which, keep, got, row, column) in enumerate(groups):
        block = first if which < 2 else 1 - first
        half = part if which % 2 == 0 else 1 - part
        keep, got = given[keep], given[got]
        columns = pl.ds(column, keep.shape[1])
        for i, c in enumerate((core, 1 - core)):
            at = pl.multiple_of(((block * 2 + c) * 2 + half) * HALF, HALF)
            here, j = slice(row + i * HALF, row + (i + 1) * HALF), 2 * k + i
            total = keep[here, :] + got[here, :].astype(f32)
            same = query_ids[pl.ds(at, HALF), :] == train_ids[:, columns]
            slot = done.at[j * HALF : (j + 1) * HALF, : keep.shape[1]]
            slot[...] = jnp.where(same, jnp.float32(0.0), total)
            copies.append(
                pltpu.make_async_copy(slot, out.at[pl.ds(at, HALF), columns], sems.at[j])
            )
            copies[-1].start()
    for copy in copies:
        copy.wait()


def call_final(train_ids, query_ids, given, groups, before=None):
    rows, n = query_ids.shape[0], train_ids.shape[1]
    inputs = [train_ids, query_ids, *given] + ([] if before is None else [before])
    return pl.pallas_call(
        functools.partial(final_kernel, groups=groups, n_given=len(given)),
        out_shape=jax.ShapeDtypeStruct((rows, n), f32),
        in_specs=[VMEM] * (2 + len(given)) + ([] if before is None else [HBM]),
        out_specs=HBM,
        scratch_shapes=[
            pltpu.VMEM((2 * len(groups) * HALF, max(a.shape[1] for a in given)), f32),
            pltpu.SemaphoreType.DMA((2 * len(groups),)),
        ],
        input_output_aliases={} if before is None else {len(inputs) - 1: 0},
        compiler_params=pltpu.CompilerParams(vmem_limit_bytes=LIMIT),
    )(*inputs)


def small(
    train_grads,
    query_grads,
    left_factor,
    right_factor,
    layer_weight,
    layer_of,
    train_ids,
    query_ids,
):
    in_hbm = lambda array: pltpu.with_memory_space_constraint(array, pltpu.HBM)
    train, queries = in_hbm(train_grads[:, 0, :]), in_hbm(query_grads[:, 0, :])
    width, side = queries.shape[1], left_factor.shape[1]
    shape = jax.ShapeDtypeStruct
    mine, lefts, rights = kernel_call(
        own_kernel,
        [shape((HALF, width), bf16), shape((2, 256, 256), bf16), shape((2, 256, 512), bf16)],
        [queries, in_hbm(left_factor[0]), in_hbm(right_factor[0])],
        [HBM] * 3,
        [
            pltpu.VMEM((HALF, width), bf16),
            pltpu.VMEM((side, side), f32),
            pltpu.VMEM((side, side), f32),
            pltpu.SemaphoreType.DMA((3,)),
        ],
    )
    near = to_near(mine, "near")
    far = to_far(mine, "far")
    rest, train, weight = kernel_call(
        rest_kernel,
        [shape((HALF, width), bf16), shape(train.shape, bf16), shape((8, STEP), f32)],
        [in_hbm(layer_weight), layer_of, queries, train, lefts, rights],
        [SMEM, SMEM, HBM, HBM, VMEM, VMEM],
        [pltpu.VMEM((HALF, width), bf16), pltpu.SemaphoreType.DMA((1 + train.shape[0] // STEP,))],
    )
    score = functools.partial(call_scores, weight, train)

    def rows_of(*pieces):
        return [(piece, ((0, piece.shape[0]),)) for piece in pieces]

    mine_x = to_core(after(mine, rest), "mine_x")
    rest_x = to_core(rest, "rest_x")
    near = after(near, rest)
    near_x = to_core(near, "near_x")
    near_p = to_part(near, "near_p")
    far = after(far, near)
    cross = to_near(far, "cross")
    far_p = to_part(far, "far_p")
    far_x = to_core(after(far, rest_x), "far_x")
    mine_x = after(mine_x, far)
    (early0,) = score(rows_of(mine, mine_x, rest, rest_x), stored=128)
    send0, keep0 = score(rows_of(far, far_x), early=[(early0, 0, 64)])
    got0 = to_layer(send0, "got0")

    near_p = after(near_p, early0)
    near_px = to_core(near_p, "near_px")
    far_p, cross = after(far_p, near_px, send0), after(cross, send0)
    far_px = to_core(far_p, "far_px")
    cross_p = to_near(far_p, "cross_p")
    cross_x = to_core(cross, "cross_x")
    early1, send1, keep1 = score(
        rows_of(near, near_x, near_p, near_px, far_p, far_px, cross, cross_x),
        stored=128,
        early=[(early0, 64, 64), (None, 0, 64)],
    )
    got1 = to_layer(send1, "got1")
    cross_p = after(cross_p, send1, got0)
    cross_pxa = to_core(cross_p[:CHUNK], "cross_pxa")
    cross_pxb = to_core(cross_p[CHUNK:], "cross_pxb")
    last = rows_of(cross_p, cross_pxa, cross_pxb)
    n = train.shape[0]
    cut = n // 2
    send2, keep2 = score(last, early=[(early1, 64, 64)], columns=(0, cut))
    got2 = to_layer(send2, "got2")
    early1 = after(early1, send2)
    send3, keep3 = score(last, early=[(early1, 64, 64)], columns=(cut, n))
    send3 = after(send3, got1)
    got3 = to_layer(send3, "got3")

    train_ids, query_ids = train_ids[None, :], query_ids[:, None]
    most = call_final(
        train_ids,
        query_ids,
        [keep0, got0, keep1, got1],
        ((0, 0, 1, 0, 0), (1, 2, 3, 0, 0), (2, 2, 3, 64, 0)),
    )
    return call_final(
        train_ids,
        query_ids,
        [keep2, got2, keep3, got3],
        ((3, 0, 1, 0, 0), (3, 2, 3, 0, cut)),
        most,
    )


def solution(mesh):
    placed = (
        P(("parts", "store"), "layer", None),
        P("store", "layer", None),
        P("layer", None, None),
        P("layer", None, None),
        P(),
        P("layer"),
        P(("parts", "store")),
        P("layer"),
    )
    sizes = tuple(mesh.shape[axis] for axis in AXES)
    return jax.shard_map(
        small if sizes == (PARTS, CHIPS * CORES, LAYERS) else general,
        mesh=mesh,
        in_specs=placed,
        out_specs=P("layer", ("parts", "store")),
        check_vma=False,
    )
```

```python
import functools

import jax
import jax.numpy as jnp
from jax import lax
from jax.experimental import pallas as pl
from jax.experimental.pallas import tpu as pltpu
from jax.sharding import PartitionSpec as P

AXES = ("parts", "store", "layer")
VMEM = pl.BlockSpec(memory_space=pltpu.VMEM)
SMEM = pl.BlockSpec(memory_space=pltpu.SMEM)
bf16, f32 = jnp.bfloat16, jnp.float32
LIMIT = 20 * 1024 * 1024


def preconditioned(query_grads, left_factor, right_factor):
    q_rows, slots, width = query_grads.shape
    side = left_factor.shape[1]
    mats = query_grads.astype(jnp.float32).reshape(q_rows, slots, side, side)
    half = jnp.einsum("lij,qljk->qlik", left_factor, mats, precision=lax.Precision.HIGHEST)
    full = jnp.einsum("qlik,lkm->qlim", half, right_factor, precision=lax.Precision.HIGHEST)
    return full.reshape(q_rows, slots, width).astype(jnp.bfloat16)


def general(
    train_grads,
    query_grads,
    left_factor,
    right_factor,
    layer_weight,
    layer_of,
    train_ids,
    query_ids,
):
    precond = preconditioned(query_grads, left_factor, right_factor)
    weight = jnp.take(layer_weight, layer_of[0])
    queries = lax.all_gather(precond, "store", axis=0, tiled=True)
    terms = weight * jnp.dot(
        queries[:, 0, :], train_grads[:, 0, :].T, preferred_element_type=jnp.float32
    )
    summed = lax.psum_scatter(terms, "layer", scatter_dimension=0, tiled=True)
    same = query_ids[:, None] == train_ids[None, :]
    return jnp.where(same, jnp.float32(0.0), summed)


PARTS, CHIPS, CORES, LAYERS = 2, 4, 2, 2
CHUNK = 16
HALF = 2 * CHUNK
STEP = 256
HBM = pl.BlockSpec(memory_space=pltpu.HBM)


def permute(value, name, target):
    pairs = []
    for p in range(PARTS):
        for z in range(CHIPS):
            for c in range(CORES):
                for l in range(LAYERS):
                    tp, tz, tc, tl = target(p, z, c, l)
                    source = ((p * CHIPS + z) * CORES + c) * LAYERS + l
                    pairs.append((source, ((tp * CHIPS + tz) * CORES + tc) * LAYERS + tl))
    with jax.named_scope(name):
        return lax.ppermute(value, AXES, pairs)


to_part = functools.partial(permute, target=lambda p, z, c, l: (1 - p, z, c, l))
to_core = functools.partial(permute, target=lambda p, z, c, l: (p, z, 1 - c, l))
to_layer = functools.partial(permute, target=lambda p, z, c, l: (p, z, c, 1 - l))
to_near = functools.partial(permute, target=lambda p, z, c, l: (p, z ^ 1, c, l))
to_far = functools.partial(permute, target=lambda p, z, c, l: (p, z ^ 3, c, l))


def after(value, *others):
    return lax.optimization_barrier((value, *others))[0]


def place():
    store = lax.axis_index("store")
    return lax.axis_index("parts"), store // CORES, store % CORES, lax.axis_index("layer")


def split(x, terms):
    out = []
    for _ in range(terms):
        term = x.astype(bf16)
        out.append(term)
        x = x - term.astype(f32)
    return out


def dot(a, b):
    return lax.dot_general(a, b, (((1,), (0,)), ((), ())), preferred_element_type=f32)


def iota(shape, dim):
    return lax.broadcasted_iota(jnp.int32, shape, dim)


def factors(left, right):
    r, c = iota((256, 64), 0), iota((256, 64), 1)
    pick = jnp.where(c == 4 * (r % 16) + (r // 16) % 4, 1.0, 0.0).astype(bf16)
    r, c = iota((64, 256), 0), iota((64, 256), 1)
    pick_t = jnp.where(r == 4 * (c % 16) + (c // 16) % 4, 1.0, 0.0).astype(bf16)
    block = iota((256, 256), 0) // 64 == iota((256, 256), 1) // 64
    lefts = [
        jnp.where(block, dot(dot(pick, term).astype(bf16), pick_t), 0.0).astype(bf16)
        for term in split(left, 2)
    ]
    row = jnp.concatenate([right, right], axis=1)
    tiled = jnp.concatenate([jnp.concatenate([row] * 4, axis=1)] * 4, axis=0)
    block = iota((256, 512), 0) // 64 == iota((256, 512), 1) // 128
    return lefts, split(jnp.where(block, tiled, 0.0), 2)


def precond_rows(q_ref, lefts, rights, out):
    rows, width = q_ref.shape
    tiles, chunks = width // 256, range(rows // CHUNK)
    side_by_side = functools.partial(jnp.concatenate, axis=1)
    r, c = iota((256, 256), 0), iota((256, 256), 1)
    swap = jnp.where((r // 16 == c % 16) & (r % 16 == c // 16), 1.0, 0.0).astype(bf16)

    def of_chunk(k):
        q = q_ref[k * CHUNK : (k + 1) * CHUNK, :]
        return jnp.concatenate([q[:, t * 256 : (t + 1) * 256] for t in range(tiles)], axis=0)

    x = dot(swap, side_by_side([of_chunk(k) for k in chunks])).astype(bf16)
    x = jnp.concatenate([x[:, k * 256 : (k + 1) * 256] for k in chunks], axis=0)
    z = dot(x, rights[0]) + dot(x, rights[1])
    sets = []
    for first in range(0, rows, 4):
        pieces = [
            z[query * 16 : (query + 1) * 16, s * 128 : (s + 1) * 128]
            for query in range(first, first + 4)
            for s in range(4)
        ]
        sets.append(jnp.concatenate(pieces, axis=0))
    high, low = split(side_by_side(sets), 2)
    z = dot(lefts[0], high) + (dot(lefts[0], low) + dot(lefts[1], high))
    side = iota((16, 128), 1) < 64
    y = []
    for query in range(rows):
        k, group = query % 4, query // 4
        o = z[k * 64 : (k + 1) * 64, group * 128 : (group + 1) * 128]
        pair = [jnp.where(side, o[0:16], o[16:32]), jnp.where(side, o[32:48], o[48:64])]
        y.append(side_by_side(pair))
    y = [jnp.concatenate(y[k * CHUNK : (k + 1) * CHUNK], axis=0) for k in chunks]
    y = dot(swap, side_by_side(y).astype(bf16)).astype(bf16)
    for k in chunks:
        for t in range(tiles):
            value = y[t * 16 : (t + 1) * 16, k * 256 : (k + 1) * 256]
            out[k * CHUNK : (k + 1) * CHUNK, t * 256 : (t + 1) * 256] = value


def own_kernel(q_hbm, left_hbm, right_hbm, mine, lefts_ref, rights_ref, q_ref, left, right, sems):
    at = pl.multiple_of(lax.axis_index("parts") * HALF, HALF)
    copies = [
        pltpu.make_async_copy(source, target, sems.at[k])
        for k, (source, target) in enumerate(
            ((left_hbm, left), (right_hbm, right), (q_hbm.at[pl.ds(at, HALF), :], q_ref))
        )
    ]
    for copy in copies:
        copy.start()
    copies[0].wait()
    copies[1].wait()
    lefts, rights = factors(left[...], right[...])
    for k in range(2):
        lefts_ref[k] = lefts[k]
        rights_ref[k] = rights[k]
    copies[2].wait()
    precond_rows(q_ref, lefts, rights, mine)


def rest_kernel(
    weight_ref, layer_ref, q_hbm, train_hbm, lefts_ref, rights_ref, rest, train, weight, q_ref, sems
):
    at = pl.multiple_of((1 - lax.axis_index("parts")) * HALF, HALF)
    q_copy = pltpu.make_async_copy(q_hbm.at[pl.ds(at, HALF), :], q_ref, sems.at[0])
    q_copy.start()
    copies = []
    for k in range(train.shape[0] // STEP):
        here = pl.ds(k * STEP, STEP)
        copies.append(pltpu.make_async_copy(train_hbm.at[here, :], train.at[here, :], sems.at[1 + k]))
        copies[-1].start()
    weight[...] = jnp.full(weight.shape, weight_ref[layer_ref[0]])
    lefts, rights = [lefts_ref[0], lefts_ref[1]], [rights_ref[0], rights_ref[1]]
    q_copy.wait()
    precond_rows(q_ref, lefts, rights, rest)
    for copy in copies:
        copy.wait()


def score_kernel(weight_ref, train_ref, *refs, picks, stored, early, columns):
    inputs, refs = refs[: len(picks)], refs[len(picks) :]
    n_before = sum(taken for _, _, taken in early)
    before, outs = refs[:n_before], refs[n_before:]
    weight = weight_ref[0:1, :]
    queries = jnp.concatenate(
        [piece[at : at + n, :] for piece, rows in zip(inputs, picks) for at, n in rows], axis=0
    )
    _, z, _, layer = place()
    near_is_mine = z // 2 == layer
    for at in range(*columns, STEP):
        there, here = slice(at, at + STEP), slice(at - columns[0], at - columns[0] + STEP)
        value = lax.dot_general(
            train_ref[there, :], queries, (((1,), (1,)), ((), ())), preferred_element_type=f32
        )
        value = weight * value.T
        if stored:
            outs[0][:, here] = value[:stored]
        if early:
            send, keep = outs[-2:]
            old, given = [], list(before)
            for first, rows, taken in early:
                old.append(
                    given.pop(0)[first : first + rows, there] if taken else value[first : first + rows]
                )
            old, new = jnp.concatenate(old, axis=0), value[stored:]
            send[:, here] = jnp.where(near_is_mine, new, old).astype(send.dtype)
            keep[:, here] = jnp.where(near_is_mine, old, new)


def kernel_call(kernel, outs, inputs, specs=None, scratch=()):
    return pl.pallas_call(
        kernel,
        out_shape=outs,
        in_specs=specs or [VMEM] * len(inputs),
        out_specs=[VMEM] * len(outs) if isinstance(outs, list) else VMEM,
        scratch_shapes=scratch,
        compiler_params=pltpu.CompilerParams(vmem_limit_bytes=LIMIT),
    )(*inputs)


def call_scores(weight, train, inputs, stored=0, early=(), columns=None):
    columns = columns or (0, train.shape[0])
    n = columns[1] - columns[0]
    total = sum(count for _, rows in inputs for _, count in rows)
    others = [a for a, _ in inputs] + [a for a, _, _ in early if a is not None]
    outs = [jax.ShapeDtypeStruct((stored, n), f32)] if stored else []
    if early:
        outs += [jax.ShapeDtypeStruct((total - stored, n), t) for t in (bf16, f32)]
    return kernel_call(
        functools.partial(
            score_kernel,
            picks=[rows for _, rows in inputs],
            stored=stored,
            early=[(first, rows, a is not None) for a, first, rows in early],
            columns=columns,
        ),
        outs,
        [weight, train, *others],
    )


def final_kernel(train_ids, query_ids, *refs, groups, n_given):
    given, refs = refs[:n_given], refs[n_given:]
    *_, out, done, sems = refs
    part, z, core, layer = place()
    low = z % 2
    first = jnp.where(z // 2 == layer, low, 1 - low)
    copies = []
    for k, (which, keep, got, row, column) in enumerate(groups):
        block = first if which < 2 else 1 - first
        half = part if which % 2 == 0 else 1 - part
        keep, got = given[keep], given[got]
        columns = pl.ds(column, keep.shape[1])
        for i, c in enumerate((core, 1 - core)):
            at = pl.multiple_of(((block * 2 + c) * 2 + half) * HALF, HALF)
            here, j = slice(row + i * HALF, row + (i + 1) * HALF), 2 * k + i
            total = keep[here, :] + got[here, :].astype(f32)
            same = query_ids[pl.ds(at, HALF), :] == train_ids[:, columns]
            slot = done.at[j * HALF : (j + 1) * HALF, : keep.shape[1]]
            slot[...] = jnp.where(same, jnp.float32(0.0), total)
            copies.append(
                pltpu.make_async_copy(slot, out.at[pl.ds(at, HALF), columns], sems.at[j])
            )
            copies[-1].start()
    for copy in copies:
        copy.wait()


def call_final(train_ids, query_ids, given, groups, before=None):
    rows, n = query_ids.shape[0], train_ids.shape[1]
    inputs = [train_ids, query_ids, *given] + ([] if before is None else [before])
    return pl.pallas_call(
        functools.partial(final_kernel, groups=groups, n_given=len(given)),
        out_shape=jax.ShapeDtypeStruct((rows, n), f32),
        in_specs=[VMEM] * (2 + len(given)) + ([] if before is None else [HBM]),
        out_specs=HBM,
        scratch_shapes=[
            pltpu.VMEM((2 * len(groups) * HALF, max(a.shape[1] for a in given)), f32),
            pltpu.SemaphoreType.DMA((2 * len(groups),)),
        ],
        input_output_aliases={} if before is None else {len(inputs) - 1: 0},
        compiler_params=pltpu.CompilerParams(vmem_limit_bytes=LIMIT),
    )(*inputs)


def small(
    train_grads,
    query_grads,
    left_factor,
    right_factor,
    layer_weight,
    layer_of,
    train_ids,
    query_ids,
):
    in_hbm = lambda array: pltpu.with_memory_space_constraint(array, pltpu.HBM)
    train, queries = in_hbm(train_grads[:, 0, :]), in_hbm(query_grads[:, 0, :])
    width, side = queries.shape[1], left_factor.shape[1]
    shape = jax.ShapeDtypeStruct
    mine, lefts, rights = kernel_call(
        own_kernel,
        [shape((HALF, width), bf16), shape((2, 256, 256), bf16), shape((2, 256, 512), bf16)],
        [queries, in_hbm(left_factor[0]), in_hbm(right_factor[0])],
        [HBM] * 3,
        [
            pltpu.VMEM((HALF, width), bf16),
            pltpu.VMEM((side, side), f32),
            pltpu.VMEM((side, side), f32),
            pltpu.SemaphoreType.DMA((3,)),
        ],
    )
    near = to_near(mine, "near")
    far = to_far(mine, "far")
    rest, train, weight = kernel_call(
        rest_kernel,
        [shape((HALF, width), bf16), shape(train.shape, bf16), shape((8, STEP), f32)],
        [in_hbm(layer_weight), layer_of, queries, train, lefts, rights],
        [SMEM, SMEM, HBM, HBM, VMEM, VMEM],
        [pltpu.VMEM((HALF, width), bf16), pltpu.SemaphoreType.DMA((1 + train.shape[0] // STEP,))],
    )
    score = functools.partial(call_scores, weight, train)

    def rows_of(*pieces):
        return [(piece, ((0, piece.shape[0]),)) for piece in pieces]

    mine_x = to_core(after(mine, rest), "mine_x")
    rest_x = to_core(rest, "rest_x")
    near = after(near, rest)
    near_x = to_core(near, "near_x")
    near_p = to_part(near, "near_p")
    far = after(far, near)
    cross = to_near(far, "cross")
    far_p = to_part(far, "far_p")
    far_x = to_core(after(far, rest_x), "far_x")
    mine_x = after(mine_x, far)
    (early0,) = score(rows_of(mine, mine_x, rest, rest_x), stored=128)
    send0, keep0 = score(rows_of(far, far_x), early=[(early0, 0, 64)])
    got0 = to_layer(send0, "got0")

    near_p = after(near_p, early0)
    near_px = to_core(near_p, "near_px")
    far_p, cross = after(far_p, near_px, send0), after(cross, send0)
    far_px = to_core(far_p, "far_px")
    cross_pa = to_part(cross[:CHUNK], "cross_pa")
    cross_pb = to_near(far_p[CHUNK:], "cross_pb")
    cross_x = to_core(cross, "cross_x")
    early1, send1, keep1 = score(
        rows_of(near, near_x, near_p, near_px, far_p, far_px, cross, cross_x),
        stored=128,
        early=[(early0, 64, 64), (None, 0, 64)],
    )
    got1 = to_layer(after(send1, got0), "got1")
    cross_pa, cross_pb = after(cross_pa, send1), after(cross_pb, send1)
    cross_px = to_core(jnp.concatenate([cross_pa, cross_pb], axis=0), "cross_px")
    last = rows_of(cross_pa, cross_pb, cross_px)
    send2, keep2 = score(last, early=[(early1, 64, 64)])
    got2 = to_layer(send2, "got2")

    train_ids, query_ids = train_ids[None, :], query_ids[:, None]
    most = call_final(
        train_ids,
        query_ids,
        [keep0, got0, keep1, got1],
        ((0, 0, 1, 0, 0), (1, 2, 3, 0, 0), (2, 2, 3, 64, 0)),
    )
    return call_final(
        train_ids,
        query_ids,
        [keep2, got2],
        ((3, 0, 1, 0, 0),),
        most,
    )


def solution(mesh):
    placed = (
        P(("parts", "store"), "layer", None),
        P("store", "layer", None),
        P("layer", None, None),
        P("layer", None, None),
        P(),
        P("layer"),
        P(("parts", "store")),
        P("layer"),
    )
    sizes = tuple(mesh.shape[axis] for axis in AXES)
    return jax.shard_map(
        small if sizes == (PARTS, CHIPS * CORES, LAYERS) else general,
        mesh=mesh,
        in_specs=placed,
        out_specs=P("layer", ("parts", "store")),
        check_vma=False,
    )
```

```python
import functools

import jax
import jax.numpy as jnp
from jax import lax
from jax.experimental import pallas as pl
from jax.experimental.pallas import tpu as pltpu
from jax.sharding import PartitionSpec as P

AXES = ("parts", "store", "layer")
VMEM = pl.BlockSpec(memory_space=pltpu.VMEM)
SMEM = pl.BlockSpec(memory_space=pltpu.SMEM)
bf16, f32 = jnp.bfloat16, jnp.float32
LIMIT = 20 * 1024 * 1024


def preconditioned(query_grads, left_factor, right_factor):
    q_rows, slots, width = query_grads.shape
    side = left_factor.shape[1]
    mats = query_grads.astype(jnp.float32).reshape(q_rows, slots, side, side)
    half = jnp.einsum("lij,qljk->qlik", left_factor, mats, precision=lax.Precision.HIGHEST)
    full = jnp.einsum("qlik,lkm->qlim", half, right_factor, precision=lax.Precision.HIGHEST)
    return full.reshape(q_rows, slots, width).astype(jnp.bfloat16)


def general(
    train_grads,
    query_grads,
    left_factor,
    right_factor,
    layer_weight,
    layer_of,
    train_ids,
    query_ids,
):
    precond = preconditioned(query_grads, left_factor, right_factor)
    weight = jnp.take(layer_weight, layer_of[0])
    queries = lax.all_gather(precond, "store", axis=0, tiled=True)
    terms = weight * jnp.dot(
        queries[:, 0, :], train_grads[:, 0, :].T, preferred_element_type=jnp.float32
    )
    summed = lax.psum_scatter(terms, "layer", scatter_dimension=0, tiled=True)
    same = query_ids[:, None] == train_ids[None, :]
    return jnp.where(same, jnp.float32(0.0), summed)


PARTS, CHIPS, CORES, LAYERS = 2, 4, 2, 2
CHUNK = 16
HALF = 2 * CHUNK
STEP = 256
HBM = pl.BlockSpec(memory_space=pltpu.HBM)


def permute(value, name, target):
    pairs = []
    for p in range(PARTS):
        for z in range(CHIPS):
            for c in range(CORES):
                for l in range(LAYERS):
                    tp, tz, tc, tl = target(p, z, c, l)
                    source = ((p * CHIPS + z) * CORES + c) * LAYERS + l
                    pairs.append((source, ((tp * CHIPS + tz) * CORES + tc) * LAYERS + tl))
    with jax.named_scope(name):
        return lax.ppermute(value, AXES, pairs)


to_part = functools.partial(permute, target=lambda p, z, c, l: (1 - p, z, c, l))
to_core = functools.partial(permute, target=lambda p, z, c, l: (p, z, 1 - c, l))
to_layer = functools.partial(permute, target=lambda p, z, c, l: (p, z, c, 1 - l))
to_near = functools.partial(permute, target=lambda p, z, c, l: (p, z ^ 1, c, l))
to_far = functools.partial(permute, target=lambda p, z, c, l: (p, z ^ 3, c, l))


def after(value, *others):
    return lax.optimization_barrier((value, *others))[0]


def place():
    store = lax.axis_index("store")
    return lax.axis_index("parts"), store // CORES, store % CORES, lax.axis_index("layer")


def split(x, terms):
    out = []
    for _ in range(terms):
        term = x.astype(bf16)
        out.append(term)
        x = x - term.astype(f32)
    return out


def dot(a, b):
    return lax.dot_general(a, b, (((1,), (0,)), ((), ())), preferred_element_type=f32)


def iota(shape, dim):
    return lax.broadcasted_iota(jnp.int32, shape, dim)


def factors(left, right):
    r, c = iota((256, 64), 0), iota((256, 64), 1)
    pick = jnp.where(c == 4 * (r % 16) + (r // 16) % 4, 1.0, 0.0).astype(bf16)
    r, c = iota((64, 256), 0), iota((64, 256), 1)
    pick_t = jnp.where(r == 4 * (c % 16) + (c // 16) % 4, 1.0, 0.0).astype(bf16)
    block = iota((256, 256), 0) // 64 == iota((256, 256), 1) // 64
    lefts = [
        jnp.where(block, dot(dot(pick, term).astype(bf16), pick_t), 0.0).astype(bf16)
        for term in split(left, 2)
    ]
    row = jnp.concatenate([right, right], axis=1)
    tiled = jnp.concatenate([jnp.concatenate([row] * 4, axis=1)] * 4, axis=0)
    block = iota((256, 512), 0) // 64 == iota((256, 512), 1) // 128
    return lefts, split(jnp.where(block, tiled, 0.0), 2)


def precond_rows(q_ref, lefts, rights, out):
    rows, width = q_ref.shape
    tiles, chunks = width // 256, range(rows // CHUNK)
    side_by_side = functools.partial(jnp.concatenate, axis=1)
    r, c = iota((256, 256), 0), iota((256, 256), 1)
    swap = jnp.where((r // 16 == c % 16) & (r % 16 == c // 16), 1.0, 0.0).astype(bf16)

    def of_chunk(k):
        q = q_ref[k * CHUNK : (k + 1) * CHUNK, :]
        return jnp.concatenate([q[:, t * 256 : (t + 1) * 256] for t in range(tiles)], axis=0)

    x = dot(swap, side_by_side([of_chunk(k) for k in chunks])).astype(bf16)
    x = jnp.concatenate([x[:, k * 256 : (k + 1) * 256] for k in chunks], axis=0)
    z = dot(x, rights[0]) + dot(x, rights[1])
    sets = []
    for first in range(0, rows, 4):
        pieces = [
            z[query * 16 : (query + 1) * 16, s * 128 : (s + 1) * 128]
            for query in range(first, first + 4)
            for s in range(4)
        ]
        sets.append(jnp.concatenate(pieces, axis=0))
    high, low = split(side_by_side(sets), 2)
    z = dot(lefts[0], high) + (dot(lefts[0], low) + dot(lefts[1], high))
    side = iota((16, 128), 1) < 64
    y = []
    for query in range(rows):
        k, group = query % 4, query // 4
        o = z[k * 64 : (k + 1) * 64, group * 128 : (group + 1) * 128]
        pair = [jnp.where(side, o[0:16], o[16:32]), jnp.where(side, o[32:48], o[48:64])]
        y.append(side_by_side(pair))
    y = [jnp.concatenate(y[k * CHUNK : (k + 1) * CHUNK], axis=0) for k in chunks]
    y = dot(swap, side_by_side(y).astype(bf16)).astype(bf16)
    for k in chunks:
        for t in range(tiles):
            value = y[t * 16 : (t + 1) * 16, k * 256 : (k + 1) * 256]
            out[k * CHUNK : (k + 1) * CHUNK, t * 256 : (t + 1) * 256] = value


def own_kernel(q_hbm, left_hbm, right_hbm, mine, lefts_ref, rights_ref, q_ref, left, right, sems):
    at = pl.multiple_of(lax.axis_index("parts") * HALF, HALF)
    copies = [
        pltpu.make_async_copy(source, target, sems.at[k])
        for k, (source, target) in enumerate(
            ((left_hbm, left), (right_hbm, right), (q_hbm.at[pl.ds(at, HALF), :], q_ref))
        )
    ]
    for copy in copies:
        copy.start()
    copies[0].wait()
    copies[1].wait()
    lefts, rights = factors(left[...], right[...])
    for k in range(2):
        lefts_ref[k] = lefts[k]
        rights_ref[k] = rights[k]
    copies[2].wait()
    precond_rows(q_ref, lefts, rights, mine)


def rest_kernel(
    weight_ref, layer_ref, q_hbm, train_hbm, lefts_ref, rights_ref, rest, train, weight, q_ref, sems
):
    at = pl.multiple_of((1 - lax.axis_index("parts")) * HALF, HALF)
    q_copy = pltpu.make_async_copy(q_hbm.at[pl.ds(at, HALF), :], q_ref, sems.at[0])
    q_copy.start()
    copies = []
    for k in range(train.shape[0] // STEP):
        here = pl.ds(k * STEP, STEP)
        copies.append(pltpu.make_async_copy(train_hbm.at[here, :], train.at[here, :], sems.at[1 + k]))
        copies[-1].start()
    weight[...] = jnp.full(weight.shape, weight_ref[layer_ref[0]])
    lefts, rights = [lefts_ref[0], lefts_ref[1]], [rights_ref[0], rights_ref[1]]
    q_copy.wait()
    precond_rows(q_ref, lefts, rights, rest)
    for copy in copies:
        copy.wait()


def score_kernel(weight_ref, train_ref, *refs, picks, stored, early, columns):
    inputs, refs = refs[: len(picks)], refs[len(picks) :]
    n_before = sum(taken for _, _, taken in early)
    before, outs = refs[:n_before], refs[n_before:]
    weight = weight_ref[0:1, :]
    queries = jnp.concatenate(
        [piece[at : at + n, :] for piece, rows in zip(inputs, picks) for at, n in rows], axis=0
    )
    _, z, _, layer = place()
    near_is_mine = z // 2 == layer
    for at in range(*columns, STEP):
        there, here = slice(at, at + STEP), slice(at - columns[0], at - columns[0] + STEP)
        value = lax.dot_general(
            train_ref[there, :], queries, (((1,), (1,)), ((), ())), preferred_element_type=f32
        )
        value = weight * value.T
        if stored:
            outs[0][:, here] = value[:stored]
        if early:
            send, keep = outs[-2:]
            old, given = [], list(before)
            for first, rows, taken in early:
                old.append(
                    given.pop(0)[first : first + rows, there] if taken else value[first : first + rows]
                )
            old, new = jnp.concatenate(old, axis=0), value[stored:]
            send[:, here] = jnp.where(near_is_mine, new, old).astype(send.dtype)
            keep[:, here] = jnp.where(near_is_mine, old, new)


def kernel_call(kernel, outs, inputs, specs=None, scratch=()):
    return pl.pallas_call(
        kernel,
        out_shape=outs,
        in_specs=specs or [VMEM] * len(inputs),
        out_specs=[VMEM] * len(outs) if isinstance(outs, list) else VMEM,
        scratch_shapes=scratch,
        compiler_params=pltpu.CompilerParams(vmem_limit_bytes=LIMIT),
    )(*inputs)


def call_scores(weight, train, inputs, stored=0, early=(), columns=None):
    columns = columns or (0, train.shape[0])
    n = columns[1] - columns[0]
    total = sum(count for _, rows in inputs for _, count in rows)
    others = [a for a, _ in inputs] + [a for a, _, _ in early if a is not None]
    outs = [jax.ShapeDtypeStruct((stored, n), f32)] if stored else []
    if early:
        outs += [jax.ShapeDtypeStruct((total - stored, n), t) for t in (bf16, f32)]
    return kernel_call(
        functools.partial(
            score_kernel,
            picks=[rows for _, rows in inputs],
            stored=stored,
            early=[(first, rows, a is not None) for a, first, rows in early],
            columns=columns,
        ),
        outs,
        [weight, train, *others],
    )


def final_kernel(train_ids, query_ids, *refs, groups, n_given):
    given, refs = refs[:n_given], refs[n_given:]
    *_, out, done, sems = refs
    part, z, core, layer = place()
    low = z % 2
    first = jnp.where(z // 2 == layer, low, 1 - low)
    copies = []
    for k, (which, keep, got, row, column) in enumerate(groups):
        block = first if which < 2 else 1 - first
        half = part if which % 2 == 0 else 1 - part
        keep, got = given[keep], given[got]
        columns = pl.ds(column, keep.shape[1])
        for i, c in enumerate((core, 1 - core)):
            at = pl.multiple_of(((block * 2 + c) * 2 + half) * HALF, HALF)
            here, j = slice(row + i * HALF, row + (i + 1) * HALF), 2 * k + i
            total = keep[here, :] + got[here, :].astype(f32)
            same = query_ids[pl.ds(at, HALF), :] == train_ids[:, columns]
            slot = done.at[j * HALF : (j + 1) * HALF, : keep.shape[1]]
            slot[...] = jnp.where(same, jnp.float32(0.0), total)
            copies.append(
                pltpu.make_async_copy(slot, out.at[pl.ds(at, HALF), columns], sems.at[j])
            )
            copies[-1].start()
    for copy in copies:
        copy.wait()


def call_final(train_ids, query_ids, given, groups, before=None):
    rows, n = query_ids.shape[0], train_ids.shape[1]
    inputs = [train_ids, query_ids, *given] + ([] if before is None else [before])
    return pl.pallas_call(
        functools.partial(final_kernel, groups=groups, n_given=len(given)),
        out_shape=jax.ShapeDtypeStruct((rows, n), f32),
        in_specs=[VMEM] * (2 + len(given)) + ([] if before is None else [HBM]),
        out_specs=HBM,
        scratch_shapes=[
            pltpu.VMEM((2 * len(groups) * HALF, max(a.shape[1] for a in given)), f32),
            pltpu.SemaphoreType.DMA((2 * len(groups),)),
        ],
        input_output_aliases={} if before is None else {len(inputs) - 1: 0},
        compiler_params=pltpu.CompilerParams(vmem_limit_bytes=LIMIT),
    )(*inputs)


def small(
    train_grads,
    query_grads,
    left_factor,
    right_factor,
    layer_weight,
    layer_of,
    train_ids,
    query_ids,
):
    in_hbm = lambda array: pltpu.with_memory_space_constraint(array, pltpu.HBM)
    train, queries = in_hbm(train_grads[:, 0, :]), in_hbm(query_grads[:, 0, :])
    width, side = queries.shape[1], left_factor.shape[1]
    shape = jax.ShapeDtypeStruct
    mine, lefts, rights = kernel_call(
        own_kernel,
        [shape((HALF, width), bf16), shape((2, 256, 256), bf16), shape((2, 256, 512), bf16)],
        [queries, in_hbm(left_factor[0]), in_hbm(right_factor[0])],
        [HBM] * 3,
        [
            pltpu.VMEM((HALF, width), bf16),
            pltpu.VMEM((side, side), f32),
            pltpu.VMEM((side, side), f32),
            pltpu.SemaphoreType.DMA((3,)),
        ],
    )
    near = to_near(mine, "near")
    far = to_far(mine, "far")
    rest, train, weight = kernel_call(
        rest_kernel,
        [shape((HALF, width), bf16), shape(train.shape, bf16), shape((8, STEP), f32)],
        [in_hbm(layer_weight), layer_of, queries, train, lefts, rights],
        [SMEM, SMEM, HBM, HBM, VMEM, VMEM],
        [pltpu.VMEM((HALF, width), bf16), pltpu.SemaphoreType.DMA((1 + train.shape[0] // STEP,))],
    )
    score = functools.partial(call_scores, weight, train)

    def rows_of(*pieces):
        return [(piece, ((0, piece.shape[0]),)) for piece in pieces]

    mine_x = to_core(after(mine, rest), "mine_x")
    rest_x = to_core(rest, "rest_x")
    near = after(near, rest)
    near_x = to_core(near, "near_x")
    near_p = to_part(near, "near_p")
    far = after(far, near)
    cross = to_near(far, "cross")
    far_p = to_part(far, "far_p")
    far_x = to_core(after(far, rest_x), "far_x")
    mine_x = after(mine_x, far)
    (early0,) = score(rows_of(mine, mine_x, rest, rest_x), stored=128)
    send0, keep0 = score(rows_of(far, far_x), early=[(early0, 0, 64)])
    got0 = to_layer(send0, "got0")

    near_p = after(near_p, early0)
    near_px = to_core(near_p, "near_px")
    far_p, cross = after(far_p, near_px, send0), after(cross, send0)
    far_px = to_core(far_p, "far_px")
    cross_pa = to_near(far_p[:CHUNK], "cross_pa")
    cross_pb = to_near(far_p[CHUNK:], "cross_pb")
    cross_x = to_core(cross, "cross_x")
    early1, send1, keep1 = score(
        rows_of(near, near_x, near_p, near_px, far_p, far_px, cross, cross_x),
        stored=128,
        early=[(early0, 64, 64), (None, 0, 64)],
    )
    got1 = to_layer(send1, "got1")
    cross_pa, cross_pb = after(cross_pa, send1, got0), after(cross_pb, send1, got0)
    cross_pxa = to_core(cross_pa, "cross_pxa")
    cross_pxb = to_core(cross_pb, "cross_pxb")
    last = rows_of(cross_pa, cross_pb, cross_pxa, cross_pxb)
    send2, keep2 = score(last, early=[(early1, 64, 64)])
    got2 = to_layer(send2, "got2")

    train_ids, query_ids = train_ids[None, :], query_ids[:, None]
    most = call_final(
        train_ids,
        query_ids,
        [keep0, got0, keep1, got1],
        ((0, 0, 1, 0, 0), (1, 2, 3, 0, 0), (2, 2, 3, 64, 0)),
    )
    return call_final(
        train_ids,
        query_ids,
        [keep2, got2],
        ((3, 0, 1, 0, 0),),
        most,
    )


def solution(mesh):
    placed = (
        P(("parts", "store"), "layer", None),
        P("store", "layer", None),
        P("layer", None, None),
        P("layer", None, None),
        P(),
        P("layer"),
        P(("parts", "store")),
        P("layer"),
    )
    sizes = tuple(mesh.shape[axis] for axis in AXES)
    return jax.shard_map(
        small if sizes == (PARTS, CHIPS * CORES, LAYERS) else general,
        mesh=mesh,
        in_specs=placed,
        out_specs=P("layer", ("parts", "store")),
        check_vma=False,
    )
```
